32 devices in a mesh: groups: 2 (over y), tp: 4 (over z), sub: 4 (over x, core).
Axes of the slice: x: 2, y: 2, z: 4, core: 2. Of those that a mesh axis runs over, the one named last changes fastest.
Arguments:
- hidden_states: bfloat16 [8192, 8192], P(('groups', 'sub'), 'tp'), parts along dimension 0, may hold values from -6 to 6
- queries: bfloat16 [8192, 4096], P(('groups', 'sub'), 'tp'), parts along dimension 0, may hold values from -400 to 400
- latent_down: bfloat16 [8192, 512], P('tp'), may hold values from -0.0625 to 0.0625
- key_up: bfloat16 [256, 512], replicated, may hold values from -0.375 to 0.375
- value_up: bfloat16 [256, 512], replicated, may hold values from -0.375 to 0.375
- doc_lengths: int32 [32], P('groups'), parts along dimension 0, may hold values from 1 to 2048, 4096 in all
- doc_owners: int32 [32], P('groups'), parts along dimension 0, may hold values from 0 to 3
Outputs:
- attention: bfloat16 [8192, 4096], P(('groups', 'sub'), 'tp'), parts along dimension 0
- decode_cache: bfloat16 [8192, 1024], P(('groups', 'tp', 'sub')), parts along dimension 0
The draws below stay inside these ranges and needn't reach their ends.
There are 2 independent parts, one for each index of `groups`. The reference program is written for one: setup_inputs(seed, part) draws one part's arguments, and reference() takes and returns one part's arrays. A program takes and returns all parts, laid end to end along the dimension named above; an argument that names none is the same for every part. Nothing has to cross between parts.
Inputs may be any that keep to these rules, and one draw needn't show every extreme that they name: `doc_lengths`: the 16 documents lie in the pack in order and their lengths sum to 4096.
All inputs are finite; a program needn't handle non-finite values.
Results may differ from the reference program's by a relative error of at most 0.008.
The reference program's roundings to bfloat16 on the way (of `latents`, `keys` and `weight`) count: a program that leaves them out, or rounds other values in their place, can miss the bound.
Values may be sent and summed in bfloat16 or wider, within the bound.
No kernel may reach another device: no remote copies, remote signals or barrier semaphores. Data moves between devices by JAX's collectives and lax.ppermute only.
A program may use at most 128 MiB of HBM per device.

```python
import math
import jax
import jax.numpy as jnp
import numpy as np
from jax import lax

D = 8192
HEAD_DIM = 128
Q_HEADS = 32
KV_HEADS = 4
RANK = 256
TOK_DEV = 1024
REQUESTS = 16
TOKENS = 4096
OWNERS = 4


def draw_queries(key, part):
    key = jax.random.fold_in(key, 11)
    base_key, scale_key = jax.random.split(key)
    normal_draw = jax.random.normal(base_key, (TOKENS, Q_HEADS * HEAD_DIM), jnp.float32)
    uniform_draw = jax.random.uniform(scale_key, (TOKENS, 1), jnp.float32)
    row_scale = jnp.exp(2.0 * uniform_draw - 1.0)
    return jnp.clip(normal_draw * row_scale, -400.0, 400.0).astype(jnp.bfloat16)


def touch_ends(values, stream_key, low, top_value):
    longest = values.shape.index(max(values.shape))
    spots = []
    for shift in (0, 1):
        where = [jax.random.randint(jax.random.fold_in(stream_key, axis), (), 0, length) for axis, length in enumerate(values.shape)]
        where[longest] = (where[longest] + shift) % values.shape[longest]
        spots.append(tuple(where))
    return values.at[spots[0]].set(low).at[spots[1]].set(top_value)


def block_scale(stream_key, extent, cuts, least, top_value):
    factor_of, own = 1.0, jax.random.fold_in(stream_key, 6)
    for position, parts in cuts:
        heights = jnp.exp(jax.random.uniform(jax.random.fold_in(own, position), (parts,), jnp.float32, least / len(cuts), top_value / len(cuts)))
        factor_of = factor_of * jnp.repeat(heights, extent[position] // parts).reshape([-1 if axis == position else 1 for axis in range(len(extent))])
    return factor_of


def rank_bounds(number_of, slope):
    portions = [(1 << 20) // math.isqrt(standing ** slope) + 1 for standing in range(1, number_of + 1)]
    spread = 1 + sum(portions) // (1 << 30)
    return np.cumsum(np.array([max(1, weight // spread) for weight in portions]))


def ranked_ids(rng, shape, amount, lean):
    grid = rank_bounds(amount, lean)
    ticket = jax.random.randint(jax.random.fold_in(rng, 1), shape, 0, int(grid[amount - 1]))
    rank = jnp.searchsorted(jnp.asarray(grid, jnp.int32), ticket, side="right")
    return jax.random.permutation(jax.random.fold_in(rng, 2), amount)[rank].astype(jnp.int32)


def split_up(amount, total, bound, slope):
    loads = [(1 << 20) // math.isqrt(rank ** slope) + 1 for rank in range(2, amount + 1)]
    rest, counts = total - bound - (amount - 1), [1] * (amount - 1)
    while rest > 0:
        free = [i for i in range(amount - 1) if counts[i] < bound]
        pool, left = sum([loads[i] for i in free]), rest
        for i in free:
            addition = min(bound - counts[i], max(1, left * loads[i] // pool), rest)
            counts[i] = counts[i] + addition
            rest = rest - addition
    return np.array([bound] + counts)


def ragged(rng, number_of, total, reach, lean):
    if number_of == 2:
        one = jax.random.randint(rng, (), max(1, total - reach), min(reach, total - 1) + 1)
        return jnp.stack([one, total - one])
    tallies = jnp.asarray(split_up(number_of, total, reach, lean), jnp.int32)
    couples = (number_of - 1) // 2
    source_of, receiver = tallies[1:1 + 2 * couples:2], tallies[2:2 + 2 * couples:2]
    margin = jnp.minimum(source_of - 1, reach - receiver)
    passed = jax.random.randint(jax.random.fold_in(rng, 1), (couples,), 0, 1 << 20) % (margin + 1)
    tallies = tallies.at[1:1 + 2 * couples:2].set(source_of - passed).at[2:2 + 2 * couples:2].set(receiver + passed)
    return tallies[jax.random.permutation(jax.random.fold_in(rng, 2), number_of)]


def normal_values(key, extent, deviation, limit, cuts=(), held_as=jnp.bfloat16):
    gain = block_scale(key, extent, cuts, -0.22, 0.18) if cuts else 1.0
    entries = jax.random.normal(key, extent, jnp.float32) * deviation * gain
    return jnp.minimum(jnp.maximum(entries, -limit), limit).astype(held_as)


def setup_inputs(seed: int = 0, part: int = 0) -> dict:
    key_of = jax.random.split(jax.random.key(seed), 8)
    part_splits = jax.random.split(jax.random.fold_in(key_of[7], part), 8)
    hidden_states = normal_values(part_splits[0], (TOKENS, D), 1.0, 6.0, ((0, 4), (1, 4)))
    queries = draw_queries(jax.random.fold_in(jax.random.fold_in(key_of[7], part), 71), part)
    latent_down = normal_values(key_of[2], (D, 2 * RANK), D ** -0.5, 0.0625, ((0, 4),))
    key_up = normal_values(key_of[3], (RANK, KV_HEADS * HEAD_DIM), RANK ** -0.5, 0.375)
    value_up = normal_values(key_of[4], (RANK, KV_HEADS * HEAD_DIM), RANK ** -0.5, 0.375)
    doc_lengths = ragged(part_splits[5], REQUESTS, TOKENS, TOKENS // 2, 2).astype(jnp.int32)
    doc_owners = touch_ends(ranked_ids(part_splits[6], (REQUESTS,), OWNERS, 2), jax.random.fold_in(part_splits[6], 3), 0, OWNERS - 1).astype(jnp.int32)
    return {"hidden_states": hidden_states, "queries": queries, "latent_down": latent_down, "key_up": key_up, "value_up": value_up, "doc_lengths": doc_lengths, "doc_owners": doc_owners}


def doc_tables(doc_lengths):
    doc_ends = jnp.cumsum(doc_lengths).astype(jnp.int32)
    doc_starts = (doc_ends - doc_lengths).astype(jnp.int32)
    return (doc_starts, doc_ends)

def doc_of(positions, doc_ends):
    return lax.optimization_barrier(jnp.sum((positions[:, None] >= doc_ends[None, :]).astype(jnp.int32), axis=1)).astype(jnp.int32)

def lookup(doc_index, doc_table):
    doc_numbers = jnp.arange(doc_table.shape[0], dtype=jnp.int32)
    picked = jnp.where(doc_index[:, None] == doc_numbers[None, :], doc_table[None, :], 0)
    return lax.optimization_barrier(jnp.sum(picked, axis=1)).astype(jnp.int32)

def owner_base(doc_lengths, doc_owners):
    doc_numbers = jnp.arange(doc_lengths.shape[0], dtype=jnp.int32)
    before = (doc_owners[None, :] < doc_owners[:, None]) | (doc_owners[None, :] == doc_owners[:, None]) & (doc_numbers[None, :] < doc_numbers[:, None])
    return lax.optimization_barrier(jnp.sum(jnp.where(before, doc_lengths[None, :], 0), axis=1)).astype(jnp.int32)

def reference(hidden_states, queries, latent_down, key_up, value_up, doc_lengths, doc_owners):
    latents = jnp.dot(hidden_states, latent_down, preferred_element_type=jnp.float32).astype(jnp.bfloat16)
    keys = jnp.dot(latents[:, :RANK], key_up, preferred_element_type=jnp.float32).astype(jnp.bfloat16)
    values = jnp.dot(latents[:, RANK:], value_up, preferred_element_type=jnp.float32).astype(jnp.bfloat16)
    doc_starts, doc_ends = doc_tables(doc_lengths)
    positions = jnp.arange(TOKENS, dtype=jnp.int32)
    doc_index = doc_of(positions, doc_ends)
    inv_root = 1.0 / math.sqrt(HEAD_DIM)
    per_group = Q_HEADS // KV_HEADS
    blocks = TOKENS // TOK_DEV

    def one_head(head_number):
        kv_head = (head_number // per_group).astype(jnp.int32)
        key_head = lax.dynamic_slice_in_dim(keys, kv_head * HEAD_DIM, HEAD_DIM, 1)
        value_head = lax.dynamic_slice_in_dim(values, kv_head * HEAD_DIM, HEAD_DIM, 1)
        query_head = lax.dynamic_slice_in_dim(queries, head_number * HEAD_DIM, HEAD_DIM, 1)

        def one_block(block_number):
            first_row = (block_number * TOK_DEV).astype(jnp.int32)
            query_block = lax.dynamic_slice_in_dim(query_head, first_row, TOK_DEV, 0)
            query_pos = first_row + jnp.arange(TOK_DEV, dtype=jnp.int32)
            query_doc = lax.dynamic_slice_in_dim(doc_index, first_row, TOK_DEV, 0)
            allowed = (positions[None, :] <= query_pos[:, None]) & (doc_index[None, :] == query_doc[:, None])
            scores = jnp.dot(query_block, key_head.T, preferred_element_type=jnp.float32) * inv_root
            scores = jnp.where(allowed, scores, -1e+30)
            row_top = lax.optimization_barrier(jnp.max(scores, axis=1, keepdims=True))
            weights = jnp.where(allowed, jnp.exp(scores - row_top), 0.0)
            totals = lax.optimization_barrier(jnp.sum(weights, axis=1, keepdims=True))
            result = jnp.dot(weights.astype(jnp.bfloat16), value_head, preferred_element_type=jnp.float32) / totals
            return result.astype(jnp.bfloat16)
        return lax.map(one_block, jnp.arange(blocks, dtype=jnp.int32)).reshape(TOKENS, HEAD_DIM)
    per_head = lax.map(one_head, jnp.arange(Q_HEADS, dtype=jnp.int32))
    attention = jnp.transpose(per_head, (1, 0, 2)).reshape(TOKENS, Q_HEADS * HEAD_DIM)
    base_table = owner_base(doc_lengths, doc_owners)
    sorted_rank = (lookup(doc_index, base_table - doc_starts) + positions).astype(jnp.int32)
    kv_rows = jnp.concatenate([keys, values], axis=1)
    decode_cache = jnp.zeros_like(kv_rows).at[sorted_rank].set(kv_rows)
    return (attention, decode_cache)
```

```python
import functools
import math

import jax
import jax.numpy as jnp
from jax import lax
from jax.experimental import pallas as pl
from jax.experimental.pallas import tpu as pltpu
from jax.sharding import PartitionSpec as P

HEAD_DIM = 128
Q_HEADS = 32
KV_HEADS = 4
RANK = 256
BLOCK = 256
VMEM_LIMIT = 48 * 1024 * 1024
F32 = jnp.float32
BF16 = jnp.bfloat16
NT = (((1,), (1,)), ((), ()))


def doc_tables(doc_lengths):
    doc_ends = jnp.cumsum(doc_lengths)
    doc_starts = doc_ends - doc_lengths
    return (doc_starts, doc_ends)


def doc_of(positions, doc_ends):
    return jnp.sum((positions[:, None] >= doc_ends[None, :]).astype(jnp.int32), axis=1)


def lookup(doc_index, doc_table):
    doc_numbers = jnp.arange(doc_table.shape[0], dtype=jnp.int32)
    picked = jnp.where(doc_index[:, None] == doc_numbers[None, :], doc_table[None, :], 0)
    return jnp.sum(picked, axis=1)


def owner_base(doc_lengths, doc_owners):
    doc_numbers = jnp.arange(doc_lengths.shape[0], dtype=jnp.int32)
    before = (doc_owners[None, :] < doc_owners[:, None]) | (
        doc_owners[None, :] == doc_owners[:, None]
    ) & (doc_numbers[None, :] < doc_numbers[:, None])
    return jnp.sum(jnp.where(before, doc_lengths[None, :], 0), axis=1)


def per_device_general(hidden_states, queries, latent_down, key_up, value_up, doc_lengths, doc_owners):
    row_count = hidden_states.shape[0]
    tp_count = lax.axis_size("tp")
    sub_count = lax.axis_size("sub")
    tp_index = lax.axis_index("tp")
    sub_index = lax.axis_index("sub")
    partial_sums = jnp.dot(hidden_states, latent_down, preferred_element_type=F32)
    latents = lax.psum(partial_sums, "tp").astype(BF16)
    local_heads = queries.shape[1] // HEAD_DIM
    per_group = Q_HEADS // KV_HEADS
    grouped = min(local_heads, per_group)
    kv_count = local_heads // grouped
    kv_first = tp_index * local_heads // per_group
    key_cols = lax.dynamic_slice_in_dim(key_up, kv_first * HEAD_DIM, kv_count * HEAD_DIM, 1)
    value_cols = lax.dynamic_slice_in_dim(value_up, kv_first * HEAD_DIM, kv_count * HEAD_DIM, 1)
    own_keys = jnp.dot(latents[:, :RANK], key_cols, preferred_element_type=F32).astype(BF16)
    own_values = jnp.dot(latents[:, RANK:], value_cols, preferred_element_type=F32).astype(BF16)
    doc_starts, doc_ends = doc_tables(doc_lengths)
    query_pos = sub_index * row_count + jnp.arange(row_count, dtype=jnp.int32)
    query_doc = doc_of(query_pos, doc_ends)
    query_grid = queries.reshape(row_count, kv_count, grouped, HEAD_DIM)
    inv_root = 1.0 / math.sqrt(HEAD_DIM)
    carried = (
        jnp.full((kv_count, grouped, row_count), -1e30, F32),
        jnp.zeros((kv_count, grouped, row_count), F32),
        jnp.zeros((kv_count, grouped, row_count, HEAD_DIM), F32),
    )
    key_piece = lax.all_gather(own_keys, "sub", axis=0, tiled=True)
    value_piece = lax.all_gather(own_values, "sub", axis=0, tiled=True)
    piece_len = key_piece.shape[0]
    block_len = math.gcd(piece_len, 1024)
    block_total = piece_len // block_len
    key_blocks = key_piece.reshape(block_total, block_len, kv_count, HEAD_DIM)
    value_blocks = value_piece.reshape(block_total, block_len, kv_count, HEAD_DIM)
    first_positions = block_len * jnp.arange(block_total, dtype=jnp.int32)

    def absorb(state, block_item):
        running_top, totals, weighted = state
        key_block, value_block, first_pos = block_item
        key_pos = first_pos + jnp.arange(block_len, dtype=jnp.int32)
        key_doc = doc_of(key_pos, doc_ends)
        allowed = (key_pos[None, :] <= query_pos[:, None]) & (
            key_doc[None, :] == query_doc[:, None]
        )
        scores = (
            jnp.einsum("qkgd,jkd->kgqj", query_grid, key_block, preferred_element_type=F32)
            * inv_root
        )
        scores = jnp.where(allowed, scores, -1e30)
        new_top = jnp.maximum(running_top, jnp.max(scores, axis=-1))
        weights = jnp.where(allowed, jnp.exp(scores - new_top[..., None]), 0.0)
        rescale = jnp.exp(running_top - new_top)
        totals = totals * rescale + jnp.sum(weights, axis=-1)
        weighted = weighted * rescale[..., None] + jnp.einsum(
            "kgqj,jkd->kgqd", weights.astype(BF16), value_block, preferred_element_type=F32
        )
        return ((new_top, totals, weighted), None)

    carried, _ = lax.scan(absorb, carried, (key_blocks, value_blocks, first_positions))
    running_top, totals, weighted = carried
    result = weighted / totals[..., None]
    attention = (
        jnp.transpose(result, (2, 0, 1, 3))
        .reshape(row_count, local_heads * HEAD_DIM)
        .astype(BF16)
    )
    base_table = owner_base(doc_lengths, doc_owners)
    sorted_rank = lookup(query_doc, base_table - doc_starts) + query_pos
    slot_count = row_count // tp_count
    column_span = slot_count * sub_count
    targets = tp_index * column_span + jnp.arange(column_span, dtype=jnp.int32)
    selector = (targets[:, None] == sorted_rank[None, :]).astype(BF16)
    placed = jnp.dot(selector, latents, preferred_element_type=F32)
    arrived = lax.psum_scatter(placed.astype(BF16), "sub", scatter_dimension=0, tiled=True)
    decode_keys = jnp.dot(arrived[:, :RANK], key_up, preferred_element_type=F32).astype(BF16)
    decode_values = jnp.dot(arrived[:, RANK:], value_up, preferred_element_type=F32).astype(BF16)
    decode_cache = jnp.concatenate([decode_keys, decode_values], axis=1)
    return (attention, decode_cache)


SMEM = pl.BlockSpec(memory_space=pltpu.SMEM)
VMEM = pl.BlockSpec(memory_space=pltpu.VMEM)
ANY = pl.BlockSpec(memory_space=pl.ANY)


def params():
    return pltpu.CompilerParams(vmem_limit_bytes=VMEM_LIMIT)


def project_kernel(parts, place, hidden, down, *refs):
    coded, scales = refs[:parts], refs[parts : 2 * parts]
    rows_buf, down_buf, row_sem, down_sem = refs[2 * parts :]
    tp_index = place[0]
    down_copy = pltpu.make_async_copy(down, down_buf, down_sem)
    down_copy.start()
    copies = []
    for k in range(parts):
        chunk = tp_index ^ ((k + 1) % parts)
        copy = pltpu.make_async_copy(
            hidden.at[pl.ds(pl.multiple_of(chunk * BLOCK, BLOCK), BLOCK), :],
            rows_buf.at[k],
            row_sem.at[k],
        )
        copy.start()
        copies.append(copy)
    down_copy.wait()
    for k in range(parts):
        slot = (k + 1) % parts
        copies[k].wait()
        sums = jnp.dot(rows_buf[k], down_buf[...], preferred_element_type=F32)
        steps = []
        for half in range(2):
            piece = sums[:, half * RANK : (half + 1) * RANK]
            top = jnp.max(jnp.abs(piece), axis=1, keepdims=True)
            step = jnp.maximum(top, 1e-30) * (1.0 / 32766.0)
            code = jnp.round(piece * (1.0 / step)).astype(jnp.int32)
            coded[slot][:, half * RANK : (half + 1) * RANK] = code.astype(jnp.int16)
            steps.append(step)
        lane = lax.broadcasted_iota(jnp.int32, (BLOCK, 128), 1)
        table = jnp.where(lane == 0, steps[0], steps[1])
        scales[slot][...] = jnp.transpose(table)[:8, :]


def project(place, hidden, down, parts):
    width = down.shape[1]
    return pl.pallas_call(
        functools.partial(project_kernel, parts),
        out_shape=[jax.ShapeDtypeStruct((BLOCK, width), jnp.int16)] * parts
        + [jax.ShapeDtypeStruct((8, BLOCK), F32)] * parts,
        in_specs=[SMEM, ANY, ANY],
        out_specs=[VMEM] * (2 * parts),
        scratch_shapes=[
            pltpu.VMEM((parts, BLOCK, hidden.shape[1]), BF16),
            pltpu.VMEM(down.shape, BF16),
            pltpu.SemaphoreType.DMA((parts,)),
            pltpu.SemaphoreType.DMA,
        ],
        compiler_params=params(),
        name="project",
    )(place, hidden, down)


def expand_kernel(parts, place, *refs):
    coded, scales = refs[:parts], refs[parts : 2 * parts]
    key_up, value_up = refs[2 * parts : 2 * parts + 2]
    latents_out = refs[2 * parts + 2]
    pieces = refs[2 * parts + 3 :]
    tp_index = place[0]
    halves = []
    columns = [jnp.transpose(scales[k][...]) for k in range(parts)]
    for half in range(2):
        total = None
        for k in range(parts):
            code = coded[k][:, half * RANK : (half + 1) * RANK].astype(jnp.int32).astype(F32)
            term = code * columns[k][:, half : half + 1]
            total = term if total is None else total + term
        halves.append(total.astype(BF16))
        latents_out[:, half * RANK : (half + 1) * RANK] = halves[half]
    for k in range(parts):
        head = tp_index ^ k
        cols = pl.ds(pl.multiple_of(head * HEAD_DIM, HEAD_DIM), HEAD_DIM)
        keys = jnp.dot(halves[0], key_up[:, cols], preferred_element_type=F32).astype(BF16)
        values = lax.dot_general(
            value_up[cols, :], halves[1], NT, preferred_element_type=F32
        ).astype(BF16)
        pieces[k][:HEAD_DIM, :] = values
        pieces[k][HEAD_DIM:, :HEAD_DIM] = keys[:HEAD_DIM]
        pieces[k][HEAD_DIM:, HEAD_DIM:] = keys[HEAD_DIM:]


def expand(place, coded, scales, key_up, value_rows):
    parts = len(coded)
    return pl.pallas_call(
        functools.partial(expand_kernel, parts),
        out_shape=[jax.ShapeDtypeStruct((BLOCK, 2 * RANK), BF16)]
        + [jax.ShapeDtypeStruct((BLOCK, BLOCK), BF16)] * parts,
        in_specs=[SMEM] + [VMEM] * (2 * parts + 2),
        out_specs=[VMEM] * (parts + 1),
        compiler_params=params(),
        name="expand",
    )(place, *coded, *scales, key_up, value_rows)


def pick_kernel(parts, subs, row_count, place, lengths, owners, *refs):
    latents, picked = refs[:subs], refs[subs:]
    tp_index, sub_index = place[0], place[1]
    docs = lengths.shape[0]
    sizes = [lengths[d] for d in range(docs)]
    holders = [owners[d] for d in range(docs)]
    shifts, begins, begin = [], [], 0
    for d in range(docs):
        base = 0
        for e in range(docs):
            if e == d:
                continue
            ahead = holders[e] <= holders[d] if e < d else holders[e] < holders[d]
            base = base + jnp.where(ahead, sizes[e], 0)
        begins.append(begin)
        shifts.append(base - begin)
        begin = begin + sizes[d]
    slot = lax.broadcasted_iota(jnp.int32, (BLOCK, 1), 0) + sub_index * BLOCK
    lane = lax.broadcasted_iota(jnp.int32, (8, BLOCK), 1)
    ranks = []
    for j in range(subs):
        position = lane + (sub_index ^ j) * row_count + tp_index * BLOCK
        shift = jnp.full((8, BLOCK), 0, jnp.int32) + shifts[0]
        for d in range(1, docs):
            shift = jnp.where(position >= begins[d], shifts[d], shift)
        ranks.append((position + shift)[:1])
    for k in range(parts):
        target = slot + (tp_index ^ k) * (subs * BLOCK)
        total = None
        for j in range(subs):
            chosen = jnp.where(target == ranks[j], 1.0, 0.0).astype(BF16)
            term = jnp.dot(chosen, latents[j][...], preferred_element_type=F32)
            total = term if total is None else total + term
        picked[k][...] = total.astype(BF16)


def pick(place, lengths, owners, latents, parts, row_count):
    subs = len(latents)
    return pl.pallas_call(
        functools.partial(pick_kernel, parts, subs, row_count),
        out_shape=[jax.ShapeDtypeStruct((BLOCK, 2 * RANK), BF16)] * parts,
        in_specs=[SMEM] * 3 + [VMEM] * subs,
        out_specs=[VMEM] * parts,
        compiler_params=params(),
        name="pick",
    )(place, lengths, owners, *latents)


def rebuild_kernel(parts, *refs):
    arrived, (key_up, value_up, out) = refs[:parts], refs[parts:]
    total = arrived[0][...]
    for k in range(1, parts):
        total = total + arrived[k][...]
    width = key_up.shape[1]
    out[:, :width] = jnp.dot(total[:, :RANK], key_up[...], preferred_element_type=F32).astype(BF16)
    out[:, width:] = jnp.dot(total[:, RANK:], value_up[...], preferred_element_type=F32).astype(BF16)


def rebuild(arrived, key_up, value_up):
    parts = len(arrived)
    return pl.pallas_call(
        functools.partial(rebuild_kernel, parts),
        out_shape=jax.ShapeDtypeStruct((BLOCK, 2 * key_up.shape[1]), BF16),
        in_specs=[VMEM] * (parts + 2),
        out_specs=VMEM,
        compiler_params=params(),
        name="rebuild",
    )(*arrived, key_up, value_up)


def attend_kernel(parts, subs, heads, row_count, place, lengths, queries, *refs):
    pieces = refs[: parts * subs]
    out, store, tops, sums, mix, sems = refs[parts * subs :]
    step = pl.program_id(0)
    tp_index, sub_index = place[0], place[1]
    docs = lengths.shape[0]

    @pl.when(step == 0)
    def _():
        copies = []
        for j in range(subs):
            for k in range(parts):
                where = (sub_index ^ j) * parts + (tp_index ^ k)
                n = j * parts + k
                copies.append(pltpu.make_async_copy(pieces[n], store.at[where], sems.at[n]))
        for copy in copies:
            copy.start()
        for copy in copies:
            copy.wait()

    first = sub_index * row_count + step * BLOCK
    position = first + lax.broadcasted_iota(jnp.int32, (1, BLOCK), 1)
    begin, low, high = 0, 0, 0
    begin_row = jnp.zeros((1, BLOCK), jnp.int32)
    for d in range(docs):
        begin_row = jnp.where(position >= begin, begin, begin_row)
        low = jnp.where(first >= begin, begin, low)
        high = jnp.where(first + BLOCK - 1 >= begin, begin, high)
        begin = begin + lengths[d]
    own = first // BLOCK
    low_block = low // BLOCK
    full_block = jnp.minimum((high + BLOCK - 1) // BLOCK, own)
    pairs = (own - full_block) // 2
    paired = own - 2 * pairs
    gain = math.log2(math.e) / math.sqrt(HEAD_DIM)
    key_iota = lax.broadcasted_iota(jnp.int32, (BLOCK, BLOCK), 0)

    def scores_of(blocks, head):
        query = queries[:, head * HEAD_DIM : (head + 1) * HEAD_DIM]
        found = []
        for block in blocks:
            for side in range(2):
                keys = store[block, HEAD_DIM:, side * HEAD_DIM : (side + 1) * HEAD_DIM]
                found.append(lax.dot_general(keys, query, NT, preferred_element_type=F32))
        return jnp.concatenate(found, axis=0)

    def product(blocks, weights):
        total = None
        for i, block in enumerate(blocks):
            term = jnp.dot(
                store[block, :HEAD_DIM, :],
                weights[i * BLOCK : (i + 1) * BLOCK],
                preferred_element_type=F32,
            )
            total = term if total is None else total + term
        return total

    def absorb(blocks, allowed, fresh):
        ahead = scores_of(blocks, 0)
        for head in range(heads):
            scores = ahead
            if head + 1 < heads:
                ahead = scores_of(blocks, head + 1)
            scores = scores * gain
            if allowed is not None:
                scores = jnp.where(allowed, scores, -1e30)
            top = jnp.max(scores, axis=0, keepdims=True)
            if not fresh:
                before = tops[head]
                top = jnp.maximum(top, before)
            weights = jnp.exp2(scores - top)
            total = jnp.sum(weights, axis=0, keepdims=True)
            result = product(blocks, weights.astype(BF16))
            tops[head] = top
            if fresh:
                sums[head] = total
                mix[head] = result
            else:
                rescale = jnp.exp2(before - top)
                sums[head] = sums[head] * rescale + total
                mix[head] = mix[head] * rescale + result

    key_pos = key_iota + first
    absorb([own], (key_pos <= position) & (key_pos >= begin_row), True)

    @pl.loop(low_block, paired)
    def _(block):
        absorb([block], key_iota + block * BLOCK >= begin_row, False)

    @pl.loop(0, pairs)
    def _(pair):
        block = paired + 2 * pair
        absorb([block, block + 1], None, False)

    for head in range(heads):
        result = mix[head] * (1.0 / sums[head])
        out[:, head * HEAD_DIM : (head + 1) * HEAD_DIM] = jnp.transpose(result).astype(BF16)


def attend(place, lengths, queries, pieces, parts, subs):
    row_count, width = queries.shape
    heads = width // HEAD_DIM
    row_spec = pl.BlockSpec((BLOCK, width), lambda i: (i, 0))
    return pl.pallas_call(
        functools.partial(attend_kernel, parts, subs, heads, row_count),
        grid=(row_count // BLOCK,),
        out_shape=jax.ShapeDtypeStruct(queries.shape, BF16),
        in_specs=[SMEM, SMEM, row_spec] + [ANY] * (parts * subs),
        out_specs=row_spec,
        scratch_shapes=[
            pltpu.VMEM((parts * subs, BLOCK, BLOCK), BF16),
            pltpu.VMEM((heads, 1, BLOCK), F32),
            pltpu.VMEM((heads, 1, BLOCK), F32),
            pltpu.VMEM((heads, HEAD_DIM, BLOCK), F32),
            pltpu.SemaphoreType.DMA((parts * subs,)),
        ],
        compiler_params=params(),
        name="attend",
    )(place, lengths, queries, *pieces)


def swap(value, axis, bits):
    count = lax.axis_size(axis)
    return lax.ppermute(value, axis, [(i, i ^ bits) for i in range(count)])


def per_device(hidden_states, queries, latent_down, key_up, value_up, doc_lengths, doc_owners):
    row_count = hidden_states.shape[0]
    parts = lax.axis_size("tp")
    subs = lax.axis_size("sub")
    place = jnp.stack([lax.axis_index("tp"), lax.axis_index("sub")]).astype(jnp.int32)
    value_rows = value_up.T
    made = project(place, hidden_states, latent_down, parts)
    coded, scales = made[:parts], made[parts:]
    coded = [coded[0]] + [swap(coded[k], "tp", k) for k in range(1, parts)]
    scales = [scales[0]] + [swap(scales[k], "tp", k) for k in range(1, parts)]
    latents, *pieces = expand(place, coded, scales, key_up, value_rows)
    pieces = [pieces[0]] + [swap(pieces[k], "tp", k) for k in range(1, parts)]

    rows = [latents]
    blocks = [pieces]
    reach = subs // 2
    while reach >= 1:
        rows = rows + [swap(item, "sub", reach) for item in rows]
        blocks = blocks + [[swap(item, "sub", reach) for item in group] for group in blocks]
        reach //= 2
    order = [0]
    reach = subs // 2
    while reach >= 1:
        order = order + [item ^ reach for item in order]
        reach //= 2
    rows = [rows[order.index(j)] for j in range(subs)]
    blocks = [blocks[order.index(j)] for j in range(subs)]

    picked = pick(place, doc_lengths, doc_owners, rows, parts, row_count)
    picked = [picked[0]] + [swap(picked[k], "tp", k) for k in range(1, parts)]
    decode_cache = rebuild(picked, key_up, value_up)
    flat = [item for group in blocks for item in group]
    attention = attend(place, doc_lengths, queries, flat, parts, subs)
    return (attention, decode_cache)


def fits(mesh):
    return mesh.shape["tp"] == KV_HEADS and mesh.shape["sub"] & (mesh.shape["sub"] - 1) == 0


def choose(mesh):
    def run(hidden_states, queries, *rest):
        rows = hidden_states.shape[0]
        direct = fits(mesh) and rows == BLOCK * mesh.shape["tp"]
        return (per_device if direct else per_device_general)(hidden_states, queries, *rest)

    return run


def solution(mesh):
    return jax.shard_map(
        choose(mesh),
        mesh=mesh,
        in_specs=(
            P(("groups", "sub"), "tp"),
            P(("groups", "sub"), "tp"),
            P("tp", None),
            P(),
            P(),
            P("groups"),
            P("groups"),
        ),
        out_specs=(P(("groups", "sub"), "tp"), P(("groups", "tp", "sub"), None)),
        check_vma=False,
    )
```

```python
import functools
import math

import jax
import jax.numpy as jnp
from jax import lax
from jax.experimental import pallas as pl
from jax.experimental.pallas import tpu as pltpu
from jax.sharding import PartitionSpec as P

HEAD_DIM = 128
Q_HEADS = 32
KV_HEADS = 4
RANK = 256
BLOCK = 256
SLICES = 4
AHEAD = 3
SCALE_ROWS = 16
CODE_TOP = 32000.0
LIFT = 24.0
SPAN = 100.0
VMEM_LIMIT = 48 * 1024 * 1024
F32 = jnp.float32
BF16 = jnp.bfloat16
NT = (((1,), (1,)), ((), ()))


def doc_tables(doc_lengths):
    doc_ends = jnp.cumsum(doc_lengths)
    doc_starts = doc_ends - doc_lengths
    return (doc_starts, doc_ends)


def doc_of(positions, doc_ends):
    return jnp.sum((positions[:, None] >= doc_ends[None, :]).astype(jnp.int32), axis=1)


def lookup(doc_index, doc_table):
    doc_numbers = jnp.arange(doc_table.shape[0], dtype=jnp.int32)
    picked = jnp.where(doc_index[:, None] == doc_numbers[None, :], doc_table[None, :], 0)
    return jnp.sum(picked, axis=1)


def owner_base(doc_lengths, doc_owners):
    doc_numbers = jnp.arange(doc_lengths.shape[0], dtype=jnp.int32)
    before = (doc_owners[None, :] < doc_owners[:, None]) | (
        doc_owners[None, :] == doc_owners[:, None]
    ) & (doc_numbers[None, :] < doc_numbers[:, None])
    return jnp.sum(jnp.where(before, doc_lengths[None, :], 0), axis=1)


def per_device_general(hidden_states, queries, latent_down, key_up, value_up, doc_lengths, doc_owners):
    row_count = hidden_states.shape[0]
    tp_count = lax.axis_size("tp")
    sub_count = lax.axis_size("sub")
    tp_index = lax.axis_index("tp")
    sub_index = lax.axis_index("sub")
    partial_sums = jnp.dot(hidden_states, latent_down, preferred_element_type=F32)
    latents = lax.psum(partial_sums, "tp").astype(BF16)
    local_heads = queries.shape[1] // HEAD_DIM
    per_group = Q_HEADS // KV_HEADS
    grouped = min(local_heads, per_group)
    kv_count = local_heads // grouped
    kv_first = tp_index * local_heads // per_group
    key_cols = lax.dynamic_slice_in_dim(key_up, kv_first * HEAD_DIM, kv_count * HEAD_DIM, 1)
    value_cols = lax.dynamic_slice_in_dim(value_up, kv_first * HEAD_DIM, kv_count * HEAD_DIM, 1)
    own_keys = jnp.dot(latents[:, :RANK], key_cols, preferred_element_type=F32).astype(BF16)
    own_values = jnp.dot(latents[:, RANK:], value_cols, preferred_element_type=F32).astype(BF16)
    doc_starts, doc_ends = doc_tables(doc_lengths)
    query_pos = sub_index * row_count + jnp.arange(row_count, dtype=jnp.int32)
    query_doc = doc_of(query_pos, doc_ends)
    query_grid = queries.reshape(row_count, kv_count, grouped, HEAD_DIM)
    inv_root = 1.0 / math.sqrt(HEAD_DIM)
    carried = (
        jnp.full((kv_count, grouped, row_count), -1e30, F32),
        jnp.zeros((kv_count, grouped, row_count), F32),
        jnp.zeros((kv_count, grouped, row_count, HEAD_DIM), F32),
    )
    key_piece = lax.all_gather(own_keys, "sub", axis=0, tiled=True)
    value_piece = lax.all_gather(own_values, "sub", axis=0, tiled=True)
    piece_len = key_piece.shape[0]
    block_len = math.gcd(piece_len, 1024)
    block_total = piece_len // block_len
    key_blocks = key_piece.reshape(block_total, block_len, kv_count, HEAD_DIM)
    value_blocks = value_piece.reshape(block_total, block_len, kv_count, HEAD_DIM)
    first_positions = block_len * jnp.arange(block_total, dtype=jnp.int32)

    def absorb(state, block_item):
        running_top, totals, weighted = state
        key_block, value_block, first_pos = block_item
        key_pos = first_pos + jnp.arange(block_len, dtype=jnp.int32)
        key_doc = doc_of(key_pos, doc_ends)
        allowed = (key_pos[None, :] <= query_pos[:, None]) & (
            key_doc[None, :] == query_doc[:, None]
        )
        scores = (
            jnp.einsum("qkgd,jkd->kgqj", query_grid, key_block, preferred_element_type=F32)
            * inv_root
        )
        scores = jnp.where(allowed, scores, -1e30)
        new_top = jnp.maximum(running_top, jnp.max(scores, axis=-1))
        weights = jnp.where(allowed, jnp.exp(scores - new_top[..., None]), 0.0)
        rescale = jnp.exp(running_top - new_top)
        totals = totals * rescale + jnp.sum(weights, axis=-1)
        weighted = weighted * rescale[..., None] + jnp.einsum(
            "kgqj,jkd->kgqd", weights.astype(BF16), value_block, preferred_element_type=F32
        )
        return ((new_top, totals, weighted), None)

    carried, _ = lax.scan(absorb, carried, (key_blocks, value_blocks, first_positions))
    running_top, totals, weighted = carried
    result = weighted / totals[..., None]
    attention = (
        jnp.transpose(result, (2, 0, 1, 3))
        .reshape(row_count, local_heads * HEAD_DIM)
        .astype(BF16)
    )
    base_table = owner_base(doc_lengths, doc_owners)
    sorted_rank = lookup(query_doc, base_table - doc_starts) + query_pos
    slot_count = row_count // tp_count
    column_span = slot_count * sub_count
    targets = tp_index * column_span + jnp.arange(column_span, dtype=jnp.int32)
    selector = (targets[:, None] == sorted_rank[None, :]).astype(BF16)
    placed = jnp.dot(selector, latents, preferred_element_type=F32)
    arrived = lax.psum_scatter(placed.astype(BF16), "sub", scatter_dimension=0, tiled=True)
    decode_keys = jnp.dot(arrived[:, :RANK], key_up, preferred_element_type=F32).astype(BF16)
    decode_values = jnp.dot(arrived[:, RANK:], value_up, preferred_element_type=F32).astype(BF16)
    decode_cache = jnp.concatenate([decode_keys, decode_values], axis=1)
    return (attention, decode_cache)


SMEM = pl.BlockSpec(memory_space=pltpu.SMEM)
VMEM = pl.BlockSpec(memory_space=pltpu.VMEM)
ANY = pl.BlockSpec(memory_space=pl.ANY)


def params():
    return pltpu.CompilerParams(vmem_limit_bytes=VMEM_LIMIT)


def project_kernel(chunks, place, hidden, down, *refs):
    count = len(chunks)
    coded = refs[:count]
    rows_buf, down_buf, row_sem, down_sem = refs[count:]
    tp_index = place[0]
    depth = down.shape[0] // SLICES
    down_copies, row_copies = [], []
    for c in range(SLICES):
        span = pl.ds(c * depth, depth)
        down_copies.append(
            pltpu.make_async_copy(down.at[span, :], down_buf.at[span, :], down_sem.at[c])
        )
        down_copies[c].start()
        for k in range(count):
            first = pl.multiple_of((tp_index ^ chunks[k]) * BLOCK, BLOCK)
            copy = pltpu.make_async_copy(
                hidden.at[pl.ds(first, BLOCK), span],
                rows_buf.at[k, :, span],
                row_sem.at[k * SLICES + c],
            )
            copy.start()
            row_copies.append(copy)
    sums = [None] * count
    for c in range(SLICES):
        span = slice(c * depth, (c + 1) * depth)
        down_copies[c].wait()
        for k in range(count):
            row_copies[c * count + k].wait()
            term = jnp.dot(rows_buf[k, :, span], down_buf[span, :], preferred_element_type=F32)
            sums[k] = term if c == 0 else sums[k] + term
    lane = lax.broadcasted_iota(jnp.int32, (BLOCK, 128), 1)
    for k in range(count):
        powers = []
        for half in range(2):
            piece = sums[k][:, half * RANK : (half + 1) * RANK]
            top = jnp.max(jnp.abs(piece), axis=1, keepdims=True)
            power = jnp.ceil(jnp.log2(jnp.maximum(top, 1e-30)) + 1e-3)
            code = jnp.round(piece * (CODE_TOP * jnp.exp2(-power))).astype(jnp.int32)
            coded[k][:BLOCK, half * RANK : (half + 1) * RANK] = code.astype(jnp.int16)
            powers.append(power)
        table = jnp.transpose(jnp.where(lane == 0, powers[0], powers[1]))[:SCALE_ROWS]
        table = table.astype(jnp.int32).astype(jnp.int16)
        coded[k][BLOCK:, :RANK] = table
        coded[k][BLOCK:, RANK:] = table


def project(place, hidden, down, chunks):
    width = down.shape[1]
    count = len(chunks)
    return pl.pallas_call(
        functools.partial(project_kernel, chunks),
        out_shape=[jax.ShapeDtypeStruct((BLOCK + SCALE_ROWS, width), jnp.int16)] * count,
        in_specs=[SMEM, ANY, ANY],
        out_specs=[VMEM] * count,
        scratch_shapes=[
            pltpu.VMEM((count, BLOCK, hidden.shape[1]), BF16),
            pltpu.VMEM(down.shape, BF16),
            pltpu.SemaphoreType.DMA((count * SLICES,)),
            pltpu.SemaphoreType.DMA((SLICES,)),
        ],
        compiler_params=pltpu.CompilerParams(vmem_limit_bytes=60 * 1024 * 1024),
        name="project",
    )(place, hidden, down)


def expand_kernel(parts, place, *refs):
    coded = refs[:parts]
    key_up, value_up, latents_out = refs[parts : parts + 3]
    pieces = refs[parts + 3 :]
    tp_index = place[0]
    halves = []
    columns = []
    for k in range(parts):
        powers = coded[k][BLOCK:, :RANK].astype(jnp.int32).astype(F32)
        columns.append(jnp.transpose(jnp.exp2(powers) * (1.0 / CODE_TOP)))
    for half in range(2):
        total = None
        for k in range(parts):
            code = coded[k][:BLOCK, half * RANK : (half + 1) * RANK].astype(jnp.int32).astype(F32)
            term = code * columns[k][:, half : half + 1]
            total = term if total is None else total + term
        halves.append(total.astype(BF16))
        latents_out[:, half * RANK : (half + 1) * RANK] = halves[half]
    for k in range(parts):
        head = tp_index ^ k
        cols = pl.ds(pl.multiple_of(head * HEAD_DIM, HEAD_DIM), HEAD_DIM)
        keys = jnp.dot(halves[0], key_up[:, cols], preferred_element_type=F32).astype(BF16)
        values = lax.dot_general(
            value_up[cols, :], halves[1], NT, preferred_element_type=F32
        ).astype(BF16)
        pieces[k][:HEAD_DIM, :] = values
        pieces[k][HEAD_DIM:, :HEAD_DIM] = keys[:HEAD_DIM]
        pieces[k][HEAD_DIM:, HEAD_DIM:] = keys[HEAD_DIM:]


def expand(place, coded, key_up, value_rows):
    parts = len(coded)
    return pl.pallas_call(
        functools.partial(expand_kernel, parts),
        out_shape=[jax.ShapeDtypeStruct((BLOCK, 2 * RANK), BF16)]
        + [jax.ShapeDtypeStruct((BLOCK, BLOCK), BF16)] * parts,
        in_specs=[SMEM] + [VMEM] * (parts + 2),
        out_specs=[VMEM] * (parts + 1),
        compiler_params=params(),
        name="expand",
    )(place, *coded, key_up, value_rows)


def pick_kernel(parts, subs, row_count, place, lengths, owners, *refs):
    latents, picked = refs[:subs], refs[subs:]
    tp_index, sub_index = place[0], place[1]
    docs = lengths.shape[0]
    sizes = [lengths[d] for d in range(docs)]
    holders = [owners[d] for d in range(docs)]
    shifts, begins, begin = [], [], 0
    for d in range(docs):
        base = 0
        for e in range(docs):
            if e == d:
                continue
            ahead = holders[e] <= holders[d] if e < d else holders[e] < holders[d]
            base = base + jnp.where(ahead, sizes[e], 0)
        begins.append(begin)
        shifts.append(base - begin)
        begin = begin + sizes[d]
    slot = lax.broadcasted_iota(jnp.int32, (BLOCK, 1), 0) + sub_index * BLOCK
    lane = lax.broadcasted_iota(jnp.int32, (8, BLOCK), 1)
    ranks = []
    for j in range(subs):
        position = lane + (sub_index ^ j) * row_count + tp_index * BLOCK
        shift = jnp.full((8, BLOCK), 0, jnp.int32) + shifts[0]
        for d in range(1, docs):
            shift = jnp.where(position >= begins[d], shifts[d], shift)
        ranks.append((position + shift)[:1])
    for k in range(parts):
        target = slot + (tp_index ^ k) * (subs * BLOCK)
        total = None
        for j in range(subs):
            chosen = jnp.where(target == ranks[j], 1.0, 0.0).astype(BF16)
            term = jnp.dot(chosen, latents[j][...], preferred_element_type=F32)
            total = term if total is None else total + term
        picked[k][...] = total.astype(BF16)


def pick(place, lengths, owners, latents, parts, row_count):
    subs = len(latents)
    return pl.pallas_call(
        functools.partial(pick_kernel, parts, subs, row_count),
        out_shape=[jax.ShapeDtypeStruct((BLOCK, 2 * RANK), BF16)] * parts,
        in_specs=[SMEM] * 3 + [VMEM] * subs,
        out_specs=[VMEM] * parts,
        compiler_params=params(),
        name="pick",
    )(place, lengths, owners, *latents)


def rebuild_kernel(parts, *refs):
    arrived, (key_up, value_up, out) = refs[:parts], refs[parts:]
    total = arrived[0][...]
    for k in range(1, parts):
        total = total + arrived[k][...]
    width = key_up.shape[1]
    out[:, :width] = jnp.dot(total[:, :RANK], key_up[...], preferred_element_type=F32).astype(BF16)
    out[:, width:] = jnp.dot(total[:, RANK:], value_up[...], preferred_element_type=F32).astype(BF16)


def rebuild(arrived, key_up, value_up):
    parts = len(arrived)
    return pl.pallas_call(
        functools.partial(rebuild_kernel, parts),
        out_shape=jax.ShapeDtypeStruct((BLOCK, 2 * key_up.shape[1]), BF16),
        in_specs=[VMEM] * (parts + 2),
        out_specs=VMEM,
        compiler_params=params(),
        name="rebuild",
    )(*arrived, key_up, value_up)


def attend_kernel(parts, subs, heads, row_count, place, lengths, queries, *refs):
    pieces = refs[: parts * subs]
    out, keys, values, tops, sums, mix, key_top, sems = refs[parts * subs :]
    step = pl.program_id(0)
    tp_index, sub_index = place[0], place[1]
    docs = lengths.shape[0]
    ones = jnp.ones((8, HEAD_DIM), BF16)

    @pl.when(step == 0)
    def _():
        copies = []
        for j in range(subs):
            for k in range(parts):
                n = j * parts + k
                first = pl.multiple_of(((sub_index ^ j) * parts + (tp_index ^ k)) * BLOCK, BLOCK)
                copies.append(
                    pltpu.make_async_copy(
                        pieces[n].at[:HEAD_DIM, :], values.at[:, pl.ds(first, BLOCK)], sems.at[n, 0]
                    )
                )
                for side in range(2):
                    copies.append(
                        pltpu.make_async_copy(
                            pieces[n].at[HEAD_DIM:, side * HEAD_DIM : (side + 1) * HEAD_DIM],
                            keys.at[pl.ds(first + side * HEAD_DIM, HEAD_DIM), :],
                            sems.at[n, side + 1],
                        )
                    )
        for copy in copies:
            copy.start()
        for copy in copies:
            copy.wait()
        every = keys[...]
        squares = lax.dot_general(ones, every * every, NT, preferred_element_type=F32)
        key_top[0] = jnp.max(squares)

    first = sub_index * row_count + step * BLOCK
    position = first + lax.broadcasted_iota(jnp.int32, (1, BLOCK), 1)
    begin, low, high = 0, 0, 0
    begin_row = jnp.zeros((1, BLOCK), jnp.int32)
    for d in range(docs):
        begin_row = jnp.where(position >= begin, begin, begin_row)
        low = jnp.where(first >= begin, begin, low)
        high = jnp.where(first + BLOCK - 1 >= begin, begin, high)
        begin = begin + lengths[d]
    own = first // BLOCK
    low_block = low // BLOCK
    full_block = jnp.minimum((high + BLOCK - 1) // BLOCK, own)
    pairs = (own - full_block) // 2
    paired = own - 2 * pairs
    gain = math.log2(math.e) / math.sqrt(HEAD_DIM)
    key_iota = lax.broadcasted_iota(jnp.int32, (BLOCK, BLOCK), 0)

    def query_of(head):
        return queries[:, head * HEAD_DIM : (head + 1) * HEAD_DIM]

    def absorb(block, count, allowed, fresh, online):
        span = pl.ds(pl.multiple_of(block * BLOCK, BLOCK), count * BLOCK)

        def scores_of(head):
            return lax.dot_general(keys[span, :], query_of(head), NT, preferred_element_type=F32)

        ahead = [scores_of(head) for head in range(min(AHEAD, heads))]
        for head in range(heads):
            scores = ahead.pop(0) * gain
            if head + AHEAD < heads:
                ahead.append(scores_of(head + AHEAD))
            if allowed is not None:
                scores = jnp.where(allowed, scores, -1e30)
            if fresh:
                top = jnp.max(scores, axis=0, keepdims=True) + LIFT
                tops[head] = top
            elif online:
                before = tops[head]
                top = jnp.maximum(before, jnp.max(scores, axis=0, keepdims=True) + LIFT)
                tops[head] = top
            else:
                top = tops[head]
            weights = jnp.exp2(scores - top)
            total = jnp.sum(weights, axis=0, keepdims=True)
            result = jnp.dot(values[:, span], weights.astype(BF16), preferred_element_type=F32)
            if fresh:
                sums[head] = total
                mix[head] = result
            elif online:
                rescale = jnp.exp2(before - top)
                sums[head] = sums[head] * rescale + total
                mix[head] = mix[head] * rescale + result
            else:
                sums[head] += total
                mix[head] += result

    def sweep(online):
        @pl.loop(low_block, paired)
        def _(block):
            absorb(block, 1, key_iota + block * BLOCK >= begin_row, False, online)

        @pl.loop(0, pairs)
        def _(pair):
            absorb(paired + 2 * pair, 2, None, False, online)

    key_pos = key_iota + first
    absorb(own, 1, (key_pos <= position) & (key_pos >= begin_row), True, False)

    reach = jnp.full((1, BLOCK), -1e30, F32)
    for head in range(heads):
        query = query_of(head)
        squares = lax.dot_general(ones, query * query, NT, preferred_element_type=F32)[:1]
        most = jnp.sqrt(squares * key_top[0]) * (gain * 1.02)
        reach = jnp.maximum(reach, most - (tops[head] - LIFT))
    safe = jnp.max(reach) <= SPAN

    @pl.when(safe)
    def _():
        sweep(False)

    @pl.when(jnp.logical_not(safe))
    def _():
        sweep(True)

    for head in range(heads):
        result = mix[head] * (1.0 / sums[head])
        out[:, head * HEAD_DIM : (head + 1) * HEAD_DIM] = jnp.transpose(result).astype(BF16)


def attend(place, lengths, queries, pieces, parts, subs):
    row_count, width = queries.shape
    heads = width // HEAD_DIM
    row_spec = pl.BlockSpec((BLOCK, width), lambda i: (i, 0))
    total = parts * subs
    return pl.pallas_call(
        functools.partial(attend_kernel, parts, subs, heads, row_count),
        grid=(row_count // BLOCK,),
        out_shape=jax.ShapeDtypeStruct(queries.shape, BF16),
        in_specs=[SMEM, SMEM, row_spec] + [ANY] * total,
        out_specs=row_spec,
        scratch_shapes=[
            pltpu.VMEM((total * BLOCK, HEAD_DIM), BF16),
            pltpu.VMEM((HEAD_DIM, total * BLOCK), BF16),
            pltpu.VMEM((heads, 1, BLOCK), F32),
            pltpu.VMEM((heads, 1, BLOCK), F32),
            pltpu.VMEM((heads, HEAD_DIM, BLOCK), F32),
            pltpu.SMEM((1,), F32),
            pltpu.SemaphoreType.DMA((total, 3)),
        ],
        compiler_params=params(),
        name="attend",
    )(place, lengths, queries, *pieces)


def swap(value, axis, bits):
    count = lax.axis_size(axis)
    return lax.ppermute(value, axis, [(i, i ^ bits) for i in range(count)])


def per_device(hidden_states, queries, latent_down, key_up, value_up, doc_lengths, doc_owners):
    row_count = hidden_states.shape[0]
    parts = lax.axis_size("tp")
    subs = lax.axis_size("sub")
    place = jnp.stack([lax.axis_index("tp"), lax.axis_index("sub")]).astype(jnp.int32)
    value_rows = value_up.T
    far = project(place, hidden_states, latent_down, tuple(range(parts // 2, parts)))
    far = [swap(item, "tp", k) for k, item in enumerate(far, parts // 2)]
    near = project(place, hidden_states, latent_down, tuple(range(parts // 2)))
    near = [near[0]] + [swap(item, "tp", k) for k, item in enumerate(near[1:], 1)]
    coded = near + far
    latents, *pieces = expand(place, coded, key_up, value_rows)
    pieces = [pieces[0]] + [swap(pieces[k], "tp", k) for k in range(1, parts)]

    rows = [latents]
    blocks = [pieces]
    reach = subs // 2
    while reach >= 1:
        rows = rows + [swap(item, "sub", reach) for item in rows]
        blocks = blocks + [[swap(item, "sub", reach) for item in group] for group in blocks]
        reach //= 2
    order = [0]
    reach = subs // 2
    while reach >= 1:
        order = order + [item ^ reach for item in order]
        reach //= 2
    rows = [rows[order.index(j)] for j in range(subs)]
    blocks = [blocks[order.index(j)] for j in range(subs)]

    picked = pick(place, doc_lengths, doc_owners, rows, parts, row_count)
    picked = [picked[0]] + [swap(picked[k], "tp", k) for k in range(1, parts)]
    decode_cache = rebuild(picked, key_up, value_up)
    flat = [item for group in blocks for item in group]
    attention = attend(place, doc_lengths, queries, flat, parts, subs)
    return (attention, decode_cache)


def fits(mesh):
    return mesh.shape["tp"] == KV_HEADS and mesh.shape["sub"] & (mesh.shape["sub"] - 1) == 0


def choose(mesh):
    def run(hidden_states, queries, *rest):
        rows = hidden_states.shape[0]
        direct = fits(mesh) and rows == BLOCK * mesh.shape["tp"]
        return (per_device if direct else per_device_general)(hidden_states, queries, *rest)

    return run


def solution(mesh):
    return jax.shard_map(
        choose(mesh),
        mesh=mesh,
        in_specs=(
            P(("groups", "sub"), "tp"),
            P(("groups", "sub"), "tp"),
            P("tp", None),
            P(),
            P(),
            P("groups"),
            P("groups"),
        ),
        out_specs=(P(("groups", "sub"), "tp"), P(("groups", "tp", "sub"), None)),
        check_vma=False,
    )
```

```python
import functools
import math

import jax
import jax.numpy as jnp
from jax import lax
from jax.experimental import pallas as pl
from jax.experimental.pallas import tpu as pltpu
from jax.sharding import PartitionSpec as P

HEAD_DIM = 128
Q_HEADS = 32
KV_HEADS = 4
RANK = 256
BLOCK = 256
SLICES = 4
AHEAD = 3
SCALE_ROWS = 16
CODE_TOP = 32000.0
LIFT = 24.0
SPAN = 100.0
VMEM_LIMIT = 48 * 1024 * 1024
F32 = jnp.float32
BF16 = jnp.bfloat16
NT = (((1,), (1,)), ((), ()))


def doc_tables(doc_lengths):
    doc_ends = jnp.cumsum(doc_lengths)
    doc_starts = doc_ends - doc_lengths
    return (doc_starts, doc_ends)


def doc_of(positions, doc_ends):
    return jnp.sum((positions[:, None] >= doc_ends[None, :]).astype(jnp.int32), axis=1)


def lookup(doc_index, doc_table):
    doc_numbers = jnp.arange(doc_table.shape[0], dtype=jnp.int32)
    picked = jnp.where(doc_index[:, None] == doc_numbers[None, :], doc_table[None, :], 0)
    return jnp.sum(picked, axis=1)


def owner_base(doc_lengths, doc_owners):
    doc_numbers = jnp.arange(doc_lengths.shape[0], dtype=jnp.int32)
    before = (doc_owners[None, :] < doc_owners[:, None]) | (
        doc_owners[None, :] == doc_owners[:, None]
    ) & (doc_numbers[None, :] < doc_numbers[:, None])
    return jnp.sum(jnp.where(before, doc_lengths[None, :], 0), axis=1)


def per_device_general(hidden_states, queries, latent_down, key_up, value_up, doc_lengths, doc_owners):
    row_count = hidden_states.shape[0]
    tp_count = lax.axis_size("tp")
    sub_count = lax.axis_size("sub")
    tp_index = lax.axis_index("tp")
    sub_index = lax.axis_index("sub")
    partial_sums = jnp.dot(hidden_states, latent_down, preferred_element_type=F32)
    latents = lax.psum(partial_sums, "tp").astype(BF16)
    local_heads = queries.shape[1] // HEAD_DIM
    per_group = Q_HEADS // KV_HEADS
    grouped = min(local_heads, per_group)
    kv_count = local_heads // grouped
    kv_first = tp_index * local_heads // per_group
    key_cols = lax.dynamic_slice_in_dim(key_up, kv_first * HEAD_DIM, kv_count * HEAD_DIM, 1)
    value_cols = lax.dynamic_slice_in_dim(value_up, kv_first * HEAD_DIM, kv_count * HEAD_DIM, 1)
    own_keys = jnp.dot(latents[:, :RANK], key_cols, preferred_element_type=F32).astype(BF16)
    own_values = jnp.dot(latents[:, RANK:], value_cols, preferred_element_type=F32).astype(BF16)
    doc_starts, doc_ends = doc_tables(doc_lengths)
    query_pos = sub_index * row_count + jnp.arange(row_count, dtype=jnp.int32)
    query_doc = doc_of(query_pos, doc_ends)
    query_grid = queries.reshape(row_count, kv_count, grouped, HEAD_DIM)
    inv_root = 1.0 / math.sqrt(HEAD_DIM)
    carried = (
        jnp.full((kv_count, grouped, row_count), -1e30, F32),
        jnp.zeros((kv_count, grouped, row_count), F32),
        jnp.zeros((kv_count, grouped, row_count, HEAD_DIM), F32),
    )
    key_piece = lax.all_gather(own_keys, "sub", axis=0, tiled=True)
    value_piece = lax.all_gather(own_values, "sub", axis=0, tiled=True)
    piece_len = key_piece.shape[0]
    block_len = math.gcd(piece_len, 1024)
    block_total = piece_len // block_len
    key_blocks = key_piece.reshape(block_total, block_len, kv_count, HEAD_DIM)
    value_blocks = value_piece.reshape(block_total, block_len, kv_count, HEAD_DIM)
    first_positions = block_len * jnp.arange(block_total, dtype=jnp.int32)

    def absorb(state, block_item):
        running_top, totals, weighted = state
        key_block, value_block, first_pos = block_item
        key_pos = first_pos + jnp.arange(block_len, dtype=jnp.int32)
        key_doc = doc_of(key_pos, doc_ends)
        allowed = (key_pos[None, :] <= query_pos[:, None]) & (
            key_doc[None, :] == query_doc[:, None]
        )
        scores = (
            jnp.einsum("qkgd,jkd->kgqj", query_grid, key_block, preferred_element_type=F32)
            * inv_root
        )
        scores = jnp.where(allowed, scores, -1e30)
        new_top = jnp.maximum(running_top, jnp.max(scores, axis=-1))
        weights = jnp.where(allowed, jnp.exp(scores - new_top[..., None]), 0.0)
        rescale = jnp.exp(running_top - new_top)
        totals = totals * rescale + jnp.sum(weights, axis=-1)
        weighted = weighted * rescale[..., None] + jnp.einsum(
            "kgqj,jkd->kgqd", weights.astype(BF16), value_block, preferred_element_type=F32
        )
        return ((new_top, totals, weighted), None)

    carried, _ = lax.scan(absorb, carried, (key_blocks, value_blocks, first_positions))
    running_top, totals, weighted = carried
    result = weighted / totals[..., None]
    attention = (
        jnp.transpose(result, (2, 0, 1, 3))
        .reshape(row_count, local_heads * HEAD_DIM)
        .astype(BF16)
    )
    base_table = owner_base(doc_lengths, doc_owners)
    sorted_rank = lookup(query_doc, base_table - doc_starts) + query_pos
    slot_count = row_count // tp_count
    column_span = slot_count * sub_count
    targets = tp_index * column_span + jnp.arange(column_span, dtype=jnp.int32)
    selector = (targets[:, None] == sorted_rank[None, :]).astype(BF16)
    placed = jnp.dot(selector, latents, preferred_element_type=F32)
    arrived = lax.psum_scatter(placed.astype(BF16), "sub", scatter_dimension=0, tiled=True)
    decode_keys = jnp.dot(arrived[:, :RANK], key_up, preferred_element_type=F32).astype(BF16)
    decode_values = jnp.dot(arrived[:, RANK:], value_up, preferred_element_type=F32).astype(BF16)
    decode_cache = jnp.concatenate([decode_keys, decode_values], axis=1)
    return (attention, decode_cache)


SMEM = pl.BlockSpec(memory_space=pltpu.SMEM)
VMEM = pl.BlockSpec(memory_space=pltpu.VMEM)
ANY = pl.BlockSpec(memory_space=pl.ANY)


def params():
    return pltpu.CompilerParams(vmem_limit_bytes=VMEM_LIMIT)


def project_kernel(chunks, place, hidden, down, *refs):
    count = len(chunks)
    coded = refs[:count]
    rows_buf, down_buf, row_sem, down_sem = refs[count:]
    tp_index = place[0]
    depth = down.shape[0] // SLICES
    down_copies, row_copies = [], []
    for c in range(SLICES):
        span = pl.ds(c * depth, depth)
        down_copies.append(
            pltpu.make_async_copy(down.at[span, :], down_buf.at[span, :], down_sem.at[c])
        )
        down_copies[c].start()
        for k in range(count):
            first = pl.multiple_of((tp_index ^ chunks[k]) * BLOCK, BLOCK)
            copy = pltpu.make_async_copy(
                hidden.at[pl.ds(first, BLOCK), span],
                rows_buf.at[k, :, span],
                row_sem.at[k * SLICES + c],
            )
            copy.start()
            row_copies.append(copy)
    sums = [None] * count
    for c in range(SLICES):
        span = slice(c * depth, (c + 1) * depth)
        down_copies[c].wait()
        for k in range(count):
            row_copies[c * count + k].wait()
            term = jnp.dot(rows_buf[k, :, span], down_buf[span, :], preferred_element_type=F32)
            sums[k] = term if c == 0 else sums[k] + term
    lane = lax.broadcasted_iota(jnp.int32, (BLOCK, 128), 1)
    for k in range(count):
        powers = []
        for half in range(2):
            piece = sums[k][:, half * RANK : (half + 1) * RANK]
            top = jnp.max(jnp.abs(piece), axis=1, keepdims=True)
            power = jnp.ceil(jnp.log2(jnp.maximum(top, 1e-30)) + 1e-3)
            code = jnp.round(piece * (CODE_TOP * jnp.exp2(-power))).astype(jnp.int32)
            coded[k][:BLOCK, half * RANK : (half + 1) * RANK] = code.astype(jnp.int16)
            powers.append(power)
        table = jnp.transpose(jnp.where(lane == 0, powers[0], powers[1]))[:SCALE_ROWS]
        table = table.astype(jnp.int32).astype(jnp.int16)
        coded[k][BLOCK:, :RANK] = table
        coded[k][BLOCK:, RANK:] = table


def project(place, hidden, down, chunks):
    width = down.shape[1]
    count = len(chunks)
    return pl.pallas_call(
        functools.partial(project_kernel, chunks),
        out_shape=[jax.ShapeDtypeStruct((BLOCK + SCALE_ROWS, width), jnp.int16)] * count,
        in_specs=[SMEM, ANY, ANY],
        out_specs=[VMEM] * count,
        scratch_shapes=[
            pltpu.VMEM((count, BLOCK, hidden.shape[1]), BF16),
            pltpu.VMEM(down.shape, BF16),
            pltpu.SemaphoreType.DMA((count * SLICES,)),
            pltpu.SemaphoreType.DMA((SLICES,)),
        ],
        compiler_params=pltpu.CompilerParams(vmem_limit_bytes=60 * 1024 * 1024),
        name="project",
    )(place, hidden, down)


def expand_kernel(parts, place, *refs):
    coded = refs[:parts]
    key_up, value_up, latents_out = refs[parts : parts + 3]
    pieces = refs[parts + 3 :]
    tp_index = place[0]
    halves = []
    columns = []
    for k in range(parts):
        powers = coded[k][BLOCK:, :RANK].astype(jnp.int32).astype(F32)
        columns.append(jnp.transpose(jnp.exp2(powers) * (1.0 / CODE_TOP)))
    for half in range(2):
        total = None
        for k in range(parts):
            code = coded[k][:BLOCK, half * RANK : (half + 1) * RANK].astype(jnp.int32).astype(F32)
            term = code * columns[k][:, half : half + 1]
            total = term if total is None else total + term
        halves.append(total.astype(BF16))
        latents_out[:, half * RANK : (half + 1) * RANK] = halves[half]
    for k in range(parts):
        head = tp_index ^ k
        cols = pl.ds(pl.multiple_of(head * HEAD_DIM, HEAD_DIM), HEAD_DIM)
        keys = jnp.dot(halves[0], key_up[:, cols], preferred_element_type=F32).astype(BF16)
        values = lax.dot_general(
            value_up[cols, :], halves[1], NT, preferred_element_type=F32
        ).astype(BF16)
        pieces[k][:HEAD_DIM, :] = values
        pieces[k][HEAD_DIM:, :HEAD_DIM] = keys[:HEAD_DIM]
        pieces[k][HEAD_DIM:, HEAD_DIM:] = keys[HEAD_DIM:]


def expand(place, coded, key_up, value_rows):
    parts = len(coded)
    return pl.pallas_call(
        functools.partial(expand_kernel, parts),
        out_shape=[jax.ShapeDtypeStruct((BLOCK, 2 * RANK), BF16)]
        + [jax.ShapeDtypeStruct((BLOCK, BLOCK), BF16)] * parts,
        in_specs=[SMEM] + [VMEM] * (parts + 2),
        out_specs=[VMEM] * (parts + 1),
        compiler_params=params(),
        name="expand",
    )(place, *coded, key_up, value_rows)


def pick_kernel(parts, subs, row_count, place, lengths, owners, *refs):
    latents, picked = refs[:subs], refs[subs:]
    tp_index, sub_index = place[0], place[1]
    docs = lengths.shape[0]
    sizes = [lengths[d] for d in range(docs)]
    holders = [owners[d] for d in range(docs)]
    shifts, begins, begin = [], [], 0
    for d in range(docs):
        base = 0
        for e in range(docs):
            if e == d:
                continue
            ahead = holders[e] <= holders[d] if e < d else holders[e] < holders[d]
            base = base + jnp.where(ahead, sizes[e], 0)
        begins.append(begin)
        shifts.append(base - begin)
        begin = begin + sizes[d]
    slot = lax.broadcasted_iota(jnp.int32, (BLOCK, 1), 0) + sub_index * BLOCK
    lane = lax.broadcasted_iota(jnp.int32, (8, BLOCK), 1)
    ranks = []
    for j in range(subs):
        position = lane + (sub_index ^ j) * row_count + tp_index * BLOCK
        shift = jnp.full((8, BLOCK), 0, jnp.int32) + shifts[0]
        for d in range(1, docs):
            shift = jnp.where(position >= begins[d], shifts[d], shift)
        ranks.append((position + shift)[:1])
    for k in range(parts):
        target = slot + (tp_index ^ k) * (subs * BLOCK)
        total = None
        for j in range(subs):
            chosen = jnp.where(target == ranks[j], 1.0, 0.0).astype(BF16)
            term = jnp.dot(chosen, latents[j][...], preferred_element_type=F32)
            total = term if total is None else total + term
        picked[k][...] = total.astype(BF16)


def pick(place, lengths, owners, latents, parts, row_count):
    subs = len(latents)
    return pl.pallas_call(
        functools.partial(pick_kernel, parts, subs, row_count),
        out_shape=[jax.ShapeDtypeStruct((BLOCK, 2 * RANK), BF16)] * parts,
        in_specs=[SMEM] * 3 + [VMEM] * subs,
        out_specs=[VMEM] * parts,
        compiler_params=params(),
        name="pick",
    )(place, lengths, owners, *latents)


def rebuild_kernel(parts, *refs):
    arrived, (key_up, value_up, out) = refs[:parts], refs[parts:]
    total = arrived[0][...]
    for k in range(1, parts):
        total = total + arrived[k][...]
    width = key_up.shape[1]
    out[:, :width] = jnp.dot(total[:, :RANK], key_up[...], preferred_element_type=F32).astype(BF16)
    out[:, width:] = jnp.dot(total[:, RANK:], value_up[...], preferred_element_type=F32).astype(BF16)


def rebuild(arrived, key_up, value_up):
    parts = len(arrived)
    return pl.pallas_call(
        functools.partial(rebuild_kernel, parts),
        out_shape=jax.ShapeDtypeStruct((BLOCK, 2 * key_up.shape[1]), BF16),
        in_specs=[VMEM] * (parts + 2),
        out_specs=VMEM,
        compiler_params=params(),
        name="rebuild",
    )(*arrived, key_up, value_up)


def attend_kernel(parts, subs, heads, row_count, place, lengths, queries, *refs):
    pieces = refs[: parts * subs]
    out, keys, values, tops, sums, mix, key_top, sems = refs[parts * subs :]
    step = pl.program_id(0)
    tp_index, sub_index = place[0], place[1]
    docs = lengths.shape[0]
    ones = jnp.ones((8, HEAD_DIM), BF16)

    @pl.when(step == 0)
    def _():
        copies = []
        for j in range(subs):
            for k in range(parts):
                n = j * parts + k
                block = (sub_index ^ j) * parts + (tp_index ^ k) + 1
                first = pl.multiple_of(block * BLOCK, BLOCK)
                copies.append(
                    pltpu.make_async_copy(
                        pieces[n].at[:HEAD_DIM, :], values.at[:, pl.ds(first, BLOCK)], sems.at[n, 0]
                    )
                )
                for side in range(2):
                    copies.append(
                        pltpu.make_async_copy(
                            pieces[n].at[HEAD_DIM:, side * HEAD_DIM : (side + 1) * HEAD_DIM],
                            keys.at[pl.ds(first + side * HEAD_DIM, HEAD_DIM), :],
                            sems.at[n, side + 1],
                        )
                    )
        for copy in copies:
            copy.start()
        keys[:BLOCK, :] = jnp.zeros((BLOCK, HEAD_DIM), BF16)
        values[:, :BLOCK] = jnp.zeros((HEAD_DIM, BLOCK), BF16)
        for copy in copies:
            copy.wait()
        every = keys[...]
        squares = lax.dot_general(ones, every * every, NT, preferred_element_type=F32)
        key_top[0] = jnp.max(squares)

    first = sub_index * row_count + step * BLOCK
    position = first + lax.broadcasted_iota(jnp.int32, (1, BLOCK), 1)
    begin, low, high = 0, 0, 0
    begin_row = jnp.zeros((1, BLOCK), jnp.int32)
    for d in range(docs):
        begin_row = jnp.where(position >= begin, begin, begin_row)
        low = jnp.where(first >= begin, begin, low)
        high = jnp.where(first + BLOCK - 1 >= begin, begin, high)
        begin = begin + lengths[d]
    own = first // BLOCK
    low_block = low // BLOCK
    full_block = (high + BLOCK - 1) // BLOCK
    last = (own - low_block) // 2
    clear = jnp.minimum(jnp.maximum(own - 1 - full_block, 0) // 2, last)
    gain = math.log2(math.e) / math.sqrt(HEAD_DIM)
    key_iota = lax.broadcasted_iota(jnp.int32, (2 * BLOCK, BLOCK), 0) + (first - BLOCK)

    def query_of(head):
        return queries[:, head * HEAD_DIM : (head + 1) * HEAD_DIM]

    def absorb(pair, allowed, fresh, online):
        span = pl.ds(pl.multiple_of((own - 2 * pair) * BLOCK, BLOCK), 2 * BLOCK)

        def scores_of(head):
            return lax.dot_general(keys[span, :], query_of(head), NT, preferred_element_type=F32)

        ahead = [scores_of(head) for head in range(min(AHEAD, heads))]
        for head in range(heads):
            scores = ahead.pop(0) * gain
            if head + AHEAD < heads:
                ahead.append(scores_of(head + AHEAD))
            if allowed is not None:
                scores = jnp.where(allowed, scores, -1e30)
            if fresh:
                top = jnp.max(scores, axis=0, keepdims=True) + LIFT
                tops[head] = top
            elif online:
                before = tops[head]
                top = jnp.maximum(before, jnp.max(scores, axis=0, keepdims=True) + LIFT)
                tops[head] = top
            else:
                top = tops[head]
            weights = jnp.exp2(scores - top)
            total = jnp.sum(weights, axis=0, keepdims=True)
            result = jnp.dot(values[:, span], weights.astype(BF16), preferred_element_type=F32)
            if fresh:
                sums[head] = total
                mix[head] = result
            elif online:
                rescale = jnp.exp2(before - top)
                sums[head] = sums[head] * rescale + total
                mix[head] = mix[head] * rescale + result
            else:
                sums[head] += total
                mix[head] += result

    def sweep(online):
        @pl.loop(1, clear + 1)
        def _(pair):
            absorb(pair, None, False, online)

        @pl.loop(clear + 1, last + 1)
        def _(pair):
            absorb(pair, key_iota - 2 * pair * BLOCK >= begin_row, False, online)

    absorb(0, (key_iota <= position) & (key_iota >= begin_row), True, False)

    reach = jnp.full((1, BLOCK), -1e30, F32)
    for head in range(heads):
        query = query_of(head)
        squares = lax.dot_general(ones, query * query, NT, preferred_element_type=F32)[:1]
        most = jnp.sqrt(squares * key_top[0]) * (gain * 1.02)
        reach = jnp.maximum(reach, most - (tops[head] - LIFT))
    safe = jnp.max(reach) <= SPAN

    @pl.when(safe)
    def _():
        sweep(False)

    @pl.when(jnp.logical_not(safe))
    def _():
        sweep(True)

    for head in range(heads):
        result = mix[head] * (1.0 / sums[head])
        out[:, head * HEAD_DIM : (head + 1) * HEAD_DIM] = jnp.transpose(result).astype(BF16)


def attend(place, lengths, queries, pieces, parts, subs):
    row_count, width = queries.shape
    heads = width // HEAD_DIM
    row_spec = pl.BlockSpec((BLOCK, width), lambda i: (i, 0))
    total = parts * subs
    return pl.pallas_call(
        functools.partial(attend_kernel, parts, subs, heads, row_count),
        grid=(row_count // BLOCK,),
        out_shape=jax.ShapeDtypeStruct(queries.shape, BF16),
        in_specs=[SMEM, SMEM, row_spec] + [ANY] * total,
        out_specs=row_spec,
        scratch_shapes=[
            pltpu.VMEM(((total + 1) * BLOCK, HEAD_DIM), BF16),
            pltpu.VMEM((HEAD_DIM, (total + 1) * BLOCK), BF16),
            pltpu.VMEM((heads, 1, BLOCK), F32),
            pltpu.VMEM((heads, 1, BLOCK), F32),
            pltpu.VMEM((heads, HEAD_DIM, BLOCK), F32),
            pltpu.SMEM((1,), F32),
            pltpu.SemaphoreType.DMA((total, 3)),
        ],
        compiler_params=params(),
        name="attend",
    )(place, lengths, queries, *pieces)


def swap(value, axis, bits):
    count = lax.axis_size(axis)
    return lax.ppermute(value, axis, [(i, i ^ bits) for i in range(count)])


def per_device(hidden_states, queries, latent_down, key_up, value_up, doc_lengths, doc_owners):
    row_count = hidden_states.shape[0]
    parts = lax.axis_size("tp")
    subs = lax.axis_size("sub")
    place = jnp.stack([lax.axis_index("tp"), lax.axis_index("sub")]).astype(jnp.int32)
    value_rows = value_up.T
    far = project(place, hidden_states, latent_down, tuple(range(parts // 2, parts)))
    far = [swap(item, "tp", k) for k, item in enumerate(far, parts // 2)]
    near = project(place, hidden_states, latent_down, tuple(range(parts // 2)))
    near = [near[0]] + [swap(item, "tp", k) for k, item in enumerate(near[1:], 1)]
    coded = near + far
    latents, *pieces = expand(place, coded, key_up, value_rows)
    pieces = [pieces[0]] + [swap(pieces[k], "tp", k) for k in range(1, parts)]

    rows = [latents]
    blocks = [pieces]
    reach = subs // 2
    while reach >= 1:
        rows = rows + [swap(item, "sub", reach) for item in rows]
        blocks = blocks + [[swap(item, "sub", reach) for item in group] for group in blocks]
        reach //= 2
    order = [0]
    reach = subs // 2
    while reach >= 1:
        order = order + [item ^ reach for item in order]
        reach //= 2
    rows = [rows[order.index(j)] for j in range(subs)]
    blocks = [blocks[order.index(j)] for j in range(subs)]

    picked = pick(place, doc_lengths, doc_owners, rows, parts, row_count)
    picked = [picked[0]] + [swap(picked[k], "tp", k) for k in range(1, parts)]
    decode_cache = rebuild(picked, key_up, value_up)
    flat = [item for group in blocks for item in group]
    attention = attend(place, doc_lengths, queries, flat, parts, subs)
    return (attention, decode_cache)


def fits(mesh):
    return mesh.shape["tp"] == KV_HEADS and mesh.shape["sub"] & (mesh.shape["sub"] - 1) == 0


def choose(mesh):
    def run(hidden_states, queries, *rest):
        rows = hidden_states.shape[0]
        direct = fits(mesh) and rows == BLOCK * mesh.shape["tp"]
        return (per_device if direct else per_device_general)(hidden_states, queries, *rest)

    return run


def solution(mesh):
    return jax.shard_map(
        choose(mesh),
        mesh=mesh,
        in_specs=(
            P(("groups", "sub"), "tp"),
            P(("groups", "sub"), "tp"),
            P("tp", None),
            P(),
            P(),
            P("groups"),
            P("groups"),
        ),
        out_specs=(P(("groups", "sub"), "tp"), P(("groups", "tp", "sub"), None)),
        check_vma=False,
    )
```

```python
import functools
import math

import jax
import jax.numpy as jnp
from jax import lax
from jax.experimental import pallas as pl
from jax.experimental.pallas import tpu as pltpu
from jax.sharding import PartitionSpec as P

HEAD_DIM = 128
Q_HEADS = 32
KV_HEADS = 4
RANK = 256
BLOCK = 256
SLICES = 4
AHEAD = 3
SCALE_ROWS = 16
CODE_TOP = 32000.0
LIFT = 24.0
SPAN = 100.0
GAIN = math.log2(math.e) / math.sqrt(HEAD_DIM)
VMEM_LIMIT = 48 * 1024 * 1024
F32 = jnp.float32
BF16 = jnp.bfloat16
NT = (((1,), (1,)), ((), ()))


def doc_tables(doc_lengths):
    doc_ends = jnp.cumsum(doc_lengths)
    doc_starts = doc_ends - doc_lengths
    return (doc_starts, doc_ends)


def doc_of(positions, doc_ends):
    return jnp.sum((positions[:, None] >= doc_ends[None, :]).astype(jnp.int32), axis=1)


def lookup(doc_index, doc_table):
    doc_numbers = jnp.arange(doc_table.shape[0], dtype=jnp.int32)
    picked = jnp.where(doc_index[:, None] == doc_numbers[None, :], doc_table[None, :], 0)
    return jnp.sum(picked, axis=1)


def owner_base(doc_lengths, doc_owners):
    doc_numbers = jnp.arange(doc_lengths.shape[0], dtype=jnp.int32)
    before = (doc_owners[None, :] < doc_owners[:, None]) | (
        doc_owners[None, :] == doc_owners[:, None]
    ) & (doc_numbers[None, :] < doc_numbers[:, None])
    return jnp.sum(jnp.where(before, doc_lengths[None, :], 0), axis=1)


def per_device_general(hidden_states, queries, latent_down, key_up, value_up, doc_lengths, doc_owners):
    row_count = hidden_states.shape[0]
    tp_count = lax.axis_size("tp")
    sub_count = lax.axis_size("sub")
    tp_index = lax.axis_index("tp")
    sub_index = lax.axis_index("sub")
    partial_sums = jnp.dot(hidden_states, latent_down, preferred_element_type=F32)
    latents = lax.psum(partial_sums, "tp").astype(BF16)
    local_heads = queries.shape[1] // HEAD_DIM
    per_group = Q_HEADS // KV_HEADS
    grouped = min(local_heads, per_group)
    kv_count = local_heads // grouped
    kv_first = tp_index * local_heads // per_group
    key_cols = lax.dynamic_slice_in_dim(key_up, kv_first * HEAD_DIM, kv_count * HEAD_DIM, 1)
    value_cols = lax.dynamic_slice_in_dim(value_up, kv_first * HEAD_DIM, kv_count * HEAD_DIM, 1)
    own_keys = jnp.dot(latents[:, :RANK], key_cols, preferred_element_type=F32).astype(BF16)
    own_values = jnp.dot(latents[:, RANK:], value_cols, preferred_element_type=F32).astype(BF16)
    doc_starts, doc_ends = doc_tables(doc_lengths)
    query_pos = sub_index * row_count + jnp.arange(row_count, dtype=jnp.int32)
    query_doc = doc_of(query_pos, doc_ends)
    query_grid = queries.reshape(row_count, kv_count, grouped, HEAD_DIM)
    inv_root = 1.0 / math.sqrt(HEAD_DIM)
    carried = (
        jnp.full((kv_count, grouped, row_count), -1e30, F32),
        jnp.zeros((kv_count, grouped, row_count), F32),
        jnp.zeros((kv_count, grouped, row_count, HEAD_DIM), F32),
    )
    key_piece = lax.all_gather(own_keys, "sub", axis=0, tiled=True)
    value_piece = lax.all_gather(own_values, "sub", axis=0, tiled=True)
    piece_len = key_piece.shape[0]
    block_len = math.gcd(piece_len, 1024)
    block_total = piece_len // block_len
    key_blocks = key_piece.reshape(block_total, block_len, kv_count, HEAD_DIM)
    value_blocks = value_piece.reshape(block_total, block_len, kv_count, HEAD_DIM)
    first_positions = block_len * jnp.arange(block_total, dtype=jnp.int32)

    def absorb(state, block_item):
        running_top, totals, weighted = state
        key_block, value_block, first_pos = block_item
        key_pos = first_pos + jnp.arange(block_len, dtype=jnp.int32)
        key_doc = doc_of(key_pos, doc_ends)
        allowed = (key_pos[None, :] <= query_pos[:, None]) & (
            key_doc[None, :] == query_doc[:, None]
        )
        scores = (
            jnp.einsum("qkgd,jkd->kgqj", query_grid, key_block, preferred_element_type=F32)
            * inv_root
        )
        scores = jnp.where(allowed, scores, -1e30)
        new_top = jnp.maximum(running_top, jnp.max(scores, axis=-1))
        weights = jnp.where(allowed, jnp.exp(scores - new_top[..., None]), 0.0)
        rescale = jnp.exp(running_top - new_top)
        totals = totals * rescale + jnp.sum(weights, axis=-1)
        weighted = weighted * rescale[..., None] + jnp.einsum(
            "kgqj,jkd->kgqd", weights.astype(BF16), value_block, preferred_element_type=F32
        )
        return ((new_top, totals, weighted), None)

    carried, _ = lax.scan(absorb, carried, (key_blocks, value_blocks, first_positions))
    running_top, totals, weighted = carried
    result = weighted / totals[..., None]
    attention = (
        jnp.transpose(result, (2, 0, 1, 3))
        .reshape(row_count, local_heads * HEAD_DIM)
        .astype(BF16)
    )
    base_table = owner_base(doc_lengths, doc_owners)
    sorted_rank = lookup(query_doc, base_table - doc_starts) + query_pos
    slot_count = row_count // tp_count
    column_span = slot_count * sub_count
    targets = tp_index * column_span + jnp.arange(column_span, dtype=jnp.int32)
    selector = (targets[:, None] == sorted_rank[None, :]).astype(BF16)
    placed = jnp.dot(selector, latents, preferred_element_type=F32)
    arrived = lax.psum_scatter(placed.astype(BF16), "sub", scatter_dimension=0, tiled=True)
    decode_keys = jnp.dot(arrived[:, :RANK], key_up, preferred_element_type=F32).astype(BF16)
    decode_values = jnp.dot(arrived[:, RANK:], value_up, preferred_element_type=F32).astype(BF16)
    decode_cache = jnp.concatenate([decode_keys, decode_values], axis=1)
    return (attention, decode_cache)


SMEM = pl.BlockSpec(memory_space=pltpu.SMEM)
VMEM = pl.BlockSpec(memory_space=pltpu.VMEM)
ANY = pl.BlockSpec(memory_space=pl.ANY)


def cost(micros):
    return pl.CostEstimate(
        flops=int(micros * 1.1e9), bytes_accessed=int(micros * 1e6), transcendentals=0
    )


def params():
    return pltpu.CompilerParams(vmem_limit_bytes=VMEM_LIMIT)


def project_kernel(chunks, place, hidden, down, *refs):
    count = len(chunks)
    coded = refs[:count]
    rows_buf, down_buf, row_sem, down_sem = refs[count:]
    tp_index = place[0]
    depth = down.shape[0] // SLICES
    down_copies, row_copies = [], []
    for c in range(SLICES):
        span = pl.ds(c * depth, depth)
        down_copies.append(
            pltpu.make_async_copy(down.at[span, :], down_buf.at[span, :], down_sem.at[c])
        )
        down_copies[c].start()
        for k in range(count):
            first = pl.multiple_of((tp_index ^ chunks[k]) * BLOCK, BLOCK)
            copy = pltpu.make_async_copy(
                hidden.at[pl.ds(first, BLOCK), span],
                rows_buf.at[k, :, span],
                row_sem.at[k * SLICES + c],
            )
            copy.start()
            row_copies.append(copy)
    sums = [None] * count
    for c in range(SLICES):
        span = slice(c * depth, (c + 1) * depth)
        down_copies[c].wait()
        for k in range(count):
            row_copies[c * count + k].wait()
            term = jnp.dot(rows_buf[k, :, span], down_buf[span, :], preferred_element_type=F32)
            sums[k] = term if c == 0 else sums[k] + term
    lane = lax.broadcasted_iota(jnp.int32, (BLOCK, 128), 1)
    for k in range(count):
        powers = []
        for half in range(2):
            piece = sums[k][:, half * RANK : (half + 1) * RANK]
            top = jnp.max(jnp.abs(piece), axis=1, keepdims=True)
            power = jnp.ceil(jnp.log2(jnp.maximum(top, 1e-30)) + 1e-3)
            code = jnp.round(piece * (CODE_TOP * jnp.exp2(-power))).astype(jnp.int32)
            coded[k][:BLOCK, half * RANK : (half + 1) * RANK] = code.astype(jnp.int16)
            powers.append(power)
        table = jnp.transpose(jnp.where(lane == 0, powers[0], powers[1]))[:SCALE_ROWS]
        table = table.astype(jnp.int32).astype(jnp.int16)
        coded[k][BLOCK:, :RANK] = table
        coded[k][BLOCK:, RANK:] = table


def project(place, hidden, down, chunks):
    width = down.shape[1]
    count = len(chunks)
    return pl.pallas_call(
        functools.partial(project_kernel, chunks),
        out_shape=[jax.ShapeDtypeStruct((BLOCK + SCALE_ROWS, width), jnp.int16)] * count,
        in_specs=[SMEM, ANY, ANY],
        out_specs=[VMEM] * count,
        scratch_shapes=[
            pltpu.VMEM((count, BLOCK, hidden.shape[1]), BF16),
            pltpu.VMEM(down.shape, BF16),
            pltpu.SemaphoreType.DMA((count * SLICES,)),
            pltpu.SemaphoreType.DMA((SLICES,)),
        ],
        compiler_params=pltpu.CompilerParams(vmem_limit_bytes=60 * 1024 * 1024),
        name="project",
    )(place, hidden, down)


def expand_kernel(parts, place, *refs):
    coded = refs[:parts]
    key_up, value_up = refs[parts : parts + 2]
    pieces = refs[parts + 2 :]
    tp_index = place[0]
    halves = []
    columns = []
    for k in range(parts):
        powers = coded[k][BLOCK:, :RANK].astype(jnp.int32).astype(F32)
        columns.append(jnp.transpose(jnp.exp2(powers) * (1.0 / CODE_TOP)))
    for half in range(2):
        total = None
        for k in range(parts):
            code = coded[k][:BLOCK, half * RANK : (half + 1) * RANK].astype(jnp.int32).astype(F32)
            term = code * columns[k][:, half : half + 1]
            total = term if total is None else total + term
        halves.append(total.astype(BF16))
        pieces[0][:, half * RANK : (half + 1) * RANK] = halves[half]
    for k in range(parts):
        lead = pieces[k].shape[1] - BLOCK
        head = tp_index ^ k
        cols = pl.ds(pl.multiple_of(head * HEAD_DIM, HEAD_DIM), HEAD_DIM)
        keys = jnp.dot(halves[0], key_up[:, cols], preferred_element_type=F32).astype(BF16)
        values = lax.dot_general(
            value_up[cols, :], halves[1], NT, preferred_element_type=F32
        ).astype(BF16)
        pieces[k][:HEAD_DIM, lead:] = values
        pieces[k][HEAD_DIM:, lead : lead + HEAD_DIM] = keys[:HEAD_DIM]
        pieces[k][HEAD_DIM:, lead + HEAD_DIM :] = keys[HEAD_DIM:]


def expand(place, coded, key_up, value_rows):
    parts = len(coded)
    return pl.pallas_call(
        functools.partial(expand_kernel, parts),
        out_shape=[jax.ShapeDtypeStruct((BLOCK, 2 * RANK + BLOCK), BF16)]
        + [jax.ShapeDtypeStruct((BLOCK, BLOCK), BF16)] * (parts - 1),
        in_specs=[SMEM] + [VMEM] * (parts + 2),
        out_specs=[VMEM] * parts,
        compiler_params=params(),
        name="expand",
    )(place, *coded, key_up, value_rows)


def pick_kernel(planes, subs, row_count, place, lengths, owners, *refs):
    latents, picked = refs[:subs], refs[subs:]
    tp_index, sub_index = place[0], place[1]
    docs = lengths.shape[0]
    sizes = [lengths[d] for d in range(docs)]
    holders = [owners[d] for d in range(docs)]
    shifts, begins, begin = [], [], 0
    for d in range(docs):
        base = 0
        for e in range(docs):
            if e == d:
                continue
            ahead = holders[e] <= holders[d] if e < d else holders[e] < holders[d]
            base = base + jnp.where(ahead, sizes[e], 0)
        begins.append(begin)
        shifts.append(base - begin)
        begin = begin + sizes[d]
    slot = lax.broadcasted_iota(jnp.int32, (BLOCK, 1), 0) + sub_index * BLOCK
    lane = lax.broadcasted_iota(jnp.int32, (8, BLOCK), 1)
    ranks = []
    for j in range(subs):
        position = lane + (sub_index ^ j) * row_count + tp_index * BLOCK
        shift = jnp.full((8, BLOCK), 0, jnp.int32) + shifts[0]
        for d in range(1, docs):
            shift = jnp.where(position >= begins[d], shifts[d], shift)
        ranks.append((position + shift)[:1])
    for out, group in zip(picked, planes):
        for n, k in enumerate(group):
            target = slot + (tp_index ^ k) * (subs * BLOCK)
            total = None
            for j in range(subs):
                chosen = jnp.where(target == ranks[j], 1.0, 0.0).astype(BF16)
                term = jnp.dot(chosen, latents[j][:, : 2 * RANK], preferred_element_type=F32)
                total = term if total is None else total + term
            out[n * BLOCK : (n + 1) * BLOCK, :] = total.astype(BF16)


def pick(place, lengths, owners, latents, planes, row_count):
    subs = len(latents)
    return pl.pallas_call(
        functools.partial(pick_kernel, planes, subs, row_count),
        out_shape=[
            jax.ShapeDtypeStruct((len(group) * BLOCK, 2 * RANK), BF16) for group in planes
        ],
        in_specs=[SMEM] * 3 + [VMEM] * subs,
        out_specs=[VMEM] * len(planes),
        compiler_params=params(),
        name="pick",
    )(place, lengths, owners, *latents)


def rebuild_kernel(parts, *refs):
    arrived, (key_up, value_up, out) = refs[:parts], refs[parts:]
    total = arrived[0][...]
    for k in range(1, parts):
        total = total + arrived[k][:BLOCK, :]
    width = key_up.shape[1]
    out[:, :width] = jnp.dot(total[:, :RANK], key_up[...], preferred_element_type=F32).astype(BF16)
    out[:, width:] = jnp.dot(total[:, RANK:], value_up[...], preferred_element_type=F32).astype(BF16)


def rebuild(arrived, key_up, value_up):
    parts = len(arrived)
    return pl.pallas_call(
        functools.partial(rebuild_kernel, parts),
        out_shape=jax.ShapeDtypeStruct((BLOCK, 2 * key_up.shape[1]), BF16),
        in_specs=[VMEM] * (parts + 2),
        out_specs=VMEM,
        compiler_params=params(),
        name="rebuild",
    )(*arrived, key_up, value_up)


def load_pieces(pieces, blocks, keys, values, sems):
    copies = []
    for n, block in enumerate(blocks):
        first = pl.multiple_of(block * BLOCK, BLOCK)
        copies.append(
            pltpu.make_async_copy(
                pieces[n].at[:HEAD_DIM, :], values.at[:, pl.ds(first, BLOCK)], sems.at[n, 0]
            )
        )
        for side in range(2):
            copies.append(
                pltpu.make_async_copy(
                    pieces[n].at[HEAD_DIM:, side * HEAD_DIM : (side + 1) * HEAD_DIM],
                    keys.at[pl.ds(first + side * HEAD_DIM, HEAD_DIM), :],
                    sems.at[n, side + 1],
                )
            )
    for copy in copies:
        copy.start()
    return copies


def split(refs):
    pieces = []
    for ref in refs:
        lead = ref.shape[1] - BLOCK
        for k in range(ref.shape[0] // BLOCK):
            pieces.append(ref.at[k * BLOCK : (k + 1) * BLOCK, lead : lead + BLOCK])
    return pieces


def clear_blocks(keys, values, first):
    keys[pl.ds(first, BLOCK), :] = jnp.zeros((BLOCK, HEAD_DIM), BF16)
    values[:, pl.ds(first, BLOCK)] = jnp.zeros((HEAD_DIM, BLOCK), BF16)


def longest(keys):
    every = keys[...]
    ones = jnp.ones((8, HEAD_DIM), BF16)
    return jnp.max(lax.dot_general(ones, every * every, NT, preferred_element_type=F32))


def row_bounds(lengths, first):
    position = first + lax.broadcasted_iota(jnp.int32, (1, BLOCK), 1)
    begin, low, high = 0, 0, 0
    begin_row = jnp.zeros((1, BLOCK), jnp.int32)
    for d in range(lengths.shape[0]):
        begin_row = jnp.where(position >= begin, begin, begin_row)
        low = jnp.where(first >= begin, begin, low)
        high = jnp.where(first + BLOCK - 1 >= begin, begin, high)
        begin = begin + lengths[d]
    return position, begin_row, low, high


def absorb(span, keys, values, queries, state, mask, fresh, online):
    tops, sums, mix = state
    heads = queries.shape[1] // HEAD_DIM

    def scores_of(head):
        query = queries[:, head * HEAD_DIM : (head + 1) * HEAD_DIM]
        return lax.dot_general(keys[span, :], query, NT, preferred_element_type=F32)

    ahead = [scores_of(head) for head in range(min(AHEAD, heads))]
    for head in range(heads):
        scores = ahead.pop(0) * GAIN
        if head + AHEAD < heads:
            ahead.append(scores_of(head + AHEAD))
        if mask is not None:
            scores = scores + mask[: scores.shape[0], :]
        row = slice(head, head + 1)
        if fresh:
            top = jnp.max(scores, axis=0, keepdims=True) + LIFT
            tops[row, :] = top
        else:
            before = tops[row, :]
            top = before
            if online:
                top = jnp.maximum(before, jnp.max(scores, axis=0, keepdims=True) + LIFT)
                tops[row, :] = top
        weights = jnp.exp2(scores - top)
        total = jnp.sum(weights, axis=0, keepdims=True)
        result = jnp.dot(values[:, span], weights.astype(BF16), preferred_element_type=F32)
        if fresh:
            sums[row, :] = total
            mix[head] = result
        elif online:
            rescale = jnp.exp2(before - top)
            sums[row, :] = sums[row, :] * rescale + total
            mix[head] = mix[head] * rescale + result
        else:
            sums[row, :] += total
            mix[head] += result


def set_mask(mask, allowed):
    mask[: allowed.shape[0], :] = jnp.where(allowed, 0.0, -1e30)


def bounded(queries, tops, key_top):
    every = queries[...]
    heads = tops.shape[0]
    lane = lax.broadcasted_iota(jnp.int32, (heads, every.shape[1]), 1) // HEAD_DIM
    of_head = lane == lax.broadcasted_iota(jnp.int32, lane.shape, 0)
    of_head = jnp.where(of_head, 1.0, 0.0).astype(BF16)
    squares = lax.dot_general(of_head, every * every, NT, preferred_element_type=F32)
    reach = jnp.sqrt(squares * key_top) * (GAIN * 1.02) - (tops[...] - LIFT)
    return jnp.max(reach) <= SPAN


def attend_near_kernel(parts, row_count, place, lengths, queries, *refs):
    pieces = refs[:parts]
    tops, sums, mix, packed, keys, values, mask, key_top, sems, pack_sems = refs[parts:]
    tops, sums, mix = state = (tops.at[0], sums.at[0], mix.at[0])
    step = pl.program_id(0)
    tp_index, sub_index = place[0], place[1]
    packs = [
        pltpu.make_async_copy(
            pieces[k], packed.at[(k - 1) * BLOCK : k * BLOCK, :], pack_sems.at[k]
        )
        for k in range(1, parts)
    ]
    pieces = split(pieces)

    @pl.when(step == 0)
    def _():
        copies = load_pieces(
            pieces, [(tp_index ^ k) + 1 for k in range(parts)], keys, values, sems
        )
        for copy in packs:
            copy.start()
        clear_blocks(keys, values, 0)
        for copy in copies:
            copy.wait()
        key_top[0] = longest(keys)

    start = sub_index * row_count
    first = start + step * BLOCK
    position, begin_row, low, high = row_bounds(lengths, first)
    begin_row = jnp.maximum(begin_row, start)
    low_block = jnp.maximum(low - start, 0) // BLOCK
    full_block = (jnp.maximum(high - start, 0) + BLOCK - 1) // BLOCK
    last = (step - low_block) // 2
    clear = jnp.minimum(jnp.maximum(step - 1 - full_block, 0) // 2, last)
    key_iota = lax.broadcasted_iota(jnp.int32, (2 * BLOCK, BLOCK), 0) + (first - BLOCK)

    def take(pair, masked, fresh, online):
        span = pl.ds(pl.multiple_of((step - 2 * pair) * BLOCK, BLOCK), 2 * BLOCK)
        absorb(span, keys, values, queries, state, mask if masked else None, fresh, online)

    set_mask(mask, (key_iota <= position) & (key_iota >= begin_row))
    take(0, True, True, False)
    safe = bounded(queries, tops, key_top[0])
    for online in (False, True):

        @pl.when(jnp.logical_not(safe) if online else safe)
        def _():
            @pl.loop(1, clear + 1)
            def _(pair):
                take(pair, False, False, online)

            @pl.loop(clear + 1, last + 1)
            def _(pair):
                set_mask(mask, key_iota - 2 * pair * BLOCK >= begin_row)
                take(pair, True, False, online)

    @pl.when(step == pl.num_programs(0) - 1)
    def _():
        for copy in packs:
            copy.wait()


def attend_far_kernel(parts, subs, groups, row_count, place, lengths, queries, *refs):
    tops_in, sums_in, mix_in = refs[:3]
    held, refs = refs[3 : 3 + groups], refs[3 + groups :]
    out, keys, values, mask, tops, sums, mix, key_top, sems = refs
    pieces = split(held)
    heads = tops.shape[0]
    step = pl.program_id(0)
    tp_index, sub_index = place[0], place[1]

    @pl.when(step == 0)
    def _():
        blocks = [
            (sub_index ^ j) * parts + (tp_index ^ k) for j in range(1, subs) for k in range(parts)
        ]
        copies = load_pieces(pieces, blocks, keys, values, sems)
        for k in range(parts):
            clear_blocks(keys, values, pl.multiple_of((sub_index * parts + k) * BLOCK, BLOCK))
        for copy in copies:
            copy.wait()
        key_top[0] = longest(keys)

    first = sub_index * row_count + step * BLOCK
    position, begin_row, low, high = row_bounds(lengths, first)
    end_block = sub_index * parts
    low_block = low // BLOCK
    full_block = (high + BLOCK - 1) // BLOCK
    count = jnp.maximum(end_block - low_block, 0)
    last = count // 2
    clear = jnp.minimum(jnp.maximum(end_block - full_block, 0) // 2, last)

    @pl.when(count == 0)
    def _():
        finish(mix_in.at[0], sums_in.at[0], out)

    @pl.when(count > 0)
    def _():
        tops[...] = tops_in[0]
        sums[...] = sums_in[0]
        mix[...] = mix_in[0]

        def take(block, blocks, masked, online):
            begin = block * BLOCK
            span = pl.ds(pl.multiple_of(begin, BLOCK), blocks * BLOCK)
            if masked:
                key_iota = lax.broadcasted_iota(jnp.int32, (blocks * BLOCK, BLOCK), 0)
                set_mask(mask, key_iota + begin >= begin_row)
            state = (tops, sums, mix)
            absorb(span, keys, values, queries, state, mask if masked else None, False, online)

        safe = bounded(queries, tops, key_top[0])
        for online in (False, True):

            @pl.when(jnp.logical_not(safe) if online else safe)
            def _():
                @pl.loop(0, clear)
                def _(pair):
                    take(end_block - 2 - 2 * pair, 2, False, online)

                @pl.loop(clear, last)
                def _(pair):
                    take(end_block - 2 - 2 * pair, 2, True, online)

                @pl.when(count > 2 * last)
                def _():
                    take(low_block, 1, True, online)

        finish(mix, sums, out)


def finish(mix, sums, out):
    for head in range(mix.shape[0]):
        result = mix[head] * (1.0 / sums[head : head + 1, :])
        out[:, head * HEAD_DIM : (head + 1) * HEAD_DIM] = jnp.transpose(result).astype(BF16)


def attend_specs(queries):
    row_count, width = queries.shape
    heads, steps = width // HEAD_DIM, row_count // BLOCK
    shapes = [(heads, BLOCK), (heads, BLOCK), (heads, HEAD_DIM, BLOCK)]
    row_spec = pl.BlockSpec((BLOCK, width), lambda i: (i, 0))
    state_specs = [
        pl.BlockSpec((1, *shape), lambda i, rank=len(shape): (i,) + (0,) * rank)
        for shape in shapes
    ]
    state_shapes = [jax.ShapeDtypeStruct((steps, *shape), F32) for shape in shapes]
    scratch = [pltpu.VMEM(shape, F32) for shape in shapes]
    return (steps,), row_spec, state_specs, state_shapes, scratch


def store_shapes(blocks, pieces):
    return [
        pltpu.VMEM((blocks * BLOCK, HEAD_DIM), BF16),
        pltpu.VMEM((HEAD_DIM, blocks * BLOCK), BF16),
        pltpu.VMEM((2 * BLOCK, BLOCK), F32),
    ], [pltpu.SMEM((1,), F32), pltpu.SemaphoreType.DMA((pieces, 3))]


def attend_near(place, lengths, queries, pieces):
    parts = len(pieces)
    grid, row_spec, state_specs, state_shapes, _ = attend_specs(queries)
    stores, rest = store_shapes(parts + 1, parts)
    return pl.pallas_call(
        functools.partial(attend_near_kernel, parts, queries.shape[0]),
        grid=grid,
        out_shape=state_shapes + [jax.ShapeDtypeStruct(((parts - 1) * BLOCK, BLOCK), BF16)],
        in_specs=[SMEM, SMEM, row_spec] + [ANY] * parts,
        out_specs=state_specs + [ANY],
        scratch_shapes=stores + rest + [pltpu.SemaphoreType.DMA((parts,))],
        compiler_params=params(),
        cost_estimate=cost(12),
        name="attend_near",
    )(place, lengths, queries, *pieces)


def attend_far(place, lengths, queries, state, pieces, parts, subs):
    grid, row_spec, state_specs, _, scratch = attend_specs(queries)
    stores, rest = store_shapes(parts * subs, parts * (subs - 1))
    return pl.pallas_call(
        functools.partial(attend_far_kernel, parts, subs, len(pieces), queries.shape[0]),
        grid=grid,
        out_shape=jax.ShapeDtypeStruct(queries.shape, BF16),
        in_specs=[SMEM, SMEM, row_spec] + state_specs + [ANY] * len(pieces),
        out_specs=row_spec,
        scratch_shapes=stores + scratch + rest,
        compiler_params=params(),
        cost_estimate=cost(20),
        name="attend_far",
    )(place, lengths, queries, *state, *pieces)


def swap(value, axis, bits):
    count = lax.axis_size(axis)
    return lax.ppermute(value, axis, [(i, i ^ bits) for i in range(count)])


def per_device(hidden_states, queries, latent_down, key_up, value_up, doc_lengths, doc_owners):
    row_count = hidden_states.shape[0]
    parts = lax.axis_size("tp")
    subs = lax.axis_size("sub")
    place = jnp.stack([lax.axis_index("tp"), lax.axis_index("sub")]).astype(jnp.int32)
    value_rows = value_up.T
    far = [
        project(place, hidden_states, latent_down, (k,))[0] for k in range(parts // 2, parts)
    ]
    far = [swap(item, "tp", k) for k, item in enumerate(far, parts // 2)]
    near = project(place, hidden_states, latent_down, tuple(range(parts // 2)))
    near = [near[0]] + [swap(item, "tp", k) for k, item in enumerate(near[1:], 1)]
    coded = near + far
    own, *pieces = expand(place, coded, key_up, value_rows)
    arrivals = [swap(item, "tp", k) for k, item in enumerate(pieces, 1)]

    half = subs // 2
    order, rows, reach = [0], [own], half
    while reach >= 1:
        order = order + [item ^ reach for item in order]
        far_rows = [swap(item, "sub", reach) for item in rows]
        far_rows, arrivals = lax.optimization_barrier((far_rows, arrivals))
        rows = rows + list(far_rows)
        reach //= 2
    rows = [rows[order.index(j)] for j in range(subs)]
    planes = ((1, 3), (0,), (2,))
    leaving, kept, across = pick(place, doc_lengths, doc_owners, rows, planes, row_count)
    passed = swap(leaving, "tp", 1)

    gate, kept = lax.optimization_barrier((place, kept))
    *state, packed = attend_near(gate, doc_lengths, queries, [own, *arrivals])
    crossed = [swap(item, "sub", half) for item in arrivals]
    crossed, state, packed, passed = lax.optimization_barrier((crossed, state, packed, passed))

    blocks, reach = [[packed], list(crossed)], half // 2
    while reach >= 1:
        blocks = blocks + [[swap(item, "sub", reach) for item in group] for group in blocks]
        reach //= 2
    blocks = [blocks[order.index(j)] for j in range(subs)]

    second = swap(across + passed[BLOCK:], "tp", 2)
    flat = []
    for j in range(1, subs):
        flat += [rows[j], *blocks[j]]
    attention = attend_far(place, doc_lengths, queries, state, flat, parts, subs)
    kept, attention = lax.optimization_barrier((kept, attention))
    decode_cache = rebuild([kept, passed, second], key_up, value_up)
    return (attention, decode_cache)


def fits(mesh):
    return mesh.shape["tp"] == KV_HEADS and mesh.shape["sub"] & (mesh.shape["sub"] - 1) == 0


def choose(mesh):
    def run(hidden_states, queries, *rest):
        rows = hidden_states.shape[0]
        direct = fits(mesh) and rows == BLOCK * mesh.shape["tp"]
        return (per_device if direct else per_device_general)(hidden_states, queries, *rest)

    return run


def solution(mesh):
    return jax.shard_map(
        choose(mesh),
        mesh=mesh,
        in_specs=(
            P(("groups", "sub"), "tp"),
            P(("groups", "sub"), "tp"),
            P("tp", None),
            P(),
            P(),
            P("groups"),
            P("groups"),
        ),
        out_specs=(P(("groups", "sub"), "tp"), P(("groups", "tp", "sub"), None)),
        check_vma=False,
    )
```

```python
import functools
import math

import jax
import jax.numpy as jnp
from jax import lax
from jax.experimental import pallas as pl
from jax.experimental.pallas import tpu as pltpu
from jax.sharding import PartitionSpec as P

HEAD_DIM = 128
Q_HEADS = 32
KV_HEADS = 4
RANK = 256
BLOCK = 256
SLICES = 4
AHEAD = 3
SCALE_ROWS = 16
CODE_TOP = 32000.0
LIFT = 24.0
SPAN = 100.0
GAIN = math.log2(math.e) / math.sqrt(HEAD_DIM)
VMEM_LIMIT = 24 * 1024 * 1024
F32 = jnp.float32
BF16 = jnp.bfloat16
NT = (((1,), (1,)), ((), ()))


def doc_tables(doc_lengths):
    doc_ends = jnp.cumsum(doc_lengths)
    doc_starts = doc_ends - doc_lengths
    return (doc_starts, doc_ends)


def doc_of(positions, doc_ends):
    return jnp.sum((positions[:, None] >= doc_ends[None, :]).astype(jnp.int32), axis=1)


def lookup(doc_index, doc_table):
    doc_numbers = jnp.arange(doc_table.shape[0], dtype=jnp.int32)
    picked = jnp.where(doc_index[:, None] == doc_numbers[None, :], doc_table[None, :], 0)
    return jnp.sum(picked, axis=1)


def owner_base(doc_lengths, doc_owners):
    doc_numbers = jnp.arange(doc_lengths.shape[0], dtype=jnp.int32)
    before = (doc_owners[None, :] < doc_owners[:, None]) | (
        doc_owners[None, :] == doc_owners[:, None]
    ) & (doc_numbers[None, :] < doc_numbers[:, None])
    return jnp.sum(jnp.where(before, doc_lengths[None, :], 0), axis=1)


def per_device_general(hidden_states, queries, latent_down, key_up, value_up, doc_lengths, doc_owners):
    row_count = hidden_states.shape[0]
    tp_count = lax.axis_size("tp")
    sub_count = lax.axis_size("sub")
    tp_index = lax.axis_index("tp")
    sub_index = lax.axis_index("sub")
    partial_sums = jnp.dot(hidden_states, latent_down, preferred_element_type=F32)
    latents = lax.psum(partial_sums, "tp").astype(BF16)
    local_heads = queries.shape[1] // HEAD_DIM
    per_group = Q_HEADS // KV_HEADS
    grouped = min(local_heads, per_group)
    kv_count = local_heads // grouped
    kv_first = tp_index * local_heads // per_group
    key_cols = lax.dynamic_slice_in_dim(key_up, kv_first * HEAD_DIM, kv_count * HEAD_DIM, 1)
    value_cols = lax.dynamic_slice_in_dim(value_up, kv_first * HEAD_DIM, kv_count * HEAD_DIM, 1)
    own_keys = jnp.dot(latents[:, :RANK], key_cols, preferred_element_type=F32).astype(BF16)
    own_values = jnp.dot(latents[:, RANK:], value_cols, preferred_element_type=F32).astype(BF16)
    doc_starts, doc_ends = doc_tables(doc_lengths)
    query_pos = sub_index * row_count + jnp.arange(row_count, dtype=jnp.int32)
    query_doc = doc_of(query_pos, doc_ends)
    query_grid = queries.reshape(row_count, kv_count, grouped, HEAD_DIM)
    inv_root = 1.0 / math.sqrt(HEAD_DIM)
    carried = (
        jnp.full((kv_count, grouped, row_count), -1e30, F32),
        jnp.zeros((kv_count, grouped, row_count), F32),
        jnp.zeros((kv_count, grouped, row_count, HEAD_DIM), F32),
    )
    key_piece = lax.all_gather(own_keys, "sub", axis=0, tiled=True)
    value_piece = lax.all_gather(own_values, "sub", axis=0, tiled=True)
    piece_len = key_piece.shape[0]
    block_len = math.gcd(piece_len, 1024)
    block_total = piece_len // block_len
    key_blocks = key_piece.reshape(block_total, block_len, kv_count, HEAD_DIM)
    value_blocks = value_piece.reshape(block_total, block_len, kv_count, HEAD_DIM)
    first_positions = block_len * jnp.arange(block_total, dtype=jnp.int32)

    def absorb(state, block_item):
        running_top, totals, weighted = state
        key_block, value_block, first_pos = block_item
        key_pos = first_pos + jnp.arange(block_len, dtype=jnp.int32)
        key_doc = doc_of(key_pos, doc_ends)
        allowed = (key_pos[None, :] <= query_pos[:, None]) & (
            key_doc[None, :] == query_doc[:, None]
        )
        scores = (
            jnp.einsum("qkgd,jkd->kgqj", query_grid, key_block, preferred_element_type=F32)
            * inv_root
        )
        scores = jnp.where(allowed, scores, -1e30)
        new_top = jnp.maximum(running_top, jnp.max(scores, axis=-1))
        weights = jnp.where(allowed, jnp.exp(scores - new_top[..., None]), 0.0)
        rescale = jnp.exp(running_top - new_top)
        totals = totals * rescale + jnp.sum(weights, axis=-1)
        weighted = weighted * rescale[..., None] + jnp.einsum(
            "kgqj,jkd->kgqd", weights.astype(BF16), value_block, preferred_element_type=F32
        )
        return ((new_top, totals, weighted), None)

    carried, _ = lax.scan(absorb, carried, (key_blocks, value_blocks, first_positions))
    running_top, totals, weighted = carried
    result = weighted / totals[..., None]
    attention = (
        jnp.transpose(result, (2, 0, 1, 3))
        .reshape(row_count, local_heads * HEAD_DIM)
        .astype(BF16)
    )
    base_table = owner_base(doc_lengths, doc_owners)
    sorted_rank = lookup(query_doc, base_table - doc_starts) + query_pos
    slot_count = row_count // tp_count
    column_span = slot_count * sub_count
    targets = tp_index * column_span + jnp.arange(column_span, dtype=jnp.int32)
    selector = (targets[:, None] == sorted_rank[None, :]).astype(BF16)
    placed = jnp.dot(selector, latents, preferred_element_type=F32)
    arrived = lax.psum_scatter(placed.astype(BF16), "sub", scatter_dimension=0, tiled=True)
    decode_keys = jnp.dot(arrived[:, :RANK], key_up, preferred_element_type=F32).astype(BF16)
    decode_values = jnp.dot(arrived[:, RANK:], value_up, preferred_element_type=F32).astype(BF16)
    decode_cache = jnp.concatenate([decode_keys, decode_values], axis=1)
    return (attention, decode_cache)


SMEM = pl.BlockSpec(memory_space=pltpu.SMEM)
VMEM = pl.BlockSpec(memory_space=pltpu.VMEM)
ANY = pl.BlockSpec(memory_space=pl.ANY)


def cost(micros):
    return pl.CostEstimate(
        flops=int(micros * 1.1e9), bytes_accessed=int(micros * 1e6), transcendentals=0
    )


def params():
    return pltpu.CompilerParams(vmem_limit_bytes=VMEM_LIMIT)


def project_kernel(chunks, place, hidden, down, *refs):
    count = len(chunks)
    coded = refs[:count]
    rows_buf, down_buf, row_sem, down_sem = refs[count:]
    tp_index = place[0]
    depth = down.shape[0] // SLICES
    down_copies, row_copies = [], []
    for c in range(SLICES):
        span = pl.ds(c * depth, depth)
        down_copies.append(
            pltpu.make_async_copy(down.at[span, :], down_buf.at[span, :], down_sem.at[c])
        )
        down_copies[c].start()
        for k in range(count):
            first = pl.multiple_of((tp_index ^ chunks[k]) * BLOCK, BLOCK)
            copy = pltpu.make_async_copy(
                hidden.at[pl.ds(first, BLOCK), span],
                rows_buf.at[k, :, span],
                row_sem.at[k * SLICES + c],
            )
            copy.start()
            row_copies.append(copy)
    sums = [None] * count
    for c in range(SLICES):
        span = slice(c * depth, (c + 1) * depth)
        down_copies[c].wait()
        for k in range(count):
            row_copies[c * count + k].wait()
            term = jnp.dot(rows_buf[k, :, span], down_buf[span, :], preferred_element_type=F32)
            sums[k] = term if c == 0 else sums[k] + term
    lane = lax.broadcasted_iota(jnp.int32, (BLOCK, 128), 1)
    for k in range(count):
        powers = []
        for half in range(2):
            piece = sums[k][:, half * RANK : (half + 1) * RANK]
            top = jnp.max(jnp.abs(piece), axis=1, keepdims=True)
            power = jnp.ceil(jnp.log2(jnp.maximum(top, 1e-30)) + 1e-3)
            code = jnp.round(piece * (CODE_TOP * jnp.exp2(-power))).astype(jnp.int32)
            coded[k][:BLOCK, half * RANK : (half + 1) * RANK] = code.astype(jnp.int16)
            powers.append(power)
        table = jnp.transpose(jnp.where(lane == 0, powers[0], powers[1]))[:SCALE_ROWS]
        table = table.astype(jnp.int32).astype(jnp.int16)
        coded[k][BLOCK:, :RANK] = table
        coded[k][BLOCK:, RANK:] = table


def project(place, hidden, down, chunks):
    width = down.shape[1]
    count = len(chunks)
    return pl.pallas_call(
        functools.partial(project_kernel, chunks),
        out_shape=[jax.ShapeDtypeStruct((BLOCK + SCALE_ROWS, width), jnp.int16)] * count,
        in_specs=[SMEM, ANY, ANY],
        out_specs=[VMEM] * count,
        scratch_shapes=[
            pltpu.VMEM((count, BLOCK, hidden.shape[1]), BF16),
            pltpu.VMEM(down.shape, BF16),
            pltpu.SemaphoreType.DMA((count * SLICES,)),
            pltpu.SemaphoreType.DMA((SLICES,)),
        ],
        compiler_params=pltpu.CompilerParams(vmem_limit_bytes=60 * 1024 * 1024),
        name="project",
    )(place, hidden, down)


def expand_kernel(parts, place, *refs):
    coded = refs[:parts]
    key_up, value_up = refs[parts : parts + 2]
    pieces = refs[parts + 2 :]
    tp_index = place[0]
    halves = []
    columns = []
    for k in range(parts):
        powers = coded[k][BLOCK:, :RANK].astype(jnp.int32).astype(F32)
        columns.append(jnp.transpose(jnp.exp2(powers) * (1.0 / CODE_TOP)))
    for half in range(2):
        total = None
        for k in range(parts):
            code = coded[k][:BLOCK, half * RANK : (half + 1) * RANK].astype(jnp.int32).astype(F32)
            term = code * columns[k][:, half : half + 1]
            total = term if total is None else total + term
        halves.append(total.astype(BF16))
        pieces[0][:, half * RANK : (half + 1) * RANK] = halves[half]
    for k in range(parts):
        lead = pieces[k].shape[1] - BLOCK
        head = tp_index ^ k
        cols = pl.ds(pl.multiple_of(head * HEAD_DIM, HEAD_DIM), HEAD_DIM)
        keys = jnp.dot(halves[0], key_up[:, cols], preferred_element_type=F32).astype(BF16)
        values = lax.dot_general(
            value_up[cols, :], halves[1], NT, preferred_element_type=F32
        ).astype(BF16)
        pieces[k][:HEAD_DIM, lead:] = values
        pieces[k][HEAD_DIM:, lead : lead + HEAD_DIM] = keys[:HEAD_DIM]
        pieces[k][HEAD_DIM:, lead + HEAD_DIM :] = keys[HEAD_DIM:]


def expand(place, coded, key_up, value_rows):
    parts = len(coded)
    return pl.pallas_call(
        functools.partial(expand_kernel, parts),
        out_shape=[jax.ShapeDtypeStruct((BLOCK, 2 * RANK + BLOCK), BF16)]
        + [jax.ShapeDtypeStruct((BLOCK, BLOCK), BF16)] * (parts - 1),
        in_specs=[SMEM] + [VMEM] * (parts + 2),
        out_specs=[VMEM] * parts,
        compiler_params=params(),
        name="expand",
    )(place, *coded, key_up, value_rows)


def pick_kernel(planes, subs, row_count, place, lengths, owners, *refs):
    latents, picked = refs[:subs], refs[subs:]
    tp_index, sub_index = place[0], place[1]
    docs = lengths.shape[0]
    sizes = [lengths[d] for d in range(docs)]
    holders = [owners[d] for d in range(docs)]
    shifts, begins, begin = [], [], 0
    for d in range(docs):
        base = 0
        for e in range(docs):
            if e == d:
                continue
            ahead = holders[e] <= holders[d] if e < d else holders[e] < holders[d]
            base = base + jnp.where(ahead, sizes[e], 0)
        begins.append(begin)
        shifts.append(base - begin)
        begin = begin + sizes[d]
    slot = lax.broadcasted_iota(jnp.int32, (BLOCK, 1), 0) + sub_index * BLOCK
    lane = lax.broadcasted_iota(jnp.int32, (8, BLOCK), 1)
    ranks = []
    for j in range(subs):
        position = lane + (sub_index ^ j) * row_count + tp_index * BLOCK
        shift = jnp.full((8, BLOCK), 0, jnp.int32) + shifts[0]
        for d in range(1, docs):
            shift = jnp.where(position >= begins[d], shifts[d], shift)
        ranks.append((position + shift)[:1])
    for out, group in zip(picked, planes):
        for n, k in enumerate(group):
            target = slot + (tp_index ^ k) * (subs * BLOCK)
            total = None
            for j in range(subs):
                chosen = jnp.where(target == ranks[j], 1.0, 0.0).astype(BF16)
                term = jnp.dot(chosen, latents[j][:, : 2 * RANK], preferred_element_type=F32)
                total = term if total is None else total + term
            out[n * BLOCK : (n + 1) * BLOCK, :] = total.astype(BF16)


def pick(place, lengths, owners, latents, planes, row_count):
    subs = len(latents)
    return pl.pallas_call(
        functools.partial(pick_kernel, planes, subs, row_count),
        out_shape=[
            jax.ShapeDtypeStruct((len(group) * BLOCK, 2 * RANK), BF16) for group in planes
        ],
        in_specs=[SMEM] * 3 + [VMEM] * subs,
        out_specs=[VMEM] * len(planes),
        compiler_params=params(),
        name="pick",
    )(place, lengths, owners, *latents)


def rebuild_kernel(parts, *refs):
    arrived, (key_up, value_up, out) = refs[:parts], refs[parts:]
    total = arrived[0][...]
    for k in range(1, parts):
        total = total + arrived[k][:BLOCK, :]
    width = key_up.shape[1]
    out[:, :width] = jnp.dot(total[:, :RANK], key_up[...], preferred_element_type=F32).astype(BF16)
    out[:, width:] = jnp.dot(total[:, RANK:], value_up[...], preferred_element_type=F32).astype(BF16)


def rebuild(arrived, key_up, value_up):
    parts = len(arrived)
    return pl.pallas_call(
        functools.partial(rebuild_kernel, parts),
        out_shape=jax.ShapeDtypeStruct((BLOCK, 2 * key_up.shape[1]), BF16),
        in_specs=[VMEM] * (parts + 2),
        out_specs=VMEM,
        compiler_params=params(),
        name="rebuild",
    )(*arrived, key_up, value_up)


def load_pieces(pieces, blocks, keys, values, sems):
    copies = []
    for n, block in enumerate(blocks):
        first = pl.multiple_of(block * BLOCK, BLOCK)
        copies.append(
            pltpu.make_async_copy(
                pieces[n].at[:HEAD_DIM, :], values.at[:, pl.ds(first, BLOCK)], sems.at[n, 0]
            )
        )
        for side in range(2):
            copies.append(
                pltpu.make_async_copy(
                    pieces[n].at[HEAD_DIM:, side * HEAD_DIM : (side + 1) * HEAD_DIM],
                    keys.at[pl.ds(first + side * HEAD_DIM, HEAD_DIM), :],
                    sems.at[n, side + 1],
                )
            )
    for copy in copies:
        copy.start()
    return copies


def split(refs):
    pieces = []
    for ref in refs:
        lead = ref.shape[1] - BLOCK
        for k in range(ref.shape[0] // BLOCK):
            pieces.append(ref.at[k * BLOCK : (k + 1) * BLOCK, lead : lead + BLOCK])
    return pieces


def clear_blocks(keys, values, first):
    keys[pl.ds(first, BLOCK), :] = jnp.zeros((BLOCK, HEAD_DIM), BF16)
    values[:, pl.ds(first, BLOCK)] = jnp.zeros((HEAD_DIM, BLOCK), BF16)


def longest(keys):
    every = keys[...]
    ones = jnp.ones((8, HEAD_DIM), BF16)
    return jnp.max(lax.dot_general(ones, every * every, NT, preferred_element_type=F32))


def row_bounds(lengths, first):
    position = first + lax.broadcasted_iota(jnp.int32, (1, BLOCK), 1)
    begin, low, high = 0, 0, 0
    begin_row = jnp.zeros((1, BLOCK), jnp.int32)
    for d in range(lengths.shape[0]):
        begin_row = jnp.where(position >= begin, begin, begin_row)
        low = jnp.where(first >= begin, begin, low)
        high = jnp.where(first + BLOCK - 1 >= begin, begin, high)
        begin = begin + lengths[d]
    return position, begin_row, low, high


def absorb(span, keys, values, queries, state, mask, fresh, online):
    tops, sums, mix = state
    heads = queries.shape[1] // HEAD_DIM

    def scores_of(head):
        query = queries[:, head * HEAD_DIM : (head + 1) * HEAD_DIM]
        return lax.dot_general(keys[span, :], query, NT, preferred_element_type=F32)

    ahead = [scores_of(head) for head in range(min(AHEAD, heads))]
    for head in range(heads):
        scores = ahead.pop(0) * GAIN
        if head + AHEAD < heads:
            ahead.append(scores_of(head + AHEAD))
        if mask is not None:
            scores = scores + mask[: scores.shape[0], :]
        row = slice(head, head + 1)
        if fresh:
            top = jnp.max(scores, axis=0, keepdims=True) + LIFT
            tops[row, :] = top
        else:
            before = tops[row, :]
            top = before
            if online:
                top = jnp.maximum(before, jnp.max(scores, axis=0, keepdims=True) + LIFT)
                tops[row, :] = top
        weights = jnp.exp2(scores - top)
        total = jnp.sum(weights, axis=0, keepdims=True)
        result = jnp.dot(values[:, span], weights.astype(BF16), preferred_element_type=F32)
        if fresh:
            sums[row, :] = total
            mix[head] = result
        elif online:
            rescale = jnp.exp2(before - top)
            sums[row, :] = sums[row, :] * rescale + total
            mix[head] = mix[head] * rescale + result
        else:
            sums[row, :] += total
            mix[head] += result


def set_mask(mask, allowed):
    mask[: allowed.shape[0], :] = jnp.where(allowed, 0.0, -1e30)


def bounded(queries, tops, key_top):
    every = queries[...]
    heads = tops.shape[0]
    lane = lax.broadcasted_iota(jnp.int32, (heads, every.shape[1]), 1) // HEAD_DIM
    of_head = lane == lax.broadcasted_iota(jnp.int32, lane.shape, 0)
    of_head = jnp.where(of_head, 1.0, 0.0).astype(BF16)
    squares = lax.dot_general(of_head, every * every, NT, preferred_element_type=F32)
    reach = jnp.sqrt(squares * key_top) * (GAIN * 1.02) - (tops[...] - LIFT)
    return jnp.max(reach) <= SPAN


def attend_near_kernel(parts, row_count, place, lengths, queries, *refs):
    pieces = refs[:parts]
    tops, sums, mix, packed, keys, values, mask, key_top, sems, pack_sems = refs[parts:]
    tops, sums, mix = state = (tops.at[0], sums.at[0], mix.at[0])
    step = pl.program_id(0)
    tp_index, sub_index = place[0], place[1]
    packs = [
        pltpu.make_async_copy(
            pieces[k], packed.at[(k - 1) * BLOCK : k * BLOCK, :], pack_sems.at[k]
        )
        for k in range(1, parts)
    ]
    pieces = split(pieces)

    @pl.when(step == 0)
    def _():
        copies = load_pieces(
            pieces, [(tp_index ^ k) + 1 for k in range(parts)], keys, values, sems
        )
        for copy in packs:
            copy.start()
        clear_blocks(keys, values, 0)
        for copy in copies:
            copy.wait()
        key_top[0] = longest(keys)

    start = sub_index * row_count
    first = start + step * BLOCK
    position, begin_row, low, high = row_bounds(lengths, first)
    begin_row = jnp.maximum(begin_row, start)
    low_block = jnp.maximum(low - start, 0) // BLOCK
    full_block = (jnp.maximum(high - start, 0) + BLOCK - 1) // BLOCK
    last = (step - low_block) // 2
    clear = jnp.minimum(jnp.maximum(step - 1 - full_block, 0) // 2, last)
    key_iota = lax.broadcasted_iota(jnp.int32, (2 * BLOCK, BLOCK), 0) + (first - BLOCK)

    def take(pair, masked, online):
        span = pl.ds(pl.multiple_of((step - 2 * pair) * BLOCK, BLOCK), 2 * BLOCK)
        absorb(span, keys, values, queries, state, mask if masked else None, False, online)

    @pl.when(low_block == step)
    def _():
        span = pl.ds(pl.multiple_of((step + 1) * BLOCK, BLOCK), BLOCK)
        own_iota = key_iota[BLOCK:, :]
        set_mask(mask, (own_iota <= position) & (own_iota >= begin_row))
        absorb(span, keys, values, queries, state, mask, True, False)

    @pl.when(low_block < step)
    def _():
        span = pl.ds(pl.multiple_of(step * BLOCK, BLOCK), 2 * BLOCK)
        set_mask(mask, (key_iota <= position) & (key_iota >= begin_row))
        absorb(span, keys, values, queries, state, mask, True, False)

    @pl.when(last > 0)
    def _():
        safe = bounded(queries, tops, key_top[0])
        for online in (False, True):

            @pl.when(jnp.logical_not(safe) if online else safe)
            def _():
                @pl.loop(1, clear + 1)
                def _(pair):
                    take(pair, False, online)

                @pl.loop(clear + 1, last + 1)
                def _(pair):
                    set_mask(mask, key_iota - 2 * pair * BLOCK >= begin_row)
                    take(pair, True, online)

    @pl.when(step == pl.num_programs(0) - 1)
    def _():
        for copy in packs:
            copy.wait()


def attend_far_kernel(parts, subs, groups, row_count, place, lengths, queries, *refs):
    tops_in, sums_in, mix_in = refs[:3]
    held, refs = refs[3 : 3 + groups], refs[3 + groups :]
    out, keys, values, mask, tops, sums, mix, key_top, sems = refs
    pieces = split(held)
    heads = tops.shape[0]
    step = pl.program_id(0)
    tp_index, sub_index = place[0], place[1]

    @pl.when(step == 0)
    def _():
        blocks = [
            (sub_index ^ j) * parts + (tp_index ^ k) for j in range(1, subs) for k in range(parts)
        ]
        copies = load_pieces(pieces, blocks, keys, values, sems)
        for k in range(parts):
            clear_blocks(keys, values, pl.multiple_of((sub_index * parts + k) * BLOCK, BLOCK))
        for copy in copies:
            copy.wait()
        key_top[0] = longest(keys)

    first = sub_index * row_count + step * BLOCK
    position, begin_row, low, high = row_bounds(lengths, first)
    end_block = sub_index * parts
    low_block = low // BLOCK
    full_block = (high + BLOCK - 1) // BLOCK
    count = jnp.maximum(end_block - low_block, 0)
    last = count // 2
    clear = jnp.minimum(jnp.maximum(end_block - full_block, 0) // 2, last)

    @pl.when(count == 0)
    def _():
        finish(mix_in.at[0], sums_in.at[0], out)

    @pl.when(count > 0)
    def _():
        tops[...] = tops_in[0]
        sums[...] = sums_in[0]
        mix[...] = mix_in[0]

        def take(block, blocks, masked, online):
            begin = block * BLOCK
            span = pl.ds(pl.multiple_of(begin, BLOCK), blocks * BLOCK)
            if masked:
                key_iota = lax.broadcasted_iota(jnp.int32, (blocks * BLOCK, BLOCK), 0)
                set_mask(mask, key_iota + begin >= begin_row)
            state = (tops, sums, mix)
            absorb(span, keys, values, queries, state, mask if masked else None, False, online)

        safe = bounded(queries, tops, key_top[0])
        for online in (False, True):

            @pl.when(jnp.logical_not(safe) if online else safe)
            def _():
                @pl.loop(0, clear)
                def _(pair):
                    take(end_block - 2 - 2 * pair, 2, False, online)

                @pl.loop(clear, last)
                def _(pair):
                    take(end_block - 2 - 2 * pair, 2, True, online)

                @pl.when(count > 2 * last)
                def _():
                    take(low_block, 1, True, online)

        finish(mix, sums, out)


def finish(mix, sums, out):
    for head in range(mix.shape[0]):
        result = mix[head] * (1.0 / sums[head : head + 1, :])
        out[:, head * HEAD_DIM : (head + 1) * HEAD_DIM] = jnp.transpose(result).astype(BF16)


def attend_specs(queries):
    row_count, width = queries.shape
    heads, steps = width // HEAD_DIM, row_count // BLOCK
    shapes = [(heads, BLOCK), (heads, BLOCK), (heads, HEAD_DIM, BLOCK)]
    row_spec = pl.BlockSpec((BLOCK, width), lambda i: (i, 0))
    state_specs = [
        pl.BlockSpec((1, *shape), lambda i, rank=len(shape): (i,) + (0,) * rank)
        for shape in shapes
    ]
    state_shapes = [jax.ShapeDtypeStruct((steps, *shape), F32) for shape in shapes]
    scratch = [pltpu.VMEM(shape, F32) for shape in shapes]
    return (steps,), row_spec, state_specs, state_shapes, scratch


def store_shapes(blocks, pieces):
    return [
        pltpu.VMEM((blocks * BLOCK, HEAD_DIM), BF16),
        pltpu.VMEM((HEAD_DIM, blocks * BLOCK), BF16),
        pltpu.VMEM((2 * BLOCK, BLOCK), F32),
    ], [pltpu.SMEM((1,), F32), pltpu.SemaphoreType.DMA((pieces, 3))]


def attend_near(place, lengths, queries, pieces):
    parts = len(pieces)
    grid, row_spec, state_specs, state_shapes, _ = attend_specs(queries)
    stores, rest = store_shapes(parts + 1, parts)
    return pl.pallas_call(
        functools.partial(attend_near_kernel, parts, queries.shape[0]),
        grid=grid,
        out_shape=state_shapes + [jax.ShapeDtypeStruct(((parts - 1) * BLOCK, BLOCK), BF16)],
        in_specs=[SMEM, SMEM, row_spec] + [ANY] * parts,
        out_specs=state_specs + [ANY],
        scratch_shapes=stores + rest + [pltpu.SemaphoreType.DMA((parts,))],
        compiler_params=params(),
        cost_estimate=cost(12),
        name="attend_near",
    )(place, lengths, queries, *pieces)


def attend_far(place, lengths, queries, state, pieces, parts, subs):
    grid, row_spec, state_specs, _, scratch = attend_specs(queries)
    stores, rest = store_shapes(parts * subs, parts * (subs - 1))
    return pl.pallas_call(
        functools.partial(attend_far_kernel, parts, subs, len(pieces), queries.shape[0]),
        grid=grid,
        out_shape=jax.ShapeDtypeStruct(queries.shape, BF16),
        in_specs=[SMEM, SMEM, row_spec] + state_specs + [ANY] * len(pieces),
        out_specs=row_spec,
        scratch_shapes=stores + scratch + rest,
        compiler_params=params(),
        cost_estimate=cost(20),
        name="attend_far",
    )(place, lengths, queries, *state, *pieces)


def swap(value, axis, bits):
    count = lax.axis_size(axis)
    return lax.ppermute(value, axis, [(i, i ^ bits) for i in range(count)])


def per_device(hidden_states, queries, latent_down, key_up, value_up, doc_lengths, doc_owners):
    row_count = hidden_states.shape[0]
    parts = lax.axis_size("tp")
    subs = lax.axis_size("sub")
    place = jnp.stack([lax.axis_index("tp"), lax.axis_index("sub")]).astype(jnp.int32)
    value_rows = value_up.T
    far = [
        project(place, hidden_states, latent_down, (k,))[0] for k in range(parts // 2, parts)
    ]
    far = [swap(item, "tp", k) for k, item in enumerate(far, parts // 2)]
    near = project(place, hidden_states, latent_down, tuple(range(parts // 2)))
    near = [near[0]] + [swap(item, "tp", k) for k, item in enumerate(near[1:], 1)]
    coded = near + far
    own, *pieces = expand(place, coded, key_up, value_rows)
    arrivals = [swap(item, "tp", k) for k, item in enumerate(pieces, 1)]

    half = subs // 2
    order, rows, reach = [0], [own], half
    while reach >= 1:
        order = order + [item ^ reach for item in order]
        far_rows = [swap(item, "sub", reach) for item in rows]
        far_rows, arrivals = lax.optimization_barrier((far_rows, arrivals))
        rows = rows + list(far_rows)
        reach //= 2
    rows = [rows[order.index(j)] for j in range(subs)]
    planes = ((1, 3), (0,), (2,))
    leaving, kept, across = pick(place, doc_lengths, doc_owners, rows, planes, row_count)
    passed = swap(leaving, "tp", 1)

    gate, kept = lax.optimization_barrier((place, kept))
    *state, packed = attend_near(gate, doc_lengths, queries, [own, *arrivals])
    crossed = [swap(item, "sub", half) for item in arrivals]
    crossed, state, packed, passed = lax.optimization_barrier((crossed, state, packed, passed))

    blocks, reach = [[packed], list(crossed)], half // 2
    while reach >= 1:
        blocks = blocks + [[swap(item, "sub", reach) for item in group] for group in blocks]
        reach //= 2
    blocks = [blocks[order.index(j)] for j in range(subs)]

    second = swap(across + passed[BLOCK:], "tp", 2)
    flat = []
    for j in range(1, subs):
        flat += [rows[j], *blocks[j]]
    attention = attend_far(place, doc_lengths, queries, state, flat, parts, subs)
    kept, attention = lax.optimization_barrier((kept, attention))
    decode_cache = rebuild([kept, passed, second], key_up, value_up)
    return (attention, decode_cache)


def fits(mesh):
    return mesh.shape["tp"] == KV_HEADS and mesh.shape["sub"] & (mesh.shape["sub"] - 1) == 0


def choose(mesh):
    def run(hidden_states, queries, *rest):
        rows = hidden_states.shape[0]
        direct = fits(mesh) and rows == BLOCK * mesh.shape["tp"]
        return (per_device if direct else per_device_general)(hidden_states, queries, *rest)

    return run


def solution(mesh):
    return jax.shard_map(
        choose(mesh),
        mesh=mesh,
        in_specs=(
            P(("groups", "sub"), "tp"),
            P(("groups", "sub"), "tp"),
            P("tp", None),
            P(),
            P(),
            P("groups"),
            P("groups"),
        ),
        out_specs=(P(("groups", "sub"), "tp"), P(("groups", "tp", "sub"), None)),
        check_vma=False,
    )
```

```python
import functools
import math

import jax
import jax.numpy as jnp
from jax import lax
from jax.experimental import pallas as pl
from jax.experimental.pallas import tpu as pltpu
from jax.sharding import PartitionSpec as P

HEAD_DIM = 128
Q_HEADS = 32
KV_HEADS = 4
RANK = 256
BLOCK = 256
SLICES = 4
AHEAD = 4
SCALE_ROWS = 16
CODE_TOP = 32000.0
LIFT = 24.0
SPAN = 100.0
GAIN = math.log2(math.e) / math.sqrt(HEAD_DIM)
VMEM_LIMIT = 24 * 1024 * 1024
FULL_VMEM = 60 * 1024 * 1024
F32 = jnp.float32
BF16 = jnp.bfloat16
NT = (((1,), (1,)), ((), ()))


def doc_tables(doc_lengths):
    doc_ends = jnp.cumsum(doc_lengths)
    doc_starts = doc_ends - doc_lengths
    return (doc_starts, doc_ends)


def doc_of(positions, doc_ends):
    return jnp.sum((positions[:, None] >= doc_ends[None, :]).astype(jnp.int32), axis=1)


def lookup(doc_index, doc_table):
    doc_numbers = jnp.arange(doc_table.shape[0], dtype=jnp.int32)
    picked = jnp.where(doc_index[:, None] == doc_numbers[None, :], doc_table[None, :], 0)
    return jnp.sum(picked, axis=1)


def owner_base(doc_lengths, doc_owners):
    doc_numbers = jnp.arange(doc_lengths.shape[0], dtype=jnp.int32)
    before = (doc_owners[None, :] < doc_owners[:, None]) | (
        doc_owners[None, :] == doc_owners[:, None]
    ) & (doc_numbers[None, :] < doc_numbers[:, None])
    return jnp.sum(jnp.where(before, doc_lengths[None, :], 0), axis=1)


def per_device_general(hidden_states, queries, latent_down, key_up, value_up, doc_lengths, doc_owners):
    row_count = hidden_states.shape[0]
    tp_count = lax.axis_size("tp")
    sub_count = lax.axis_size("sub")
    tp_index = lax.axis_index("tp")
    sub_index = lax.axis_index("sub")
    partial_sums = jnp.dot(hidden_states, latent_down, preferred_element_type=F32)
    latents = lax.psum(partial_sums, "tp").astype(BF16)
    local_heads = queries.shape[1] // HEAD_DIM
    per_group = Q_HEADS // KV_HEADS
    grouped = min(local_heads, per_group)
    kv_count = local_heads // grouped
    kv_first = tp_index * local_heads // per_group
    key_cols = lax.dynamic_slice_in_dim(key_up, kv_first * HEAD_DIM, kv_count * HEAD_DIM, 1)
    value_cols = lax.dynamic_slice_in_dim(value_up, kv_first * HEAD_DIM, kv_count * HEAD_DIM, 1)
    own_keys = jnp.dot(latents[:, :RANK], key_cols, preferred_element_type=F32).astype(BF16)
    own_values = jnp.dot(latents[:, RANK:], value_cols, preferred_element_type=F32).astype(BF16)
    doc_starts, doc_ends = doc_tables(doc_lengths)
    query_pos = sub_index * row_count + jnp.arange(row_count, dtype=jnp.int32)
    query_doc = doc_of(query_pos, doc_ends)
    query_grid = queries.reshape(row_count, kv_count, grouped, HEAD_DIM)
    inv_root = 1.0 / math.sqrt(HEAD_DIM)
    carried = (
        jnp.full((kv_count, grouped, row_count), -1e30, F32),
        jnp.zeros((kv_count, grouped, row_count), F32),
        jnp.zeros((kv_count, grouped, row_count, HEAD_DIM), F32),
    )
    key_piece = lax.all_gather(own_keys, "sub", axis=0, tiled=True)
    value_piece = lax.all_gather(own_values, "sub", axis=0, tiled=True)
    piece_len = key_piece.shape[0]
    block_len = math.gcd(piece_len, 1024)
    block_total = piece_len // block_len
    key_blocks = key_piece.reshape(block_total, block_len, kv_count, HEAD_DIM)
    value_blocks = value_piece.reshape(block_total, block_len, kv_count, HEAD_DIM)
    first_positions = block_len * jnp.arange(block_total, dtype=jnp.int32)

    def absorb(state, block_item):
        running_top, totals, weighted = state
        key_block, value_block, first_pos = block_item
        key_pos = first_pos + jnp.arange(block_len, dtype=jnp.int32)
        key_doc = doc_of(key_pos, doc_ends)
        allowed = (key_pos[None, :] <= query_pos[:, None]) & (
            key_doc[None, :] == query_doc[:, None]
        )
        scores = (
            jnp.einsum("qkgd,jkd->kgqj", query_grid, key_block, preferred_element_type=F32)
            * inv_root
        )
        scores = jnp.where(allowed, scores, -1e30)
        new_top = jnp.maximum(running_top, jnp.max(scores, axis=-1))
        weights = jnp.where(allowed, jnp.exp(scores - new_top[..., None]), 0.0)
        rescale = jnp.exp(running_top - new_top)
        totals = totals * rescale + jnp.sum(weights, axis=-1)
        weighted = weighted * rescale[..., None] + jnp.einsum(
            "kgqj,jkd->kgqd", weights.astype(BF16), value_block, preferred_element_type=F32
        )
        return ((new_top, totals, weighted), None)

    carried, _ = lax.scan(absorb, carried, (key_blocks, value_blocks, first_positions))
    running_top, totals, weighted = carried
    result = weighted / totals[..., None]
    attention = (
        jnp.transpose(result, (2, 0, 1, 3))
        .reshape(row_count, local_heads * HEAD_DIM)
        .astype(BF16)
    )
    base_table = owner_base(doc_lengths, doc_owners)
    sorted_rank = lookup(query_doc, base_table - doc_starts) + query_pos
    slot_count = row_count // tp_count
    column_span = slot_count * sub_count
    targets = tp_index * column_span + jnp.arange(column_span, dtype=jnp.int32)
    selector = (targets[:, None] == sorted_rank[None, :]).astype(BF16)
    placed = jnp.dot(selector, latents, preferred_element_type=F32)
    arrived = lax.psum_scatter(placed.astype(BF16), "sub", scatter_dimension=0, tiled=True)
    decode_keys = jnp.dot(arrived[:, :RANK], key_up, preferred_element_type=F32).astype(BF16)
    decode_values = jnp.dot(arrived[:, RANK:], value_up, preferred_element_type=F32).astype(BF16)
    decode_cache = jnp.concatenate([decode_keys, decode_values], axis=1)
    return (attention, decode_cache)


SMEM = pl.BlockSpec(memory_space=pltpu.SMEM)
VMEM = pl.BlockSpec(memory_space=pltpu.VMEM)
ANY = pl.BlockSpec(memory_space=pl.ANY)


def cost(micros):
    return pl.CostEstimate(
        flops=int(micros * 1.1e9), bytes_accessed=int(micros * 1e6), transcendentals=0
    )


def params():
    return pltpu.CompilerParams(vmem_limit_bytes=VMEM_LIMIT)


def project_kernel(chunks, hidden, down, *refs):
    count = len(chunks)
    coded = refs[:count]
    rows_buf, down_buf, row_sem, down_sem = refs[count:]
    tp_index = lax.axis_index("tp")
    depth = down.shape[0] // SLICES
    down_copies, row_copies = [], []
    for c in range(SLICES):
        span = pl.ds(c * depth, depth)
        down_copies.append(
            pltpu.make_async_copy(down.at[span, :], down_buf.at[span, :], down_sem.at[c])
        )
        down_copies[c].start()
        for k in range(count):
            first = pl.multiple_of((tp_index ^ chunks[k]) * BLOCK, BLOCK)
            copy = pltpu.make_async_copy(
                hidden.at[pl.ds(first, BLOCK), span],
                rows_buf.at[k, :, span],
                row_sem.at[k * SLICES + c],
            )
            copy.start()
            row_copies.append(copy)
    sums = [None] * count
    for c in range(SLICES):
        span = slice(c * depth, (c + 1) * depth)
        down_copies[c].wait()
        for k in range(count):
            row_copies[c * count + k].wait()
            term = jnp.dot(rows_buf[k, :, span], down_buf[span, :], preferred_element_type=F32)
            sums[k] = term if c == 0 else sums[k] + term
    lane = lax.broadcasted_iota(jnp.int32, (BLOCK, 128), 1)
    for k in range(count):
        powers = []
        for half in range(2):
            piece = sums[k][:, half * RANK : (half + 1) * RANK]
            top = jnp.max(jnp.abs(piece), axis=1, keepdims=True)
            power = jnp.ceil(jnp.log2(jnp.maximum(top, 1e-30)) + 1e-3)
            code = jnp.round(piece * (CODE_TOP * jnp.exp2(-power))).astype(jnp.int32)
            coded[k][:BLOCK, half * RANK : (half + 1) * RANK] = code.astype(jnp.int16)
            powers.append(power)
        table = jnp.transpose(jnp.where(lane == 0, powers[0], powers[1]))[:SCALE_ROWS]
        table = table.astype(jnp.int32).astype(jnp.int16)
        coded[k][BLOCK:, :RANK] = table
        coded[k][BLOCK:, RANK:] = table


def project(hidden, down, chunks, limit=VMEM_LIMIT):
    width = down.shape[1]
    count = len(chunks)
    return pl.pallas_call(
        functools.partial(project_kernel, chunks),
        out_shape=[jax.ShapeDtypeStruct((BLOCK + SCALE_ROWS, width), jnp.int16)] * count,
        in_specs=[ANY, ANY],
        out_specs=[VMEM] * count,
        scratch_shapes=[
            pltpu.VMEM((count, BLOCK, hidden.shape[1]), BF16),
            pltpu.VMEM(down.shape, BF16),
            pltpu.SemaphoreType.DMA((count * SLICES,)),
            pltpu.SemaphoreType.DMA((SLICES,)),
        ],
        compiler_params=pltpu.CompilerParams(vmem_limit_bytes=limit),
        name="project",
    )(hidden, down)


def expand_kernel(parts, place, *refs):
    coded = refs[:parts]
    key_up, value_up = refs[parts : parts + 2]
    pieces = refs[parts + 2 :]
    tp_index = place[0]
    halves = []
    columns = []
    for k in range(parts):
        powers = coded[k][BLOCK:, :RANK].astype(jnp.int32).astype(F32)
        columns.append(jnp.transpose(jnp.exp2(powers) * (1.0 / CODE_TOP)))
    for half in range(2):
        total = None
        for k in range(parts):
            code = coded[k][:BLOCK, half * RANK : (half + 1) * RANK].astype(jnp.int32).astype(F32)
            term = code * columns[k][:, half : half + 1]
            total = term if total is None else total + term
        halves.append(total.astype(BF16))
        pieces[0][:, half * RANK : (half + 1) * RANK] = halves[half]
    for k in range(parts):
        lead = pieces[k].shape[1] - BLOCK
        head = tp_index ^ k
        cols = pl.ds(pl.multiple_of(head * HEAD_DIM, HEAD_DIM), HEAD_DIM)
        keys = jnp.dot(halves[0], key_up[:, cols], preferred_element_type=F32).astype(BF16)
        values = lax.dot_general(
            value_up[cols, :], halves[1], NT, preferred_element_type=F32
        ).astype(BF16)
        pieces[k][:HEAD_DIM, lead:] = values
        pieces[k][HEAD_DIM:, lead : lead + HEAD_DIM] = keys[:HEAD_DIM]
        pieces[k][HEAD_DIM:, lead + HEAD_DIM :] = keys[HEAD_DIM:]


def expand(place, coded, key_up, value_rows):
    parts = len(coded)
    return pl.pallas_call(
        functools.partial(expand_kernel, parts),
        out_shape=[jax.ShapeDtypeStruct((BLOCK, 2 * RANK + BLOCK), BF16)]
        + [jax.ShapeDtypeStruct((BLOCK, BLOCK), BF16)] * (parts - 1),
        in_specs=[SMEM] + [VMEM] * (parts + 2),
        out_specs=[VMEM] * parts,
        compiler_params=params(),
        name="expand",
    )(place, *coded, key_up, value_rows)


def pick_kernel(planes, subs, row_count, place, lengths, owners, *refs):
    latents, picked = refs[:subs], refs[subs:]
    tp_index, sub_index = place[0], place[1]
    docs = lengths.shape[0]
    sizes = [lengths[d] for d in range(docs)]
    holders = [owners[d] for d in range(docs)]
    shifts, begins, begin = [], [], 0
    for d in range(docs):
        base = 0
        for e in range(docs):
            if e == d:
                continue
            ahead = holders[e] <= holders[d] if e < d else holders[e] < holders[d]
            base = base + jnp.where(ahead, sizes[e], 0)
        begins.append(begin)
        shifts.append(base - begin)
        begin = begin + sizes[d]
    slot = lax.broadcasted_iota(jnp.int32, (BLOCK, 1), 0) + sub_index * BLOCK
    lane = lax.broadcasted_iota(jnp.int32, (8, BLOCK), 1)
    ranks = []
    for j in range(subs):
        position = lane + (sub_index ^ j) * row_count + tp_index * BLOCK
        shift = jnp.full((8, BLOCK), 0, jnp.int32) + shifts[0]
        for d in range(1, docs):
            shift = jnp.where(position >= begins[d], shifts[d], shift)
        ranks.append((position + shift)[:1])
    for out, group in zip(picked, planes):
        for n, k in enumerate(group):
            target = slot + (tp_index ^ k) * (subs * BLOCK)
            total = None
            for j in range(subs):
                chosen = jnp.where(target == ranks[j], 1.0, 0.0).astype(BF16)
                term = jnp.dot(chosen, latents[j][:, : 2 * RANK], preferred_element_type=F32)
                total = term if total is None else total + term
            out[n * BLOCK : (n + 1) * BLOCK, :] = total.astype(BF16)


def pick(place, lengths, owners, latents, planes, row_count):
    subs = len(latents)
    return pl.pallas_call(
        functools.partial(pick_kernel, planes, subs, row_count),
        out_shape=[
            jax.ShapeDtypeStruct((len(group) * BLOCK, 2 * RANK), BF16) for group in planes
        ],
        in_specs=[SMEM] * 3 + [VMEM] * subs,
        out_specs=[VMEM] * len(planes),
        compiler_params=params(),
        name="pick",
    )(place, lengths, owners, *latents)


def rebuild_kernel(parts, *refs):
    arrived, (key_up, value_up, out) = refs[:parts], refs[parts:]
    total = arrived[0][...]
    for k in range(1, parts):
        total = total + arrived[k][:BLOCK, :]
    width = key_up.shape[1]
    out[:, :width] = jnp.dot(total[:, :RANK], key_up[...], preferred_element_type=F32).astype(BF16)
    out[:, width:] = jnp.dot(total[:, RANK:], value_up[...], preferred_element_type=F32).astype(BF16)


def rebuild(arrived, key_up, value_up):
    parts = len(arrived)
    return pl.pallas_call(
        functools.partial(rebuild_kernel, parts),
        out_shape=jax.ShapeDtypeStruct((BLOCK, 2 * key_up.shape[1]), BF16),
        in_specs=[VMEM] * (parts + 2),
        out_specs=VMEM,
        compiler_params=params(),
        name="rebuild",
    )(*arrived, key_up, value_up)


def load_pieces(pieces, blocks, keys, values, sems):
    copies = []
    for n, block in enumerate(blocks):
        first = pl.multiple_of(block * BLOCK, BLOCK)
        copies.append(
            pltpu.make_async_copy(
                pieces[n].at[:HEAD_DIM, :], values.at[:, pl.ds(first, BLOCK)], sems.at[n, 0]
            )
        )
        for side in range(2):
            copies.append(
                pltpu.make_async_copy(
                    pieces[n].at[HEAD_DIM:, side * HEAD_DIM : (side + 1) * HEAD_DIM],
                    keys.at[pl.ds(first + side * HEAD_DIM, HEAD_DIM), :],
                    sems.at[n, side + 1],
                )
            )
    for copy in copies:
        copy.start()
    return copies


def split(refs):
    pieces = []
    for ref in refs:
        lead = ref.shape[1] - BLOCK
        for k in range(ref.shape[0] // BLOCK):
            pieces.append(ref.at[k * BLOCK : (k + 1) * BLOCK, lead : lead + BLOCK])
    return pieces


def clear_blocks(keys, values, first):
    keys[pl.ds(first, BLOCK), :] = jnp.zeros((BLOCK, HEAD_DIM), BF16)
    values[:, pl.ds(first, BLOCK)] = jnp.zeros((HEAD_DIM, BLOCK), BF16)


def lengths_of(every):
    ones = jnp.ones((8, HEAD_DIM), BF16)
    return lax.dot_general(ones, every * every, NT, preferred_element_type=F32)


def row_bounds(lengths, first):
    position = first + lax.broadcasted_iota(jnp.int32, (1, BLOCK), 1)
    begin, low, high = 0, 0, 0
    begin_row = jnp.zeros((1, BLOCK), jnp.int32)
    for d in range(lengths.shape[0]):
        begin_row = jnp.where(position >= begin, begin, begin_row)
        low = jnp.where(first >= begin, begin, low)
        high = jnp.where(first + BLOCK - 1 >= begin, begin, high)
        begin = begin + lengths[d]
    return position, begin_row, low, high


def absorb(span, keys, values, queries, state, mask, fresh, online):
    tops, sums, mix = state
    heads = queries.shape[1] // HEAD_DIM

    def scores_of(head):
        query = queries[:, head * HEAD_DIM : (head + 1) * HEAD_DIM]
        return lax.dot_general(keys[span, :], query, NT, preferred_element_type=F32)

    ahead = [scores_of(head) for head in range(min(AHEAD, heads))]
    for head in range(heads):
        scores = ahead.pop(0) * GAIN
        if head + AHEAD < heads:
            ahead.append(scores_of(head + AHEAD))
        if mask is not None:
            scores = scores + mask[: scores.shape[0], :]
        row = slice(head, head + 1)
        if fresh:
            top = jnp.max(scores, axis=0, keepdims=True) + LIFT
            tops[row, :] = top
        else:
            before = tops[row, :]
            top = before
            if online:
                top = jnp.maximum(before, jnp.max(scores, axis=0, keepdims=True) + LIFT)
                tops[row, :] = top
        weights = jnp.exp2(scores - top)
        total = jnp.sum(weights, axis=0, keepdims=True)
        result = jnp.dot(values[:, span], weights.astype(BF16), preferred_element_type=F32)
        if fresh:
            sums[row, :] = total
            mix[head] = result
        elif online:
            rescale = jnp.exp2(before - top)
            sums[row, :] = sums[row, :] * rescale + total
            mix[head] = mix[head] * rescale + result
        else:
            sums[row, :] += total
            mix[head] += result


def set_mask(mask, allowed):
    mask[: allowed.shape[0], :] = jnp.where(allowed, 0.0, -1e30)


def bounded(queries, tops, key_top):
    every = queries[...]
    heads = tops.shape[0]
    lane = lax.broadcasted_iota(jnp.int32, (heads, every.shape[1]), 1) // HEAD_DIM
    of_head = lane == lax.broadcasted_iota(jnp.int32, lane.shape, 0)
    of_head = jnp.where(of_head, 1.0, 0.0).astype(BF16)
    squares = lax.dot_general(of_head, every * every, NT, preferred_element_type=F32)
    reach = jnp.sqrt(squares * key_top) * (GAIN * 1.02) - (tops[...] - LIFT)
    return jnp.max(reach) <= SPAN


def attend_near_kernel(parts, row_count, place, lengths, queries, *refs):
    pieces = refs[:parts]
    tops, sums, mix, packed, keys, values, mask, key_top, sems, pack_sems = refs[parts:]
    tops, sums, mix = state = (tops.at[0], sums.at[0], mix.at[0])
    step = pl.program_id(0)
    tp_index, sub_index = place[0], place[1]
    packs = [
        pltpu.make_async_copy(
            pieces[k], packed.at[(k - 1) * BLOCK : k * BLOCK, :], pack_sems.at[k]
        )
        for k in range(1, parts)
    ]
    pieces = split(pieces)

    @pl.when(step == 0)
    def _():
        copies = load_pieces(
            pieces, [(tp_index ^ k) + 1 for k in range(parts)], keys, values, sems
        )
        for copy in packs:
            copy.start()
        clear_blocks(keys, values, 0)
        for copy in copies:
            copy.wait()
        key_top[0] = jnp.max(lengths_of(keys[...]))

    start = sub_index * row_count
    first = start + step * BLOCK
    position, begin_row, low, high = row_bounds(lengths, first)
    begin_row = jnp.maximum(begin_row, start)
    low_block = jnp.maximum(low - start, 0) // BLOCK
    full_block = (jnp.maximum(high - start, 0) + BLOCK - 1) // BLOCK
    last = (step - low_block) // 2
    clear = jnp.minimum(jnp.maximum(step - 1 - full_block, 0) // 2, last)
    key_iota = lax.broadcasted_iota(jnp.int32, (2 * BLOCK, BLOCK), 0) + (first - BLOCK)

    def take(pair, masked, online):
        span = pl.ds(pl.multiple_of((step - 2 * pair) * BLOCK, BLOCK), 2 * BLOCK)
        absorb(span, keys, values, queries, state, mask if masked else None, False, online)

    @pl.when(low_block == step)
    def _():
        span = pl.ds(pl.multiple_of((step + 1) * BLOCK, BLOCK), BLOCK)
        own_iota = key_iota[BLOCK:, :]
        set_mask(mask, (own_iota <= position) & (own_iota >= begin_row))
        absorb(span, keys, values, queries, state, mask, True, False)

    @pl.when(low_block < step)
    def _():
        span = pl.ds(pl.multiple_of(step * BLOCK, BLOCK), 2 * BLOCK)
        set_mask(mask, (key_iota <= position) & (key_iota >= begin_row))
        absorb(span, keys, values, queries, state, mask, True, False)

    @pl.when(last > 0)
    def _():
        safe = bounded(queries, tops, key_top[0])
        for online in (False, True):

            @pl.when(jnp.logical_not(safe) if online else safe)
            def _():
                @pl.loop(1, clear + 1)
                def _(pair):
                    take(pair, False, online)

                @pl.loop(clear + 1, last + 1)
                def _(pair):
                    set_mask(mask, key_iota - 2 * pair * BLOCK >= begin_row)
                    take(pair, True, online)

    @pl.when(step == pl.num_programs(0) - 1)
    def _():
        for copy in packs:
            copy.wait()


def attend_far_kernel(parts, subs, groups, row_count, place, lengths, queries, *refs):
    tops_in, sums_in, mix_in = refs[:3]
    held, refs = refs[3 : 3 + groups], refs[3 + groups :]
    out, keys, values, mask, tops, sums, mix, key_top, sems = refs
    pieces = split(held)
    heads = tops.shape[0]
    step = pl.program_id(0)
    tp_index, sub_index = place[0], place[1]

    @pl.when(step == 0)
    def _():
        blocks = [
            (sub_index ^ j) * parts + (tp_index ^ k) for j in range(1, subs) for k in range(parts)
        ]
        copies = load_pieces(pieces, blocks, keys, values, sems)
        for copy in copies:
            copy.wait()
        most = lax.fori_loop(
            0,
            sub_index,
            lambda j, most: jnp.maximum(
                most, lengths_of(keys[pl.ds(pl.multiple_of(j * row_count, BLOCK), row_count), :])
            ),
            jnp.zeros((8, row_count), F32),
        )
        key_top[0] = jnp.max(most)

    first = sub_index * row_count + step * BLOCK
    position, begin_row, low, high = row_bounds(lengths, first)
    end_block = sub_index * parts
    low_block = low // BLOCK
    full_block = (high + BLOCK - 1) // BLOCK
    count = jnp.maximum(end_block - low_block, 0)
    last = count // 2
    clear = jnp.minimum(jnp.maximum(end_block - full_block, 0) // 2, last)

    @pl.when(count == 0)
    def _():
        finish(mix_in.at[0], sums_in.at[0], out)

    @pl.when(count > 0)
    def _():
        tops[...] = tops_in[0]
        sums[...] = sums_in[0]
        mix[...] = mix_in[0]

        def take(block, blocks, masked, online):
            begin = block * BLOCK
            span = pl.ds(pl.multiple_of(begin, BLOCK), blocks * BLOCK)
            if masked:
                key_iota = lax.broadcasted_iota(jnp.int32, (blocks * BLOCK, BLOCK), 0)
                set_mask(mask, key_iota + begin >= begin_row)
            state = (tops, sums, mix)
            absorb(span, keys, values, queries, state, mask if masked else None, False, online)

        safe = bounded(queries, tops, key_top[0])
        for online in (False, True):

            @pl.when(jnp.logical_not(safe) if online else safe)
            def _():
                @pl.loop(0, clear)
                def _(pair):
                    take(end_block - 2 - 2 * pair, 2, False, online)

                @pl.loop(clear, last)
                def _(pair):
                    take(end_block - 2 - 2 * pair, 2, True, online)

                @pl.when(count > 2 * last)
                def _():
                    take(low_block, 1, True, online)

        finish(mix, sums, out)


def finish(mix, sums, out):
    for head in range(mix.shape[0]):
        result = mix[head] * (1.0 / sums[head : head + 1, :])
        out[:, head * HEAD_DIM : (head + 1) * HEAD_DIM] = jnp.transpose(result).astype(BF16)


def attend_specs(queries):
    row_count, width = queries.shape
    heads, steps = width // HEAD_DIM, row_count // BLOCK
    shapes = [(heads, BLOCK), (heads, BLOCK), (heads, HEAD_DIM, BLOCK)]
    row_spec = pl.BlockSpec((BLOCK, width), lambda i: (i, 0))
    state_specs = [
        pl.BlockSpec((1, *shape), lambda i, rank=len(shape): (i,) + (0,) * rank)
        for shape in shapes
    ]
    state_shapes = [jax.ShapeDtypeStruct((steps, *shape), F32) for shape in shapes]
    scratch = [pltpu.VMEM(shape, F32) for shape in shapes]
    return (steps,), row_spec, state_specs, state_shapes, scratch


def store_shapes(blocks, pieces):
    return [
        pltpu.VMEM((blocks * BLOCK, HEAD_DIM), BF16),
        pltpu.VMEM((HEAD_DIM, blocks * BLOCK), BF16),
        pltpu.VMEM((2 * BLOCK, BLOCK), F32),
    ], [pltpu.SMEM((1,), F32), pltpu.SemaphoreType.DMA((pieces, 3))]


def attend_near(place, lengths, queries, pieces):
    parts = len(pieces)
    grid, row_spec, state_specs, state_shapes, _ = attend_specs(queries)
    stores, rest = store_shapes(parts + 1, parts)
    return pl.pallas_call(
        functools.partial(attend_near_kernel, parts, queries.shape[0]),
        grid=grid,
        out_shape=state_shapes + [jax.ShapeDtypeStruct(((parts - 1) * BLOCK, BLOCK), BF16)],
        in_specs=[SMEM, SMEM, row_spec] + [ANY] * parts,
        out_specs=state_specs + [ANY],
        scratch_shapes=stores + rest + [pltpu.SemaphoreType.DMA((parts,))],
        compiler_params=params(),
        cost_estimate=cost(12),
        name="attend_near",
    )(place, lengths, queries, *pieces)


def attend_far(place, lengths, queries, state, pieces, parts, subs):
    grid, row_spec, state_specs, _, scratch = attend_specs(queries)
    stores, rest = store_shapes(parts * subs, parts * (subs - 1))
    return pl.pallas_call(
        functools.partial(attend_far_kernel, parts, subs, len(pieces), queries.shape[0]),
        grid=grid,
        out_shape=jax.ShapeDtypeStruct(queries.shape, BF16),
        in_specs=[SMEM, SMEM, row_spec] + state_specs + [ANY] * len(pieces),
        out_specs=row_spec,
        scratch_shapes=stores + scratch + rest,
        compiler_params=params(),
        cost_estimate=cost(20),
        name="attend_far",
    )(place, lengths, queries, *state, *pieces)


def swap(value, axis, bits):
    count = lax.axis_size(axis)
    return lax.ppermute(value, axis, [(i, i ^ bits) for i in range(count)])


def per_device(hidden_states, queries, latent_down, key_up, value_up, doc_lengths, doc_owners):
    row_count = hidden_states.shape[0]
    parts = lax.axis_size("tp")
    subs = lax.axis_size("sub")
    place = jnp.stack([lax.axis_index("tp"), lax.axis_index("sub")]).astype(jnp.int32)
    value_rows = value_up.T
    far = [
        project(hidden_states, latent_down, (k,), FULL_VMEM)[0]
        for k in range(parts // 2, parts)
    ]
    far = [swap(item, "tp", k) for k, item in enumerate(far, parts // 2)]
    near = project(hidden_states, latent_down, tuple(range(parts // 2)))
    near = [near[0]] + [swap(item, "tp", k) for k, item in enumerate(near[1:], 1)]
    coded = near + far
    own, *pieces = expand(place, coded, key_up, value_rows)
    arrivals = [swap(item, "tp", k) for k, item in enumerate(pieces, 1)]

    half = subs // 2
    order, rows, reach = [0], [own], half
    while reach >= 1:
        order = order + [item ^ reach for item in order]
        far_rows = [swap(item, "sub", reach) for item in rows]
        far_rows, arrivals = lax.optimization_barrier((far_rows, arrivals))
        rows = rows + list(far_rows)
        reach //= 2
    rows = [rows[order.index(j)] for j in range(subs)]
    planes = ((1, 3), (0,), (2,))
    leaving, kept, across = pick(place, doc_lengths, doc_owners, rows, planes, row_count)
    passed = swap(leaving, "tp", 1)

    gate, kept = lax.optimization_barrier((place, kept))
    *state, packed = attend_near(gate, doc_lengths, queries, [own, *arrivals])
    crossed = [swap(item, "sub", half) for item in arrivals]
    crossed, state, packed, passed = lax.optimization_barrier((crossed, state, packed, passed))

    blocks, reach = [[packed], list(crossed)], half // 2
    while reach >= 1:
        blocks = blocks + [[swap(item, "sub", reach) for item in group] for group in blocks]
        reach //= 2
    blocks = [blocks[order.index(j)] for j in range(subs)]

    second = swap(across + passed[BLOCK:], "tp", 2)
    flat = []
    for j in range(1, subs):
        flat += [rows[j], *blocks[j]]
    attention = attend_far(place, doc_lengths, queries, state, flat, parts, subs)
    kept, attention = lax.optimization_barrier((kept, attention))
    decode_cache = rebuild([kept, passed, second], key_up, value_up)
    return (attention, decode_cache)


def fits(mesh):
    return mesh.shape["tp"] == KV_HEADS and mesh.shape["sub"] & (mesh.shape["sub"] - 1) == 0


def choose(mesh):
    def run(hidden_states, queries, *rest):
        rows = hidden_states.shape[0]
        direct = fits(mesh) and rows == BLOCK * mesh.shape["tp"]
        return (per_device if direct else per_device_general)(hidden_states, queries, *rest)

    return run


def solution(mesh):
    return jax.shard_map(
        choose(mesh),
        mesh=mesh,
        in_specs=(
            P(("groups", "sub"), "tp"),
            P(("groups", "sub"), "tp"),
            P("tp", None),
            P(),
            P(),
            P("groups"),
            P("groups"),
        ),
        out_specs=(P(("groups", "sub"), "tp"), P(("groups", "tp", "sub"), None)),
        check_vma=False,
    )
```

```python
import functools
import math

import jax
import jax.numpy as jnp
from jax import lax
from jax.experimental import pallas as pl
from jax.experimental.pallas import tpu as pltpu
from jax.sharding import PartitionSpec as P

HEAD_DIM = 128
Q_HEADS = 32
KV_HEADS = 4
RANK = 256
BLOCK = 256
SLICES = 4
AHEAD = 4
SCALE_ROWS = 16
CODE_TOP = 32000.0
LIFT = 24.0
SPAN = 100.0
GAIN = math.log2(math.e) / math.sqrt(HEAD_DIM)
VMEM_LIMIT = 24 * 1024 * 1024
FULL_VMEM = 60 * 1024 * 1024
F32 = jnp.float32
BF16 = jnp.bfloat16
NT = (((1,), (1,)), ((), ()))


def doc_tables(doc_lengths):
    doc_ends = jnp.cumsum(doc_lengths)
    doc_starts = doc_ends - doc_lengths
    return (doc_starts, doc_ends)


def doc_of(positions, doc_ends):
    return jnp.sum((positions[:, None] >= doc_ends[None, :]).astype(jnp.int32), axis=1)


def lookup(doc_index, doc_table):
    doc_numbers = jnp.arange(doc_table.shape[0], dtype=jnp.int32)
    picked = jnp.where(doc_index[:, None] == doc_numbers[None, :], doc_table[None, :], 0)
    return jnp.sum(picked, axis=1)


def owner_base(doc_lengths, doc_owners):
    doc_numbers = jnp.arange(doc_lengths.shape[0], dtype=jnp.int32)
    before = (doc_owners[None, :] < doc_owners[:, None]) | (
        doc_owners[None, :] == doc_owners[:, None]
    ) & (doc_numbers[None, :] < doc_numbers[:, None])
    return jnp.sum(jnp.where(before, doc_lengths[None, :], 0), axis=1)


def per_device_general(hidden_states, queries, latent_down, key_up, value_up, doc_lengths, doc_owners):
    row_count = hidden_states.shape[0]
    tp_count = lax.axis_size("tp")
    sub_count = lax.axis_size("sub")
    tp_index = lax.axis_index("tp")
    sub_index = lax.axis_index("sub")
    partial_sums = jnp.dot(hidden_states, latent_down, preferred_element_type=F32)
    latents = lax.psum(partial_sums, "tp").astype(BF16)
    local_heads = queries.shape[1] // HEAD_DIM
    per_group = Q_HEADS // KV_HEADS
    grouped = min(local_heads, per_group)
    kv_count = local_heads // grouped
    kv_first = tp_index * local_heads // per_group
    key_cols = lax.dynamic_slice_in_dim(key_up, kv_first * HEAD_DIM, kv_count * HEAD_DIM, 1)
    value_cols = lax.dynamic_slice_in_dim(value_up, kv_first * HEAD_DIM, kv_count * HEAD_DIM, 1)
    own_keys = jnp.dot(latents[:, :RANK], key_cols, preferred_element_type=F32).astype(BF16)
    own_values = jnp.dot(latents[:, RANK:], value_cols, preferred_element_type=F32).astype(BF16)
    doc_starts, doc_ends = doc_tables(doc_lengths)
    query_pos = sub_index * row_count + jnp.arange(row_count, dtype=jnp.int32)
    query_doc = doc_of(query_pos, doc_ends)
    query_grid = queries.reshape(row_count, kv_count, grouped, HEAD_DIM)
    inv_root = 1.0 / math.sqrt(HEAD_DIM)
    carried = (
        jnp.full((kv_count, grouped, row_count), -1e30, F32),
        jnp.zeros((kv_count, grouped, row_count), F32),
        jnp.zeros((kv_count, grouped, row_count, HEAD_DIM), F32),
    )
    key_piece = lax.all_gather(own_keys, "sub", axis=0, tiled=True)
    value_piece = lax.all_gather(own_values, "sub", axis=0, tiled=True)
    piece_len = key_piece.shape[0]
    block_len = math.gcd(piece_len, 1024)
    block_total = piece_len // block_len
    key_blocks = key_piece.reshape(block_total, block_len, kv_count, HEAD_DIM)
    value_blocks = value_piece.reshape(block_total, block_len, kv_count, HEAD_DIM)
    first_positions = block_len * jnp.arange(block_total, dtype=jnp.int32)

    def absorb(state, block_item):
        running_top, totals, weighted = state
        key_block, value_block, first_pos = block_item
        key_pos = first_pos + jnp.arange(block_len, dtype=jnp.int32)
        key_doc = doc_of(key_pos, doc_ends)
        allowed = (key_pos[None, :] <= query_pos[:, None]) & (
            key_doc[None, :] == query_doc[:, None]
        )
        scores = (
            jnp.einsum("qkgd,jkd->kgqj", query_grid, key_block, preferred_element_type=F32)
            * inv_root
        )
        scores = jnp.where(allowed, scores, -1e30)
        new_top = jnp.maximum(running_top, jnp.max(scores, axis=-1))
        weights = jnp.where(allowed, jnp.exp(scores - new_top[..., None]), 0.0)
        rescale = jnp.exp(running_top - new_top)
        totals = totals * rescale + jnp.sum(weights, axis=-1)
        weighted = weighted * rescale[..., None] + jnp.einsum(
            "kgqj,jkd->kgqd", weights.astype(BF16), value_block, preferred_element_type=F32
        )
        return ((new_top, totals, weighted), None)

    carried, _ = lax.scan(absorb, carried, (key_blocks, value_blocks, first_positions))
    running_top, totals, weighted = carried
    result = weighted / totals[..., None]
    attention = (
        jnp.transpose(result, (2, 0, 1, 3))
        .reshape(row_count, local_heads * HEAD_DIM)
        .astype(BF16)
    )
    base_table = owner_base(doc_lengths, doc_owners)
    sorted_rank = lookup(query_doc, base_table - doc_starts) + query_pos
    slot_count = row_count // tp_count
    column_span = slot_count * sub_count
    targets = tp_index * column_span + jnp.arange(column_span, dtype=jnp.int32)
    selector = (targets[:, None] == sorted_rank[None, :]).astype(BF16)
    placed = jnp.dot(selector, latents, preferred_element_type=F32)
    arrived = lax.psum_scatter(placed.astype(BF16), "sub", scatter_dimension=0, tiled=True)
    decode_keys = jnp.dot(arrived[:, :RANK], key_up, preferred_element_type=F32).astype(BF16)
    decode_values = jnp.dot(arrived[:, RANK:], value_up, preferred_element_type=F32).astype(BF16)
    decode_cache = jnp.concatenate([decode_keys, decode_values], axis=1)
    return (attention, decode_cache)


SMEM = pl.BlockSpec(memory_space=pltpu.SMEM)
VMEM = pl.BlockSpec(memory_space=pltpu.VMEM)
ANY = pl.BlockSpec(memory_space=pl.ANY)


def cost(micros):
    return pl.CostEstimate(
        flops=int(micros * 1.1e9), bytes_accessed=int(micros * 1e6), transcendentals=0
    )


def params():
    return pltpu.CompilerParams(vmem_limit_bytes=VMEM_LIMIT)


def project_kernel(chunks, hidden, down, *refs):
    count = len(chunks)
    coded = refs[:count]
    rows_buf, down_buf, row_sem, down_sem = refs[count:]
    tp_index = lax.axis_index("tp")
    depth = down.shape[0] // SLICES
    down_copies, row_copies = [], []
    for c in range(SLICES):
        span = pl.ds(c * depth, depth)
        down_copies.append(
            pltpu.make_async_copy(down.at[span, :], down_buf.at[span, :], down_sem.at[c])
        )
        down_copies[c].start()
        for k in range(count):
            first = pl.multiple_of((tp_index ^ chunks[k]) * BLOCK, BLOCK)
            copy = pltpu.make_async_copy(
                hidden.at[pl.ds(first, BLOCK), span],
                rows_buf.at[k, :, span],
                row_sem.at[k * SLICES + c],
            )
            copy.start()
            row_copies.append(copy)
    sums = [None] * count
    for c in range(SLICES):
        span = slice(c * depth, (c + 1) * depth)
        down_copies[c].wait()
        for k in range(count):
            row_copies[c * count + k].wait()
            term = jnp.dot(rows_buf[k, :, span], down_buf[span, :], preferred_element_type=F32)
            sums[k] = term if c == 0 else sums[k] + term
    lane = lax.broadcasted_iota(jnp.int32, (BLOCK, 128), 1)
    for k in range(count):
        powers = []
        for half in range(2):
            piece = sums[k][:, half * RANK : (half + 1) * RANK]
            top = jnp.max(jnp.abs(piece), axis=1, keepdims=True)
            power = jnp.ceil(jnp.log2(jnp.maximum(top, 1e-30)) + 1e-3)
            code = jnp.round(piece * (CODE_TOP * jnp.exp2(-power))).astype(jnp.int32)
            coded[k][:BLOCK, half * RANK : (half + 1) * RANK] = code.astype(jnp.int16)
            powers.append(power)
        table = jnp.transpose(jnp.where(lane == 0, powers[0], powers[1]))[:SCALE_ROWS]
        table = table.astype(jnp.int32).astype(jnp.int16)
        coded[k][BLOCK:, :RANK] = table
        coded[k][BLOCK:, RANK:] = table


def project(hidden, down, chunks, limit=VMEM_LIMIT):
    width = down.shape[1]
    count = len(chunks)
    return pl.pallas_call(
        functools.partial(project_kernel, chunks),
        out_shape=[jax.ShapeDtypeStruct((BLOCK + SCALE_ROWS, width), jnp.int16)] * count,
        in_specs=[ANY, ANY],
        out_specs=[VMEM] * count,
        scratch_shapes=[
            pltpu.VMEM((count, BLOCK, hidden.shape[1]), BF16),
            pltpu.VMEM(down.shape, BF16),
            pltpu.SemaphoreType.DMA((count * SLICES,)),
            pltpu.SemaphoreType.DMA((SLICES,)),
        ],
        compiler_params=pltpu.CompilerParams(vmem_limit_bytes=limit),
        name="project",
    )(hidden, down)


def expand_kernel(parts, place, *refs):
    coded = refs[:parts]
    key_up, value_up = refs[parts : parts + 2]
    pieces = refs[parts + 2 :]
    tp_index = place[0]
    halves = []
    columns = []
    for k in range(parts):
        powers = coded[k][BLOCK:, :RANK].astype(jnp.int32).astype(F32)
        columns.append(jnp.transpose(jnp.exp2(powers) * (1.0 / CODE_TOP)))
    for half in range(2):
        total = None
        for k in range(parts):
            code = coded[k][:BLOCK, half * RANK : (half + 1) * RANK].astype(jnp.int32).astype(F32)
            term = code * columns[k][:, half : half + 1]
            total = term if total is None else total + term
        halves.append(total.astype(BF16))
        pieces[0][:, half * RANK : (half + 1) * RANK] = halves[half]
    for k in range(parts):
        lead = pieces[k].shape[1] - BLOCK
        head = tp_index ^ k
        cols = pl.ds(pl.multiple_of(head * HEAD_DIM, HEAD_DIM), HEAD_DIM)
        keys = jnp.dot(halves[0], key_up[:, cols], preferred_element_type=F32).astype(BF16)
        values = lax.dot_general(
            value_up[cols, :], halves[1], NT, preferred_element_type=F32
        ).astype(BF16)
        pieces[k][:HEAD_DIM, lead:] = values
        pieces[k][HEAD_DIM:, lead : lead + HEAD_DIM] = keys[:HEAD_DIM]
        pieces[k][HEAD_DIM:, lead + HEAD_DIM :] = keys[HEAD_DIM:]


def expand(place, coded, key_up, value_rows):
    parts = len(coded)
    return pl.pallas_call(
        functools.partial(expand_kernel, parts),
        out_shape=[jax.ShapeDtypeStruct((BLOCK, 2 * RANK + BLOCK), BF16)]
        + [jax.ShapeDtypeStruct((BLOCK, BLOCK), BF16)] * (parts - 1),
        in_specs=[SMEM] + [VMEM] * (parts + 2),
        out_specs=[VMEM] * parts,
        compiler_params=params(),
        name="expand",
    )(place, *coded, key_up, value_rows)


def pick_kernel(planes, subs, row_count, place, lengths, owners, *refs):
    latents, picked = refs[:subs], refs[subs:]
    tp_index, sub_index = place[0], place[1]
    docs = lengths.shape[0]
    sizes = [lengths[d] for d in range(docs)]
    holders = [owners[d] for d in range(docs)]
    shifts, begins, begin = [], [], 0
    for d in range(docs):
        base = 0
        for e in range(docs):
            if e == d:
                continue
            ahead = holders[e] <= holders[d] if e < d else holders[e] < holders[d]
            base = base + jnp.where(ahead, sizes[e], 0)
        begins.append(begin)
        shifts.append(base - begin)
        begin = begin + sizes[d]
    slot = lax.broadcasted_iota(jnp.int32, (BLOCK, 1), 0) + sub_index * BLOCK
    lane = lax.broadcasted_iota(jnp.int32, (8, BLOCK), 1)
    ranks = []
    for j in range(subs):
        position = lane + (sub_index ^ j) * row_count + tp_index * BLOCK
        shift = jnp.full((8, BLOCK), 0, jnp.int32) + shifts[0]
        for d in range(1, docs):
            shift = jnp.where(position >= begins[d], shifts[d], shift)
        ranks.append((position + shift)[:1])
    for out, group in zip(picked, planes):
        for n, k in enumerate(group):
            target = slot + (tp_index ^ k) * (subs * BLOCK)
            total = None
            for j in range(subs):
                chosen = jnp.where(target == ranks[j], 1.0, 0.0).astype(BF16)
                term = jnp.dot(chosen, latents[j][:, : 2 * RANK], preferred_element_type=F32)
                total = term if total is None else total + term
            out[n * BLOCK : (n + 1) * BLOCK, :] = total.astype(BF16)


def pick(place, lengths, owners, latents, planes, row_count):
    subs = len(latents)
    return pl.pallas_call(
        functools.partial(pick_kernel, planes, subs, row_count),
        out_shape=[
            jax.ShapeDtypeStruct((len(group) * BLOCK, 2 * RANK), BF16) for group in planes
        ],
        in_specs=[SMEM] * 3 + [VMEM] * subs,
        out_specs=[VMEM] * len(planes),
        compiler_params=params(),
        name="pick",
    )(place, lengths, owners, *latents)


def rebuild_kernel(parts, *refs):
    arrived, (key_up, value_up, out) = refs[:parts], refs[parts:]
    total = arrived[0][...]
    for k in range(1, parts):
        total = total + arrived[k][:BLOCK, :]
    width = key_up.shape[1]
    out[:, :width] = jnp.dot(total[:, :RANK], key_up[...], preferred_element_type=F32).astype(BF16)
    out[:, width:] = jnp.dot(total[:, RANK:], value_up[...], preferred_element_type=F32).astype(BF16)


def rebuild(arrived, key_up, value_up):
    parts = len(arrived)
    return pl.pallas_call(
        functools.partial(rebuild_kernel, parts),
        out_shape=jax.ShapeDtypeStruct((BLOCK, 2 * key_up.shape[1]), BF16),
        in_specs=[VMEM] * (parts + 2),
        out_specs=VMEM,
        compiler_params=params(),
        name="rebuild",
    )(*arrived, key_up, value_up)


def load_pieces(pieces, blocks, keys, values, sems):
    copies = []
    for n, block in enumerate(blocks):
        first = pl.multiple_of(block * BLOCK, BLOCK)
        copies.append(
            pltpu.make_async_copy(
                pieces[n].at[:HEAD_DIM, :], values.at[:, pl.ds(first, BLOCK)], sems.at[n, 0]
            )
        )
        for side in range(2):
            copies.append(
                pltpu.make_async_copy(
                    pieces[n].at[HEAD_DIM:, side * HEAD_DIM : (side + 1) * HEAD_DIM],
                    keys.at[pl.ds(first + side * HEAD_DIM, HEAD_DIM), :],
                    sems.at[n, side + 1],
                )
            )
    for copy in copies:
        copy.start()
    return copies


def split(refs):
    pieces = []
    for ref in refs:
        lead = ref.shape[1] - BLOCK
        for k in range(ref.shape[0] // BLOCK):
            pieces.append(ref.at[k * BLOCK : (k + 1) * BLOCK, lead : lead + BLOCK])
    return pieces


def clear_blocks(keys, values, first):
    keys[pl.ds(first, BLOCK), :] = jnp.zeros((BLOCK, HEAD_DIM), BF16)
    values[:, pl.ds(first, BLOCK)] = jnp.zeros((HEAD_DIM, BLOCK), BF16)


def longest(keys):
    every = keys[...]
    ones = jnp.ones((8, HEAD_DIM), BF16)
    return jnp.max(lax.dot_general(ones, every * every, NT, preferred_element_type=F32))


def row_bounds(lengths, first):
    position = first + lax.broadcasted_iota(jnp.int32, (1, BLOCK), 1)
    begin, low, high = 0, 0, 0
    begin_row = jnp.zeros((1, BLOCK), jnp.int32)
    for d in range(lengths.shape[0]):
        begin_row = jnp.where(position >= begin, begin, begin_row)
        low = jnp.where(first >= begin, begin, low)
        high = jnp.where(first + BLOCK - 1 >= begin, begin, high)
        begin = begin + lengths[d]
    return position, begin_row, low, high


def absorb(span, keys, values, queries, state, mask, fresh, online):
    tops, sums, mix = state
    heads = queries.shape[1] // HEAD_DIM

    def scores_of(head):
        query = queries[:, head * HEAD_DIM : (head + 1) * HEAD_DIM]
        return lax.dot_general(keys[span, :], query, NT, preferred_element_type=F32)

    ahead = [scores_of(head) for head in range(min(AHEAD, heads))]
    for head in range(heads):
        scores = ahead.pop(0) * GAIN
        if head + AHEAD < heads:
            ahead.append(scores_of(head + AHEAD))
        if mask is not None:
            scores = scores + mask[: scores.shape[0], :]
        row = slice(head, head + 1)
        if fresh:
            top = jnp.max(scores, axis=0, keepdims=True) + LIFT
            tops[row, :] = top
        else:
            before = tops[row, :]
            top = before
            if online:
                top = jnp.maximum(before, jnp.max(scores, axis=0, keepdims=True) + LIFT)
                tops[row, :] = top
        weights = jnp.exp2(scores - top)
        total = jnp.sum(weights, axis=0, keepdims=True)
        result = jnp.dot(values[:, span], weights.astype(BF16), preferred_element_type=F32)
        if fresh:
            sums[row, :] = total
            mix[head] = result
        elif online:
            rescale = jnp.exp2(before - top)
            sums[row, :] = sums[row, :] * rescale + total
            mix[head] = mix[head] * rescale + result
        else:
            sums[row, :] += total
            mix[head] += result


def set_mask(mask, allowed):
    mask[: allowed.shape[0], :] = jnp.where(allowed, 0.0, -1e30)


def bounded(queries, tops, key_top):
    every = queries[...]
    heads = tops.shape[0]
    lane = lax.broadcasted_iota(jnp.int32, (heads, every.shape[1]), 1) // HEAD_DIM
    of_head = lane == lax.broadcasted_iota(jnp.int32, lane.shape, 0)
    of_head = jnp.where(of_head, 1.0, 0.0).astype(BF16)
    squares = lax.dot_general(of_head, every * every, NT, preferred_element_type=F32)
    reach = jnp.sqrt(squares * key_top) * (GAIN * 1.02) - (tops[...] - LIFT)
    return jnp.max(reach) <= SPAN


def attend_near_kernel(parts, row_count, place, lengths, queries, *refs):
    pieces = refs[:parts]
    tops, sums, mix, packed, keys, values, mask, key_top, sems, pack_sems = refs[parts:]
    tops, sums, mix = state = (tops.at[0], sums.at[0], mix.at[0])
    step = pl.program_id(0)
    tp_index, sub_index = place[0], place[1]
    packs = [
        pltpu.make_async_copy(
            pieces[k], packed.at[(k - 1) * BLOCK : k * BLOCK, :], pack_sems.at[k]
        )
        for k in range(1, parts)
    ]
    pieces = split(pieces)

    @pl.when(step == 0)
    def _():
        copies = load_pieces(
            pieces, [(tp_index ^ k) + 1 for k in range(parts)], keys, values, sems
        )
        for copy in packs:
            copy.start()
        clear_blocks(keys, values, 0)
        for copy in copies:
            copy.wait()
        key_top[0] = longest(keys)

    start = sub_index * row_count
    first = start + step * BLOCK
    position, begin_row, low, high = row_bounds(lengths, first)
    begin_row = jnp.maximum(begin_row, start)
    low_block = jnp.maximum(low - start, 0) // BLOCK
    full_block = (jnp.maximum(high - start, 0) + BLOCK - 1) // BLOCK
    last = (step - low_block) // 2
    clear = jnp.minimum(jnp.maximum(step - 1 - full_block, 0) // 2, last)
    key_iota = lax.broadcasted_iota(jnp.int32, (2 * BLOCK, BLOCK), 0) + (first - BLOCK)

    def take(pair, masked, online):
        span = pl.ds(pl.multiple_of((step - 2 * pair) * BLOCK, BLOCK), 2 * BLOCK)
        absorb(span, keys, values, queries, state, mask if masked else None, False, online)

    @pl.when(low_block == step)
    def _():
        span = pl.ds(pl.multiple_of((step + 1) * BLOCK, BLOCK), BLOCK)
        own_iota = key_iota[BLOCK:, :]
        set_mask(mask, (own_iota <= position) & (own_iota >= begin_row))
        absorb(span, keys, values, queries, state, mask, True, False)

    @pl.when(low_block < step)
    def _():
        span = pl.ds(pl.multiple_of(step * BLOCK, BLOCK), 2 * BLOCK)
        set_mask(mask, (key_iota <= position) & (key_iota >= begin_row))
        absorb(span, keys, values, queries, state, mask, True, False)

    @pl.when(last > 0)
    def _():
        safe = bounded(queries, tops, key_top[0])
        for online in (False, True):

            @pl.when(jnp.logical_not(safe) if online else safe)
            def _():
                @pl.loop(1, clear + 1)
                def _(pair):
                    take(pair, False, online)

                @pl.loop(clear + 1, last + 1)
                def _(pair):
                    set_mask(mask, key_iota - 2 * pair * BLOCK >= begin_row)
                    take(pair, True, online)

    @pl.when(step == pl.num_programs(0) - 1)
    def _():
        for copy in packs:
            copy.wait()


def attend_far_kernel(parts, subs, groups, row_count, place, lengths, queries, *refs):
    tops_in, sums_in, mix_in = refs[:3]
    held, refs = refs[3 : 3 + groups], refs[3 + groups :]
    out, keys, values, mask, tops, sums, mix, key_top, sems = refs
    pieces = split(held)
    heads = tops.shape[0]
    step = pl.program_id(0)
    tp_index, sub_index = place[0], place[1]

    @pl.when(step == 0)
    def _():
        blocks = [
            (sub_index ^ j) * parts + (tp_index ^ k) for j in range(1, subs) for k in range(parts)
        ]
        copies = load_pieces(pieces, blocks, keys, values, sems)
        for k in range(parts):
            clear_blocks(keys, values, pl.multiple_of((sub_index * parts + k) * BLOCK, BLOCK))
        for copy in copies:
            copy.wait()
        key_top[0] = longest(keys)

    first = sub_index * row_count + step * BLOCK
    position, begin_row, low, high = row_bounds(lengths, first)
    end_block = sub_index * parts
    low_block = low // BLOCK
    full_block = (high + BLOCK - 1) // BLOCK
    count = jnp.maximum(end_block - low_block, 0)
    last = count // 2
    clear = jnp.minimum(jnp.maximum(end_block - full_block, 0) // 2, last)

    @pl.when(count == 0)
    def _():
        finish(mix_in.at[0], sums_in.at[0], out)

    @pl.when(count > 0)
    def _():
        tops[...] = tops_in[0]
        sums[...] = sums_in[0]
        mix[...] = mix_in[0]

        def take(block, blocks, masked, online):
            begin = block * BLOCK
            span = pl.ds(pl.multiple_of(begin, BLOCK), blocks * BLOCK)
            if masked:
                key_iota = lax.broadcasted_iota(jnp.int32, (blocks * BLOCK, BLOCK), 0)
                set_mask(mask, key_iota + begin >= begin_row)
            state = (tops, sums, mix)
            absorb(span, keys, values, queries, state, mask if masked else None, False, online)

        safe = bounded(queries, tops, key_top[0])
        for online in (False, True):

            @pl.when(jnp.logical_not(safe) if online else safe)
            def _():
                @pl.loop(0, clear)
                def _(pair):
                    take(end_block - 2 - 2 * pair, 2, False, online)

                @pl.loop(clear, last)
                def _(pair):
                    take(end_block - 2 - 2 * pair, 2, True, online)

                @pl.when(count > 2 * last)
                def _():
                    take(low_block, 1, True, online)

        finish(mix, sums, out)


def finish(mix, sums, out):
    for head in range(mix.shape[0]):
        result = mix[head] * (1.0 / sums[head : head + 1, :])
        out[:, head * HEAD_DIM : (head + 1) * HEAD_DIM] = jnp.transpose(result).astype(BF16)


def attend_specs(queries):
    row_count, width = queries.shape
    heads, steps = width // HEAD_DIM, row_count // BLOCK
    shapes = [(heads, BLOCK), (heads, BLOCK), (heads, HEAD_DIM, BLOCK)]
    row_spec = pl.BlockSpec((BLOCK, width), lambda i: (i, 0))
    state_specs = [
        pl.BlockSpec((1, *shape), lambda i, rank=len(shape): (i,) + (0,) * rank)
        for shape in shapes
    ]
    state_shapes = [jax.ShapeDtypeStruct((steps, *shape), F32) for shape in shapes]
    scratch = [pltpu.VMEM(shape, F32) for shape in shapes]
    return (steps,), row_spec, state_specs, state_shapes, scratch


def store_shapes(blocks, pieces):
    return [
        pltpu.VMEM((blocks * BLOCK, HEAD_DIM), BF16),
        pltpu.VMEM((HEAD_DIM, blocks * BLOCK), BF16),
        pltpu.VMEM((2 * BLOCK, BLOCK), F32),
    ], [pltpu.SMEM((1,), F32), pltpu.SemaphoreType.DMA((pieces, 3))]


def attend_near(place, lengths, queries, pieces):
    parts = len(pieces)
    grid, row_spec, state_specs, state_shapes, _ = attend_specs(queries)
    stores, rest = store_shapes(parts + 1, parts)
    return pl.pallas_call(
        functools.partial(attend_near_kernel, parts, queries.shape[0]),
        grid=grid,
        out_shape=state_shapes + [jax.ShapeDtypeStruct(((parts - 1) * BLOCK, BLOCK), BF16)],
        in_specs=[SMEM, SMEM, row_spec] + [ANY] * parts,
        out_specs=state_specs + [ANY],
        scratch_shapes=stores + rest + [pltpu.SemaphoreType.DMA((parts,))],
        compiler_params=params(),
        cost_estimate=cost(12),
        name="attend_near",
    )(place, lengths, queries, *pieces)


def attend_far(place, lengths, queries, state, pieces, parts, subs):
    grid, row_spec, state_specs, _, scratch = attend_specs(queries)
    stores, rest = store_shapes(parts * subs, parts * (subs - 1))
    return pl.pallas_call(
        functools.partial(attend_far_kernel, parts, subs, len(pieces), queries.shape[0]),
        grid=grid,
        out_shape=jax.ShapeDtypeStruct(queries.shape, BF16),
        in_specs=[SMEM, SMEM, row_spec] + state_specs + [ANY] * len(pieces),
        out_specs=row_spec,
        scratch_shapes=stores + scratch + rest,
        compiler_params=params(),
        cost_estimate=cost(20),
        name="attend_far",
    )(place, lengths, queries, *state, *pieces)


def swap(value, axis, bits):
    count = lax.axis_size(axis)
    return lax.ppermute(value, axis, [(i, i ^ bits) for i in range(count)])


def per_device(hidden_states, queries, latent_down, key_up, value_up, doc_lengths, doc_owners):
    row_count = hidden_states.shape[0]
    parts = lax.axis_size("tp")
    subs = lax.axis_size("sub")
    place = jnp.stack([lax.axis_index("tp"), lax.axis_index("sub")]).astype(jnp.int32)
    value_rows = value_up.T
    far = [
        project(hidden_states, latent_down, (k,), FULL_VMEM)[0]
        for k in range(parts // 2, parts)
    ]
    far = [swap(item, "tp", k) for k, item in enumerate(far, parts // 2)]
    near = project(hidden_states, latent_down, tuple(range(parts // 2)))
    near = [near[0]] + [swap(item, "tp", k) for k, item in enumerate(near[1:], 1)]
    coded = near + far
    own, *pieces = expand(place, coded, key_up, value_rows)
    arrivals = [swap(item, "tp", k) for k, item in enumerate(pieces, 1)]

    half = subs // 2
    order, rows, reach = [0], [own], half
    while reach >= 1:
        order = order + [item ^ reach for item in order]
        far_rows = [swap(item, "sub", reach) for item in rows]
        far_rows, arrivals = lax.optimization_barrier((far_rows, arrivals))
        rows = rows + list(far_rows)
        reach //= 2
    rows = [rows[order.index(j)] for j in range(subs)]
    planes = ((1, 3), (0,), (2,))
    leaving, kept, across = pick(place, doc_lengths, doc_owners, rows, planes, row_count)
    passed = swap(leaving, "tp", 1)

    gate, kept = lax.optimization_barrier((place, kept))
    *state, packed = attend_near(gate, doc_lengths, queries, [own, *arrivals])
    onward = [(i, i ^ half) for i in range(half)]
    crossed = [lax.ppermute(item, "sub", onward) for item in arrivals]
    crossed, state, packed, passed = lax.optimization_barrier((crossed, state, packed, passed))

    blocks, reach = [[packed], list(crossed)], half // 2
    while reach >= 1:
        blocks = blocks + [[swap(item, "sub", reach) for item in group] for group in blocks]
        reach //= 2
    blocks = [blocks[order.index(j)] for j in range(subs)]

    second = swap(across + passed[BLOCK:], "tp", 2)
    flat = []
    for j in range(1, subs):
        flat += [rows[j], *blocks[j]]
    attention = attend_far(place, doc_lengths, queries, state, flat, parts, subs)
    kept, attention = lax.optimization_barrier((kept, attention))
    decode_cache = rebuild([kept, passed, second], key_up, value_up)
    return (attention, decode_cache)


def fits(mesh):
    return mesh.shape["tp"] == KV_HEADS and mesh.shape["sub"] & (mesh.shape["sub"] - 1) == 0


def choose(mesh):
    def run(hidden_states, queries, *rest):
        rows = hidden_states.shape[0]
        direct = fits(mesh) and rows == BLOCK * mesh.shape["tp"]
        return (per_device if direct else per_device_general)(hidden_states, queries, *rest)

    return run


def solution(mesh):
    return jax.shard_map(
        choose(mesh),
        mesh=mesh,
        in_specs=(
            P(("groups", "sub"), "tp"),
            P(("groups", "sub"), "tp"),
            P("tp", None),
            P(),
            P(),
            P("groups"),
            P("groups"),
        ),
        out_specs=(P(("groups", "sub"), "tp"), P(("groups", "tp", "sub"), None)),
        check_vma=False,
    )
```
